128 devices in a mesh: row: 32 (over x, y, core), col: 4 (over z).
Axes of the slice: x: 4, y: 4, z: 4, core: 2. Of those that a mesh axis runs over, the one named last changes fastest.
Arguments:
- coeffs: bfloat16 [4096, 1024], P('row', 'col'), may hold values from -0.09375 to 0.09375
- coef_pattern: int32 [32, 8], replicated, may hold values 0 or 1
- keep_density: int32 [2, 32, 32], replicated, may hold values 0 or 1
- keep_square: int32 [2, 32, 32], replicated, may hold values 0 or 1
Outputs:
- density: float32 [4096, 4096], P('row', 'col')
The draws below stay inside these ranges and needn't reach their ends.
All inputs are finite; a program needn't handle non-finite values.
Results may differ from the reference program's by a relative error of at most 0.0042.
Values may be sent and summed in bfloat16 or wider, within the bound.
No kernel may reach another device: no remote copies, remote signals or barrier semaphores. Data moves between devices by JAX's collectives and lax.ppermute only.
A program may use at most 64 MiB of HBM per device.

```python
import jax
import jax.numpy as jnp

B = 128
STEPS = 2
NBLK = 32
KBLK = 8
N = 4096
K = 1024


def with_ends(entries, rng, smallest, largest):
    index_at = [jax.random.randint(jax.random.fold_in(rng, axis), (), 0, length) for axis, length in enumerate(entries.shape)]
    widest = entries.shape.index(max(entries.shape))
    neighbour = index_at[:widest] + [(index_at[widest] + 1) % entries.shape[widest]] + index_at[widest + 1:]
    return entries.at[tuple(index_at)].set(smallest).at[tuple(neighbour)].set(largest)


def levels(own_key, extent, shards, least, largest):
    factor_of, own = 1.0, jax.random.fold_in(own_key, 6)
    for axis_at, blocks in shards:
        draws = jnp.exp(jax.random.uniform(jax.random.fold_in(own, axis_at), (blocks,), jnp.float32, least / len(shards), largest / len(shards)))
        factor_of = factor_of * jnp.repeat(draws, extent[axis_at] // blocks).reshape([-1 if axis == axis_at else 1 for axis in range(len(extent))])
    return factor_of


def bell_draw(rng, dims, deviation, bound, pieces=(), dtype=jnp.bfloat16):
    loudness = levels(rng, dims, pieces, -0.22, 0.18) if pieces else 1.0
    entries = jax.random.normal(rng, dims, jnp.float32) * deviation * loudness
    return jnp.minimum(jnp.maximum(entries, -bound), bound).astype(dtype)


def setup_inputs(seed: int = 0) -> dict:
    splits = jax.random.split(jax.random.key(seed), 5)
    return {
        "coeffs": bell_draw(splits[0], (N, K), N ** -0.5, 0.09375, ((0, 32), (1, 4))),
        "coef_pattern": with_ends((jax.random.randint(splits[1], (NBLK, KBLK), 0, 2) < 1).astype(jnp.int32), jax.random.fold_in(splits[1], 1), 0, 1),
        "keep_density": with_ends((jax.random.randint(splits[2], (STEPS, NBLK, NBLK), 0, 4) < 3).astype(jnp.int32), jax.random.fold_in(splits[2], 1), 0, 1),
        "keep_square": with_ends((jax.random.randint(splits[3], (STEPS, NBLK, NBLK), 0, 4) < 3).astype(jnp.int32), jax.random.fold_in(splits[3], 1), 0, 1),
    }


def widen(blocks):
    return jnp.repeat(jnp.repeat(blocks, B, 0), B, 1)


def reference(coeffs, coef_pattern, keep_density, keep_square):
    kept = coeffs * widen(coef_pattern).astype(jnp.bfloat16)
    density = jnp.dot(kept, kept.T, preferred_element_type=jnp.float32)
    for step in range(STEPS):
        current = (density * widen(keep_density[step]).astype(jnp.float32)).astype(jnp.bfloat16)
        square = jnp.dot(current, current, preferred_element_type=jnp.float32)
        square = square * widen(keep_square[step]).astype(jnp.float32)
        square_low = square.astype(jnp.bfloat16)
        cube = jnp.dot(square_low, current, preferred_element_type=jnp.float32)
        density = 3.0 * square - 2.0 * cube
    return density
```

```python
import jax
import jax.numpy as jnp
from jax import lax
from jax.experimental import pallas as pl
from jax.experimental.pallas import tpu as pltpu
from jax.sharding import PartitionSpec as P

B = 128
N = 4096
K = 1024
ROWS = 256
COLS = 512
AXES = ("row", "col")
MIB = 1024 * 1024


def device(x, y, core, z):
    return (((x % 4) * 4 + y % 4) * 2 + core) * 4 + z % 4


def pairs(target):
    return [
        (device(x, y, core, z), device(*target(x, y, core, z)))
        for x in range(4) for y in range(4) for core in range(2) for z in range(4)
    ]


def other_core(a):
    return lax.ppermute(a, AXES, pairs(lambda x, y, core, z: (x, y, 1 - core, z)))


def from_z(a, d):
    return lax.ppermute(a, AXES, pairs(lambda x, y, core, z: (x, y, core, z - d)))


def from_first(a, d):
    return lax.ppermute(a, AXES, pairs(
        lambda x, y, core, z: (x - d, y, core, z) if core == 0 else (x, y - d, core, z)))


def from_second(a, d):
    return lax.ppermute(a, AXES, pairs(
        lambda x, y, core, z: (x, y - d, core, z) if core == 0 else (x - d, y, core, z)))


def gather_z(a):
    return [a] + [from_z(a, d) for d in (1, 3, 2)]


def by_offset(parts):
    own, one, three, two = parts
    return [own, one, two, three]


def gather_plane(a):
    line = jnp.concatenate(by_offset([a] + [from_first(a, d) for d in (1, 3, 2)]), axis=0)
    return by_offset([line] + [from_second(line, d) for d in (1, 3, 2)])


def place(x, y, kind, first, second):
    px = jnp.where(kind == 0, x + first, x + second) & 3
    py = jnp.where(kind == 0, y + second, y + first) & 3
    return px, py


def dot_t(a, b):
    return lax.dot_general(a, b, (((1,), (1,)), ((), ())), preferred_element_type=jnp.float32)


def dot(a, b):
    return jnp.dot(a, b, preferred_element_type=jnp.float32)


def first_square(where, keep_d, keep_s, *refs):
    parts, (panel, square, low), (kept, col_rows, row, sems) = refs[:8], refs[8:11], refs[11:]
    x, y, core, z = where[0], where[1], where[2], where[3]
    chip = x * 4 + y
    copies = [
        pltpu.make_async_copy(part, kept.at[pl.ds(i * 512, 512)], sems.at[i])
        for i, part in enumerate(parts)
    ]
    for copy in copies:
        copy.start()
    for copy in copies:
        copy.wait()

    def position(block):
        px, py, kind = block >> 3, (block >> 1) & 3, block & 1
        dx, dy = (px - x) & 3, (py - y) & 3
        first = jnp.where(kind == 0, dx, dy)
        second = jnp.where(kind == 0, dy, dx)
        return jnp.where(kind == core, 0, 16) + second * 4 + first

    col_block = z * 8 + core * 4
    for t in range(4):
        at = pl.multiple_of(position(col_block + t) * B, B)
        col_rows[pl.ds(t * B, B), :] = kept[pl.ds(at, B), :]
    for t in range(2):
        at = pl.multiple_of(position(chip * 2 + t) * B, B)
        col_rows[pl.ds(512 + t * B, B), :] = kept[pl.ds(at, B), :]

    @pl.loop(0, 8)
    def _(part):
        kind = jnp.where(part < 4, core, 1 - core)
        second = part & 3
        chunk = kept[pl.ds(pl.multiple_of(part * 512, 512), 512), :]
        blocks = []
        for first in range(4):
            px, py = place(x, y, kind, first, second)
            blocks.append(px * 8 + py * 2 + kind)
        down = dot_t(chunk, col_rows[0:512, :])
        for i in range(4):
            at = pl.multiple_of(blocks[i] * B, B)
            for t in range(4):
                keep = keep_d[0, blocks[i], col_block + t].astype(jnp.float32)
                piece = down[i * B:(i + 1) * B, t * B:(t + 1) * B] * keep
                panel[pl.ds(at, B), t * B:(t + 1) * B] = piece.astype(jnp.bfloat16)
        across = dot_t(col_rows[512:768, :], chunk)
        for i in range(4):
            at = pl.multiple_of(blocks[i] * B, B)
            for t in range(2):
                keep = keep_d[0, chip * 2 + t, blocks[i]].astype(jnp.float32)
                piece = across[t * B:(t + 1) * B, i * B:(i + 1) * B] * keep
                row[t * B:(t + 1) * B, pl.ds(at, B)] = piece.astype(jnp.bfloat16)

    finish_square(dot(row[...], panel[...]), keep_s, 0, chip * 2, col_block, square, low)


def finish_square(value, keep_s, step, row_block, col_block, square, low):
    for t in range(2):
        for u in range(4):
            keep = keep_s[step, row_block + t, col_block + u].astype(jnp.float32)
            piece = value[t * B:(t + 1) * B, u * B:(u + 1) * B] * keep
            square[t * B:(t + 1) * B, u * B:(u + 1) * B] = piece
            low[t * B:(t + 1) * B, u * B:(u + 1) * B] = piece.astype(jnp.bfloat16)


def row_times_panel(own, other, core, z, panel):
    total = None
    for d in range(4):
        for ref, half in ((own[d], core), (other[d], 1 - core)):
            at = pl.multiple_of((((z + d) & 3) * 2 + half) * COLS, COLS)
            term = dot(ref[...], panel[pl.ds(at, COLS), :])
            total = term if total is None else total + term
    return total


def first_density(where, keep_d, *refs):
    own, other, (square, panel), (out,) = refs[:4], refs[4:8], refs[8:10], refs[10:]
    x, y, core, z = where[0], where[1], where[2], where[3]
    cube = row_times_panel(own, other, core, z, panel)
    value = 3.0 * square[...] - 2.0 * cube
    for t in range(2):
        for u in range(4):
            keep = keep_d[1, (x * 4 + y) * 2 + t, z * 8 + core * 4 + u].astype(jnp.float32)
            piece = value[t * B:(t + 1) * B, u * B:(u + 1) * B] * keep
            out[t * B:(t + 1) * B, u * B:(u + 1) * B] = piece.astype(jnp.bfloat16)


def load_panel(parts, panel, sems, x, y, core):
    copies = []
    for second, part in enumerate(parts):
        for first in range(4):
            px, py = place(x, y, core, first, second)
            at = pl.multiple_of((px * 4 + py) * ROWS, ROWS)
            copies.append(pltpu.make_async_copy(
                part.at[pl.ds(first * ROWS, ROWS)], panel.at[pl.ds(at, ROWS)], sems.at[second * 4 + first]))
    for copy in copies:
        copy.start()
    for copy in copies:
        copy.wait()


def second_square(where, keep_s, *refs):
    own, other, parts, (square, low), (panel, sems) = refs[:4], refs[4:8], refs[8:12], refs[12:14], refs[14:]
    x, y, core, z = where[0], where[1], where[2], where[3]
    load_panel(parts, panel, sems, x, y, core)
    value = row_times_panel(own, other, core, z, panel)
    finish_square(value, keep_s, 1, (x * 4 + y) * 2, z * 8 + core * 4, square, low)


def second_density(where, *refs):
    own, other, (square,), parts, (stay, leave), (panel, sems) = (
        refs[:4], refs[4:8], refs[8:9], refs[9:13], refs[13:15], refs[15:])
    x, y, core, z = where[0], where[1], where[2], where[3]
    load_panel(parts, panel, sems, x, y, core)
    value = 3.0 * square[...] - 2.0 * row_times_panel(own, other, core, z, panel)
    first = core == 0
    stay[...] = jnp.where(first, value[:B], value[B:])
    leave[...] = jnp.where(first, value[B:], value[:B])


SMEM = pl.BlockSpec(memory_space=pltpu.SMEM)
VMEM = pl.BlockSpec(memory_space=pltpu.VMEM)
ANY = pl.BlockSpec(memory_space=pl.ANY)


def call(kernel, ins, outs, scratch, flops, moved):
    return pl.pallas_call(
        kernel,
        in_specs=ins,
        out_specs=[VMEM] * len(outs),
        out_shape=outs,
        scratch_shapes=scratch,
        cost_estimate=pl.CostEstimate(flops=flops, bytes_accessed=moved, transcendentals=0),
        compiler_params=pltpu.CompilerParams(vmem_limit_bytes=40 * MIB),
    )


def body(coeffs, coef_pattern, keep_density, keep_square):
    r, z = lax.axis_index("row"), lax.axis_index("col")
    x, y, core = r // 8, (r // 2) % 4, r % 2
    where = jnp.stack([x, y, core, z]).astype(jnp.int32)
    low_block = jax.ShapeDtypeStruct((ROWS, COLS), jnp.bfloat16)
    full_block = jax.ShapeDtypeStruct((ROWS, COLS), jnp.float32)
    panel_scratch = [pltpu.VMEM((N, COLS), jnp.bfloat16), pltpu.SemaphoreType.DMA((16,))]

    pattern = lax.dynamic_slice(coef_pattern, (r, z * 2), (1, 2))
    kept = coeffs * jnp.repeat(pattern, B, 1).astype(jnp.bfloat16)

    kept = jnp.concatenate(by_offset(gather_z(kept)), axis=1)
    parts = gather_plane(kept)
    parts = parts + [other_core(part) for part in parts]
    panel, square, low = call(
        first_square, [SMEM] * 3 + [ANY] * 8,
        [jax.ShapeDtypeStruct((N, COLS), jnp.bfloat16), full_block, low_block],
        [
            pltpu.VMEM((N, K), jnp.bfloat16),
            pltpu.VMEM((COLS + ROWS, K), jnp.bfloat16),
            pltpu.VMEM((ROWS, N), jnp.bfloat16),
            pltpu.SemaphoreType.DMA((8,)),
        ],
        2 * N * K * (COLS + ROWS) + 2 * ROWS * N * COLS, 13 * MIB,
    )(where, keep_density, keep_square, *parts)

    own = by_offset(gather_z(low))
    other = [other_core(part) for part in own]
    (current,) = call(
        first_density, [SMEM] * 2 + [VMEM] * 10, [low_block], [], 2 * ROWS * N * COLS, 7 * MIB,
    )(where, keep_density, *own, *other, square, panel)

    parts = gather_plane(current)
    own = by_offset(gather_z(current))
    other = [other_core(part) for part in own]
    square, low = call(
        second_square, [SMEM] * 2 + [VMEM] * 8 + [ANY] * 4, [full_block, low_block],
        panel_scratch, 2 * ROWS * N * COLS, 7 * MIB,
    )(where, keep_square, *own, *other, *parts)

    own = by_offset(gather_z(low))
    other = [other_core(part) for part in own]
    half = jax.ShapeDtypeStruct((B, COLS), jnp.float32)
    stay, leave = call(
        second_density, [SMEM] + [VMEM] * 9 + [ANY] * 4, [half, half],
        panel_scratch, 2 * ROWS * N * COLS, 8 * MIB,
    )(where, *own, *other, square, *parts)
    come = other_core(leave)
    left = core == 0
    return jnp.concatenate([jnp.where(left, stay, come), jnp.where(left, come, stay)], axis=1)


def solution(mesh):
    placed = (P("row", "col"), P(), P(), P())
    return jax.shard_map(
        body, mesh=mesh, in_specs=placed, out_specs=P("row", "col"), check_vma=False
    )
```

```python
import jax
import jax.numpy as jnp
from jax import lax
from jax.experimental import pallas as pl
from jax.experimental.pallas import tpu as pltpu
from jax.sharding import PartitionSpec as P

B = 128
N = 4096
K = 1024
ROWS = 256
COLS = 512
AXES = ("row", "col")
MIB = 1024 * 1024


def device(x, y, core, z):
    return (((x % 4) * 4 + y % 4) * 2 + core) * 4 + z % 4


def pairs(target):
    return [
        (device(x, y, core, z), device(*target(x, y, core, z)))
        for x in range(4) for y in range(4) for core in range(2) for z in range(4)
    ]


def other_core(a):
    return lax.ppermute(a, AXES, pairs(lambda x, y, core, z: (x, y, 1 - core, z)))


def from_z(a, d):
    return lax.ppermute(a, AXES, pairs(lambda x, y, core, z: (x, y, core, z - d)))


def from_x(a, d):
    return lax.ppermute(a, AXES, pairs(lambda x, y, core, z: (x - d, y, core, z)))


def from_y(a, d):
    return lax.ppermute(a, AXES, pairs(lambda x, y, core, z: (x, y - d, core, z)))


def by_offset(own, one, three, two):
    return [own, one, two, three]


def gather_z(a):
    return by_offset(a, *[from_z(a, d) for d in (1, 3, 2)])


def gather_plane(a, b):
    firsts = [from_x(a, 1), from_x(a, 3), from_y(b, 1), from_y(b, 3), from_x(a, 2), from_y(b, 2)]
    a, b, *firsts = lax.optimization_barrier((a, b, *firsts))
    a = jnp.concatenate(by_offset(a, firsts[0], firsts[1], firsts[4]), axis=0)
    b = jnp.concatenate(by_offset(b, firsts[2], firsts[3], firsts[5]), axis=0)
    a, b = lax.optimization_barrier((a, b))
    return by_offset(a, *[from_y(a, d) for d in (1, 3, 2)]), by_offset(b, *[from_x(b, d) for d in (1, 3, 2)])


def block_at(x, y, kind, i, j):
    return ((x + i) & 3) * 8 + ((y + j) & 3) * 2 + kind


def dot_t(a, b):
    return lax.dot_general(a, b, (((1,), (1,)), ((), ())), preferred_element_type=jnp.float32)


def dot(a, b):
    return jnp.dot(a, b, preferred_element_type=jnp.float32)


def first_square(where, keep_d, keep_s, *refs):
    left, right, (panel, square, low), (rows, row, sems) = (
        (refs[0:4], refs[4:8]), (refs[8:12], refs[12:16]), refs[16:19], refs[19:])
    x, y, core, z = where[0], where[1], where[2], where[3]
    row_block, col_block = (x * 4 + y) * 2, z * 8 + core * 4

    def fetch(source, block, target, half):
        return pltpu.make_async_copy(
            source.at[pl.ds(pl.multiple_of(block * B, B), B)],
            rows.at[pl.ds(pl.multiple_of(target * B, B), B), pl.ds(half * 512, 512)],
            sems.at[half, target])

    i = (z - x) & 3
    js = [(core * 2 + pair - y) & 3 for pair in range(2)]
    for c in range(2):
        for j in range(4):
            @pl.when((core == c) & (i == j))
            def _():
                for t in range(4):
                    fetch(right[(t & 1) ^ c][j], js[t >> 1], t, 1).start()

            for pair in range(2):
                @pl.when((core == c) & (js[pair] == j))
                def _():
                    for t in (2 * pair, 2 * pair + 1):
                        fetch(left[(t & 1) ^ c][j], i, t, 0).start()
    kinds = (core, 1 - core)
    for own in range(2):
        fetch(left[own][0], 0, 4 + kinds[own], 0).start()
        fetch(right[own][0], 0, 4 + kinds[own], 1).start()
    for t in range(6):
        fetch(left[0][0], 0, t, 0).wait()
        fetch(right[0][0], 0, t, 1).wait()

    for own in range(2):
        for j in range(4):
            beside = [right[own][i][j * B:(j + 1) * B, :] for i in range(4)]
            chunk = jnp.concatenate([left[own][j][...], jnp.concatenate(beside, axis=0)], axis=1)
            value = dot_t(chunk, rows[...])
            for i in range(4):
                block = block_at(x, y, kinds[own], i, j)
                at = pl.multiple_of(block * B, B)
                for t in range(4):
                    keep = keep_d[0, block, col_block + t].astype(jnp.float32)
                    piece = value[i * B:(i + 1) * B, t * B:(t + 1) * B] * keep
                    panel[pl.ds(at, B), t * B:(t + 1) * B] = piece.astype(jnp.bfloat16)
                for t in range(2):
                    keep = keep_d[0, row_block + t, block].astype(jnp.float32)
                    piece = value[i * B:(i + 1) * B, COLS + t * B:COLS + (t + 1) * B] * keep
                    row[t * B:(t + 1) * B, pl.ds(at, B)] = piece.astype(jnp.bfloat16).T

    finish_square(dot(row[...], panel[...]), keep_s, 0, row_block, col_block, square, low)


def finish_square(value, keep_s, step, row_block, col_block, square, low):
    for t in range(2):
        for u in range(4):
            keep = keep_s[step, row_block + t, col_block + u].astype(jnp.float32)
            piece = value[t * B:(t + 1) * B, u * B:(u + 1) * B] * keep
            square[t * B:(t + 1) * B, u * B:(u + 1) * B] = piece
            low[t * B:(t + 1) * B, u * B:(u + 1) * B] = piece.astype(jnp.bfloat16)


def row_times_panel(own, other, core, z, panel):
    total = None
    for d in range(4):
        for ref, half in ((own[d], core), (other[d], 1 - core)):
            at = pl.multiple_of((((z + d) & 3) * 2 + half) * COLS, COLS)
            term = dot(ref[...], panel[pl.ds(at, COLS), :])
            total = term if total is None else total + term
    return total


def first_density(where, keep_d, *refs):
    own, other, (square, panel), (out,) = refs[:4], refs[4:8], refs[8:10], refs[10:]
    x, y, core, z = where[0], where[1], where[2], where[3]
    cube = row_times_panel(own, other, core, z, panel)
    value = 3.0 * square[...] - 2.0 * cube
    for t in range(2):
        for u in range(4):
            keep = keep_d[1, (x * 4 + y) * 2 + t, z * 8 + core * 4 + u].astype(jnp.float32)
            piece = value[t * B:(t + 1) * B, u * B:(u + 1) * B] * keep
            out[t * B:(t + 1) * B, u * B:(u + 1) * B] = piece.astype(jnp.bfloat16)


def load_panel(parts, panel, sems, x, y):
    copies = []
    for kind in range(2):
        for j in range(4):
            for i in range(4):
                at = pl.multiple_of((block_at(x, y, 0, i, j) if kind == 0 else block_at(x, y, 1, j, i)) * B, B)
                copies.append(pltpu.make_async_copy(
                    parts[kind * 4 + j].at[pl.ds(i * B, B)], panel.at[pl.ds(at, B)],
                    sems.at[(kind * 4 + j) * 4 + i]))
    for copy in copies:
        copy.start()
    for copy in copies:
        copy.wait()


def second_square(where, keep_s, line, *refs):
    parts, (square, low), (panel, sems) = refs[:8], refs[8:10], refs[10:]
    x, y, core, z = where[0], where[1], where[2], where[3]
    load_panel(parts, panel, sems, x, y)
    value = None
    for q in range(8):
        term = dot(line[q * ROWS:(q + 1) * ROWS, :], panel[q * COLS:(q + 1) * COLS, :])
        value = term if value is None else value + term
    finish_square(value, keep_s, 1, (x * 4 + y) * 2, z * 8 + core * 4, square, low)


def second_density(where, *refs):
    own, other, (square,), parts, (stay, leave), (panel, sems) = (
        refs[:4], refs[4:8], refs[8:9], refs[9:17], refs[17:19], refs[19:])
    x, y, core, z = where[0], where[1], where[2], where[3]
    load_panel(parts, panel, sems, x, y)
    value = 3.0 * square[...] - 2.0 * row_times_panel(own, other, core, z, panel)
    first = core == 0
    stay[...] = jnp.where(first, value[:B], value[B:])
    leave[...] = jnp.where(first, value[B:], value[:B])


SMEM = pl.BlockSpec(memory_space=pltpu.SMEM)
VMEM = pl.BlockSpec(memory_space=pltpu.VMEM)
ANY = pl.BlockSpec(memory_space=pl.ANY)


def call(kernel, ins, outs, scratch, flops, moved):
    return pl.pallas_call(
        kernel,
        in_specs=ins,
        out_specs=[VMEM] * len(outs),
        out_shape=outs,
        scratch_shapes=scratch,
        cost_estimate=pl.CostEstimate(flops=flops, bytes_accessed=moved, transcendentals=0),
        compiler_params=pltpu.CompilerParams(vmem_limit_bytes=48 * MIB),
    )


def body(coeffs, coef_pattern, keep_density, keep_square):
    r, z = lax.axis_index("row"), lax.axis_index("col")
    x, y, core = r // 8, (r // 2) % 4, r % 2
    where = jnp.stack([x, y, core, z]).astype(jnp.int32)
    low_block = jax.ShapeDtypeStruct((ROWS, COLS), jnp.bfloat16)
    full_block = jax.ShapeDtypeStruct((ROWS, COLS), jnp.float32)
    panel_scratch = [pltpu.VMEM((N, COLS), jnp.bfloat16), pltpu.SemaphoreType.DMA((32,))]

    wide = jnp.concatenate(gather_z(coeffs), axis=1)
    pattern = lax.dynamic_slice(coef_pattern, (r, 0), (1, 8)).reshape(4, 2)
    pattern = jnp.concatenate([pattern, pattern], axis=0)
    pattern = lax.dynamic_slice(pattern, (z, 0), (4, 2)).reshape(1, 8)
    wide = wide * jnp.repeat(pattern, B, 1).astype(jnp.bfloat16)
    left, right = lax.optimization_barrier((wide[:, :512], wide[:, 512:]))
    left, right = gather_plane(left, right)
    left_other, right_other = [other_core(part) for part in left], [other_core(part) for part in right]
    panel, square, low = call(
        first_square, [SMEM] * 3 + [VMEM] * 16,
        [jax.ShapeDtypeStruct((N, COLS), jnp.bfloat16), full_block, low_block],
        [
            pltpu.VMEM((COLS + ROWS, K), jnp.bfloat16),
            pltpu.VMEM((ROWS, N), jnp.bfloat16),
            pltpu.SemaphoreType.DMA((2, 6)),
        ],
        2 * N * K * (COLS + ROWS) + 2 * ROWS * N * COLS, 13 * MIB,
    )(where, keep_density, keep_square, *left, *left_other, *right, *right_other)

    own = gather_z(low)
    other = [other_core(part) for part in own]
    (current,) = call(
        first_density, [SMEM] * 2 + [VMEM] * 10, [low_block], [], 2 * ROWS * N * COLS, 7 * MIB,
    )(where, keep_density, *own, *other, square, panel)

    line = lax.all_gather(current, AXES, axis=0, tiled=True, axis_index_groups=[
        [device(x, y, core, z) for z in range(4) for core in range(2)] for x in range(4) for y in range(4)])
    even, odd = lax.optimization_barrier((current[:B], current[B:]))
    even, odd = gather_plane(even, odd)
    parts = even + odd
    square, low = call(
        second_square, [SMEM] * 2 + [VMEM] * 9, [full_block, low_block],
        panel_scratch, 2 * ROWS * N * COLS, 7 * MIB,
    )(where, keep_square, line, *parts)

    own = gather_z(low)
    other = [other_core(part) for part in own]
    half = jax.ShapeDtypeStruct((B, COLS), jnp.float32)
    stay, leave = call(
        second_density, [SMEM] + [VMEM] * 17, [half, half],
        panel_scratch, 2 * ROWS * N * COLS, 8 * MIB,
    )(where, *own, *other, square, *parts)
    come = other_core(leave)
    first = core == 0
    return jnp.concatenate([jnp.where(first, stay, come), jnp.where(first, come, stay)], axis=1)


def solution(mesh):
    placed = (P("row", "col"), P(), P(), P())
    return jax.shard_map(
        body, mesh=mesh, in_specs=placed, out_specs=P("row", "col"), check_vma=False
    )
```

```python
import jax
import jax.numpy as jnp
from jax import lax
from jax.experimental import pallas as pl
from jax.experimental.pallas import tpu as pltpu
from jax.sharding import PartitionSpec as P

B = 128
N = 4096
K = 1024
ROWS = 256
COLS = 512
AXES = ("row", "col")
MIB = 1024 * 1024


def device(x, y, core, z):
    return (((x % 4) * 4 + y % 4) * 2 + core) * 4 + z % 4


def pairs(target):
    return [
        (device(x, y, core, z), device(*target(x, y, core, z)))
        for x in range(4) for y in range(4) for core in range(2) for z in range(4)
    ]


def other_core(a):
    return lax.ppermute(a, AXES, pairs(lambda x, y, core, z: (x, y, 1 - core, z)))


def from_z(a, d):
    return lax.ppermute(a, AXES, pairs(lambda x, y, core, z: (x, y, core, z - d)))


def from_first(a, d):
    return lax.ppermute(a, AXES, pairs(
        lambda x, y, core, z: (x - d, y, core, z) if core == 0 else (x, y - d, core, z)))


def from_second(a, d):
    return lax.ppermute(a, AXES, pairs(
        lambda x, y, core, z: (x, y - d, core, z) if core == 0 else (x - d, y, core, z)))


def by_offset(own, one, three, two):
    return [own, one, two, three]


def gather_z(a):
    return by_offset(a, *[from_z(a, d) for d in (1, 3, 2)])


def gather_plane(a):
    one, three, two, far = from_first(a, 1), from_first(a, 3), from_first(a, 2), from_second(a, 2)
    a, one, three, two, far = lax.optimization_barrier((a, one, three, two, far))
    line = jnp.concatenate(by_offset(a, one, three, two), axis=0)
    far_line = jnp.concatenate(by_offset(far, *[from_first(far, d) for d in (1, 3, 2)]), axis=0)
    return by_offset(line, from_second(line, 1), from_second(line, 3), far_line)


def place(x, y, kind, first, second):
    px = jnp.where(kind == 0, x + first, x + second) & 3
    py = jnp.where(kind == 0, y + second, y + first) & 3
    return px, py


def dot_t(a, b):
    return lax.dot_general(a, b, (((1,), (1,)), ((), ())), preferred_element_type=jnp.float32)


def dot(a, b):
    return jnp.dot(a, b, preferred_element_type=jnp.float32)


def first_square(where, keep_d, keep_s, *refs):
    parts, (panel, square, low), (rows, row, sems) = (refs[0:4], refs[4:8]), refs[8:11], refs[11:]
    x, y, core, z = where[0], where[1], where[2], where[3]
    row_block, col_block = (x * 4 + y) * 2, z * 8 + core * 4
    kinds = (core, 1 - core)

    def fetch(source, block, target):
        return pltpu.make_async_copy(
            source.at[pl.ds(pl.multiple_of(block * B, B), B)],
            rows.at[pl.ds(pl.multiple_of(target * B, B), B)], sems.at[target])

    for t in range(4):
        dx, dy = (z - x) & 3, (core * 2 + (t >> 1) - y) & 3
        first, second = (dx, dy) if t & 1 == 0 else (dy, dx)
        for c in range(2):
            for j in range(4):
                @pl.when((core == c) & (second == j))
                def _():
                    fetch(parts[(t & 1) ^ c][j], first, t).start()
    for own in range(2):
        fetch(parts[own][0], 0, 4 + kinds[own]).start()
    for t in range(6):
        fetch(parts[0][0], 0, t).wait()

    for own in range(2):
        for j in range(4):
            value = dot_t(parts[own][j][...], rows[...])
            for i in range(4):
                px, py = place(x, y, kinds[own], i, j)
                block = px * 8 + py * 2 + kinds[own]
                at = pl.multiple_of(block * B, B)
                for t in range(4):
                    keep = keep_d[0, block, col_block + t].astype(jnp.float32)
                    piece = value[i * B:(i + 1) * B, t * B:(t + 1) * B] * keep
                    panel[pl.ds(at, B), t * B:(t + 1) * B] = piece.astype(jnp.bfloat16)
                for t in range(2):
                    keep = keep_d[0, row_block + t, block].astype(jnp.float32)
                    piece = value[i * B:(i + 1) * B, COLS + t * B:COLS + (t + 1) * B] * keep
                    row[t * B:(t + 1) * B, pl.ds(at, B)] = piece.astype(jnp.bfloat16).T

    finish_square(dot(row[...], panel[...]), keep_s, 0, row_block, col_block, square, low)


def finish_square(value, keep_s, step, row_block, col_block, square, low):
    for t in range(2):
        for u in range(4):
            keep = keep_s[step, row_block + t, col_block + u].astype(jnp.float32)
            piece = value[t * B:(t + 1) * B, u * B:(u + 1) * B] * keep
            square[t * B:(t + 1) * B, u * B:(u + 1) * B] = piece
            low[t * B:(t + 1) * B, u * B:(u + 1) * B] = piece.astype(jnp.bfloat16)


def row_times_panel(own, other, core, z, panel):
    total = None
    for d in range(4):
        for ref, half in ((own[d], core), (other[d], 1 - core)):
            at = pl.multiple_of((((z + d) & 3) * 2 + half) * COLS, COLS)
            term = dot(ref[...], panel[pl.ds(at, COLS), :])
            total = term if total is None else total + term
    return total


def first_density(where, keep_d, *refs):
    own, other, (square, panel), (out,) = refs[:4], refs[4:8], refs[8:10], refs[10:]
    x, y, core, z = where[0], where[1], where[2], where[3]
    cube = row_times_panel(own, other, core, z, panel)
    value = 3.0 * square[...] - 2.0 * cube
    for t in range(2):
        for u in range(4):
            keep = keep_d[1, (x * 4 + y) * 2 + t, z * 8 + core * 4 + u].astype(jnp.float32)
            piece = value[t * B:(t + 1) * B, u * B:(u + 1) * B] * keep
            out[t * B:(t + 1) * B, u * B:(u + 1) * B] = piece.astype(jnp.bfloat16)


def load_panel(parts, panel, sems, x, y, core):
    copies = []
    for second, part in enumerate(parts):
        for first in range(4):
            px, py = place(x, y, core, first, second)
            at = pl.multiple_of((px * 4 + py) * ROWS, ROWS)
            copies.append(pltpu.make_async_copy(
                part.at[pl.ds(first * ROWS, ROWS)], panel.at[pl.ds(at, ROWS)], sems.at[second * 4 + first]))
    for copy in copies:
        copy.start()
    for copy in copies:
        copy.wait()


def second_square(where, keep_s, line, *refs):
    parts, (square, low), (panel, sems) = refs[:4], refs[4:6], refs[6:]
    x, y, core, z = where[0], where[1], where[2], where[3]
    load_panel(parts, panel, sems, x, y, core)
    value = None
    for q in range(8):
        term = dot(line[q * ROWS:(q + 1) * ROWS, :], panel[q * COLS:(q + 1) * COLS, :])
        value = term if value is None else value + term
    finish_square(value, keep_s, 1, (x * 4 + y) * 2, z * 8 + core * 4, square, low)


def second_density(where, *refs):
    own, other, (square,), parts, (stay, leave), (panel, sems) = (
        refs[:4], refs[4:8], refs[8:9], refs[9:13], refs[13:15], refs[15:])
    x, y, core, z = where[0], where[1], where[2], where[3]
    load_panel(parts, panel, sems, x, y, core)
    value = 3.0 * square[...] - 2.0 * row_times_panel(own, other, core, z, panel)
    first = core == 0
    stay[...] = jnp.where(first, value[:B], value[B:])
    leave[...] = jnp.where(first, value[B:], value[:B])


SMEM = pl.BlockSpec(memory_space=pltpu.SMEM)
VMEM = pl.BlockSpec(memory_space=pltpu.VMEM)
ANY = pl.BlockSpec(memory_space=pl.ANY)


def call(kernel, ins, outs, scratch, flops, moved, limit):
    return pl.pallas_call(
        kernel,
        in_specs=ins,
        out_specs=[VMEM] * len(outs),
        out_shape=outs,
        scratch_shapes=scratch,
        cost_estimate=pl.CostEstimate(flops=flops, bytes_accessed=moved, transcendentals=0),
        compiler_params=pltpu.CompilerParams(vmem_limit_bytes=limit * MIB),
    )


def body(coeffs, coef_pattern, keep_density, keep_square):
    r, z = lax.axis_index("row"), lax.axis_index("col")
    x, y, core = r // 8, (r // 2) % 4, r % 2
    where = jnp.stack([x, y, core, z]).astype(jnp.int32)
    low_block = jax.ShapeDtypeStruct((ROWS, COLS), jnp.bfloat16)
    full_block = jax.ShapeDtypeStruct((ROWS, COLS), jnp.float32)
    panel_scratch = [pltpu.VMEM((N, COLS), jnp.bfloat16), pltpu.SemaphoreType.DMA((16,))]

    wide = jnp.concatenate(gather_z(coeffs), axis=1)
    pattern = lax.dynamic_slice(coef_pattern, (r, 0), (1, 8)).reshape(4, 2)
    pattern = jnp.concatenate([pattern, pattern], axis=0)
    pattern = lax.dynamic_slice(pattern, (z, 0), (4, 2)).reshape(1, 8)
    wide = wide * jnp.repeat(pattern, B, 1).astype(jnp.bfloat16)
    parts = gather_plane(wide)
    others = [other_core(part) for part in parts]
    panel, square, low = call(
        first_square, [SMEM] * 3 + [VMEM] * 8,
        [jax.ShapeDtypeStruct((N, COLS), jnp.bfloat16), full_block, low_block],
        [
            pltpu.VMEM((COLS + ROWS, K), jnp.bfloat16),
            pltpu.VMEM((ROWS, N), jnp.bfloat16),
            pltpu.SemaphoreType.DMA((6,)),
        ],
        2 * N * K * (COLS + ROWS) + 2 * ROWS * N * COLS, 13 * MIB, 16,
    )(where, keep_density, keep_square, *parts, *others)

    own = gather_z(low)
    other = [other_core(part) for part in own]
    (current,) = call(
        first_density, [SMEM] * 2 + [VMEM] * 10, [low_block], [], 2 * ROWS * N * COLS, 7 * MIB, 8,
    )(where, keep_density, *own, *other, square, panel)

    line = lax.all_gather(current, AXES, axis=0, tiled=True, axis_index_groups=[
        [device(x, y, core, z) for z in range(4) for core in range(2)] for x in range(4) for y in range(4)])
    parts = gather_plane(current)
    square, low = call(
        second_square, [SMEM] * 2 + [VMEM] + [ANY] * 4, [full_block, low_block],
        panel_scratch, 2 * ROWS * N * COLS, 7 * MIB, 12,
    )(where, keep_square, line, *parts)

    own = gather_z(low)
    other = [other_core(part) for part in own]
    half = jax.ShapeDtypeStruct((B, COLS), jnp.float32)
    stay, leave = call(
        second_density, [SMEM] + [VMEM] * 9 + [ANY] * 4, [half, half],
        panel_scratch, 2 * ROWS * N * COLS, 8 * MIB, 12,
    )(where, *own, *other, square, *parts)
    come = other_core(leave)
    first = core == 0
    return jnp.concatenate([jnp.where(first, stay, come), jnp.where(first, come, stay)], axis=1)


def solution(mesh):
    placed = (P("row", "col"), P(), P(), P())
    return jax.shard_map(
        body, mesh=mesh, in_specs=placed, out_specs=P("row", "col"), check_vma=False
    )
```

```python
import jax
import jax.numpy as jnp
from jax import lax
from jax.experimental import pallas as pl
from jax.experimental.pallas import tpu as pltpu
from jax.sharding import PartitionSpec as P

B = 128
N = 4096
K = 1024
ROWS = 256
COLS = 512
DEPTH = 256
AXES = ("row", "col")
MIB = 1024 * 1024


def device(x, y, core, z):
    return (((x % 4) * 4 + y % 4) * 2 + core) * 4 + z % 4


def pairs(target):
    return [
        (device(x, y, core, z), device(*target(x, y, core, z)))
        for x in range(4) for y in range(4) for core in range(2) for z in range(4)
    ]


def other_core(a):
    return lax.ppermute(a, AXES, pairs(lambda x, y, core, z: (x, y, 1 - core, z)))


def from_z(a, d):
    return lax.ppermute(a, AXES, pairs(lambda x, y, core, z: (x, y, core, z - d)))


def from_first(a, d):
    return lax.ppermute(a, AXES, pairs(
        lambda x, y, core, z: (x - d, y, core, z) if core == 0 else (x, y - d, core, z)))


def from_second(a, d):
    return lax.ppermute(a, AXES, pairs(
        lambda x, y, core, z: (x, y - d, core, z) if core == 0 else (x - d, y, core, z)))


def gather(a, fetch):
    one, three, two = fetch(a, 1), fetch(a, 3), fetch(a, 2)
    return [a, one, two, three]


def place(x, y, kind, first, second):
    px = jnp.where(kind == 0, x + first, x + second) & 3
    py = jnp.where(kind == 0, y + second, y + first) & 3
    return px, py


def dot_t(a, b):
    return lax.dot_general(a, b, (((1,), (1,)), ((), ())), preferred_element_type=jnp.float32)


def dot(a, b):
    return jnp.dot(a, b, preferred_element_type=jnp.float32)


def aligned(block, size):
    return pl.ds(pl.multiple_of(block * size, size), size)


def pick_rows(where, own, other, rows):
    x, y, core, z = where[0], where[1], where[2], where[3]
    for t in range(6):
        kind = t & 1
        if t < 4:
            dx, dy = (z - x) & 3, (core * 2 + (t >> 1) - y) & 3
            first, second = (dx, dy) if kind == 0 else (dy, dx)
            at = aligned(second * 4 + first, B)
        else:
            at = pl.ds(0, B)
        rows[t * B:(t + 1) * B, :] = jnp.where(kind == core, own[at, :], other[at, :])


def early_density(where, *refs):
    sets, total, rows = refs[:-2], refs[-2], refs[-1]
    add = len(sets) % 2 == 1
    if add:
        before, sets = sets[0], sets[1:]
    for n in range(len(sets) // 2):
        own, other = sets[2 * n], sets[2 * n + 1]
        pick_rows(where, own, other, rows.at[:, pl.ds(n * DEPTH, DEPTH)])
    for half in range(2):
        for j in range(4):
            part = jnp.concatenate([sets[2 * n + half][j * 512:(j + 1) * 512, :] for n in range(len(sets) // 2)], axis=1)
            at = slice((half * 4 + j) * 512, (half * 4 + j + 1) * 512)
            value = dot_t(part, rows[...])
            total[at, :] = before[at, :] + value if add else value


def first_square(where, keep_d, keep_s, before, own, other, panel, square, low, rows, row):
    x, y, core, z = where[0], where[1], where[2], where[3]
    row_block, col_block = (x * 4 + y) * 2, z * 8 + core * 4
    pick_rows(where, own, other, rows)
    for half, (part, kind) in enumerate(((own, core), (other, 1 - core))):
        for j in range(4):
            at = slice((half * 4 + j) * 512, (half * 4 + j + 1) * 512)
            value = before[at, :] + dot_t(part[j * 512:(j + 1) * 512, :], rows[...])
            for i in range(4):
                px, py = place(x, y, kind, i, j)
                block = px * 8 + py * 2 + kind
                for t in range(4):
                    keep = keep_d[0, block, col_block + t].astype(jnp.float32)
                    piece = value[i * B:(i + 1) * B, t * B:(t + 1) * B] * keep
                    panel[aligned(block, B), t * B:(t + 1) * B] = piece.astype(jnp.bfloat16)
                for t in range(2):
                    keep = keep_d[0, row_block + t, block].astype(jnp.float32)
                    piece = value[i * B:(i + 1) * B, COLS + t * B:COLS + (t + 1) * B] * keep
                    row[t * B:(t + 1) * B, aligned(block, B)] = piece.astype(jnp.bfloat16).T
    finish_square(dot(row[...], panel[...]), keep_s, 0, row_block, col_block, square, low)


def finish_square(value, keep_s, step, row_block, col_block, square, low):
    for t in range(2):
        for u in range(4):
            keep = keep_s[step, row_block + t, col_block + u].astype(jnp.float32)
            piece = value[t * B:(t + 1) * B, u * B:(u + 1) * B] * keep
            square[t * B:(t + 1) * B, u * B:(u + 1) * B] = piece
            low[t * B:(t + 1) * B, u * B:(u + 1) * B] = piece.astype(jnp.bfloat16)


def parts_times_panel(parts, core, z, panel):
    total = None
    for ref, d, half in parts:
        term = dot(ref[...], panel[aligned(((z + d) & 3) * 2 + half, COLS), :])
        total = term if total is None else total + term
    return total


def early_cube(where, *refs):
    own, other, panel, out = refs[:4], refs[4], refs[5], refs[6]
    core, z = where[2], where[3]
    parts = [(own[d], d, core) for d in range(4)] + [(other, 0, 1 - core)]
    out[...] = parts_times_panel(parts, core, z, panel)


def late_cube(where, others, early, panel):
    core, z = where[2], where[3]
    parts = [(others[d - 1], d, 1 - core) for d in (1, 2, 3)]
    return early[...] + parts_times_panel(parts, core, z, panel)


def first_density(where, keep_d, *refs):
    others, (early, square, panel, out) = refs[:3], refs[3:]
    x, y, core, z = where[0], where[1], where[2], where[3]
    value = 3.0 * square[...] - 2.0 * late_cube(where, others, early, panel)
    for t in range(2):
        for u in range(4):
            keep = keep_d[1, (x * 4 + y) * 2 + t, z * 8 + core * 4 + u].astype(jnp.float32)
            piece = value[t * B:(t + 1) * B, u * B:(u + 1) * B] * keep
            out[t * B:(t + 1) * B, u * B:(u + 1) * B] = piece.astype(jnp.bfloat16)


def chips_times(where, line, chips, panel, sems):
    x, y, core = where[0], where[1], where[2]
    copies, left, right = [], [], []
    for n, (ref, offset, first, second) in enumerate(chips):
        px, py = place(x, y, core, first, second)
        copies.append(pltpu.make_async_copy(
            ref.at[pl.ds(offset, ROWS)], panel.at[aligned(px * 4 + py, ROWS)], sems.at[n]))
        copies[-1].start()
        at = aligned(px * 2 + (py >> 1), ROWS)
        left.append(jnp.where(py & 1 == 0, line[at, :ROWS], line[at, ROWS:]))
        right.append(ref[offset:offset + ROWS, :])
    total = None
    for n in range(0, len(chips), 4):
        term = dot(jnp.concatenate(left[n:n + 4], axis=1), jnp.concatenate(right[n:n + 4], axis=0))
        total = term if total is None else total + term
    return total, copies


def early_square(where, *refs):
    own, other, near, far, (early, line, panel), (sems,) = (
        refs[:4], refs[4:8], refs[8], refs[9:13], refs[13:16], refs[16:])
    core, z = where[2], where[3]
    for d in range(4):
        line[aligned(((z + d) & 3) * 2 + core, ROWS), :] = own[d][...]
        line[aligned(((z + d) & 3) * 2 + 1 - core, ROWS), :] = other[d][...]
    chips = [(near, i * ROWS, i, 0) for i in range(4)] + [(far[i], 0, i, 2) for i in range(4)]
    value, copies = chips_times(where, line, chips, panel, sems)
    early[...] = value
    for copy in copies:
        copy.wait()


def second_square(where, keep_s, one, three, early, line, _, square, low, panel, sems):
    x, y, core, z = where[0], where[1], where[2], where[3]
    chips = [(ref, i * ROWS, i, j) for ref, j in ((one, 1), (three, 3)) for i in range(4)]
    value, copies = chips_times(where, line, chips, panel, sems)
    finish_square(early[...] + value, keep_s, 1, (x * 4 + y) * 2, z * 8 + core * 4, square, low)
    for copy in copies:
        copy.wait()


def second_density(where, *refs):
    others, (early, square, panel, stay, leave) = refs[:3], refs[3:]
    value = 3.0 * square[...] - 2.0 * late_cube(where, others, early, panel)
    first = where[2] == 0
    stay[...] = jnp.where(first, value[:B], value[B:])
    leave[...] = jnp.where(first, value[B:], value[:B])


SMEM = pl.BlockSpec(memory_space=pltpu.SMEM)
VMEM = pl.BlockSpec(memory_space=pltpu.VMEM)


def call(kernel, n_smem, ins, outs, scratch, flops, moved, aliases={}):
    return pl.pallas_call(
        kernel,
        in_specs=[SMEM] * n_smem + [VMEM] * (len(ins) - n_smem),
        out_specs=[VMEM] * len(outs),
        out_shape=outs,
        scratch_shapes=scratch,
        input_output_aliases=aliases,
        cost_estimate=pl.CostEstimate(flops=flops, bytes_accessed=moved, transcendentals=0),
        compiler_params=pltpu.CompilerParams(vmem_limit_bytes=12 * MIB),
    )(*ins)


def body(coeffs, coef_pattern, keep_density, keep_square):
    r, z = lax.axis_index("row"), lax.axis_index("col")
    x, y, core = r // 8, (r // 2) % 4, r % 2
    where = jnp.stack([x, y, core, z]).astype(jnp.int32)
    low_block = jax.ShapeDtypeStruct((ROWS, COLS), jnp.bfloat16)
    full_block = jax.ShapeDtypeStruct((ROWS, COLS), jnp.float32)
    panel_shape = jax.ShapeDtypeStruct((N, COLS), jnp.bfloat16)
    total_shape = jax.ShapeDtypeStruct((N, COLS + ROWS), jnp.float32)
    block_flops = 2 * ROWS * N * COLS
    density_flops = 2 * N * K * (COLS + ROWS)

    patterns = []
    for i in range(4):
        px, py = place(x, y, core, i, 0)
        patterns.append(lax.dynamic_slice(coef_pattern, (px * 8 + py * 2 + core, z * 2), (1, 2)))
    patterns = jnp.repeat(jnp.repeat(jnp.concatenate(patterns, axis=0), B, 0), B, 1).astype(jnp.bfloat16)
    line = jnp.concatenate(gather(coeffs, from_first), axis=0) * patterns
    kept = jnp.concatenate(gather(line, from_second), axis=0)
    own = gather(kept, from_z)
    other = [other_core(part) for part in own]

    (total,) = call(
        early_density, 1, [where, own[0], other[0]], [total_shape],
        [pltpu.VMEM((COLS + ROWS, DEPTH), jnp.bfloat16)], density_flops // 4, 14 * MIB)
    (total,) = call(
        early_density, 1, [where, total, own[1], other[1], own[3], other[3]], [total_shape],
        [pltpu.VMEM((COLS + ROWS, 2 * DEPTH), jnp.bfloat16)], density_flops // 2, 28 * MIB, {1: 0})
    panel, square, low = call(
        first_square, 3, [where, keep_density, keep_square, total, own[2], other[2]],
        [panel_shape, full_block, low_block],
        [pltpu.VMEM((COLS + ROWS, DEPTH), jnp.bfloat16), pltpu.VMEM((ROWS, N), jnp.bfloat16)],
        density_flops // 4 + block_flops, 19 * MIB)

    own = gather(low, from_z)
    other = [other_core(part) for part in own]
    (early,) = call(
        early_cube, 1, [where, *own, other[0], panel], [full_block], [], block_flops * 5 // 8, 4 * MIB)
    (current,) = call(
        first_density, 2, [where, keep_density, *other[1:], early, square, panel], [low_block], [],
        block_flops * 3 // 8, 3 * MIB)

    one, three, two, far = (
        from_first(current, 1), from_first(current, 3), from_first(current, 2), from_second(current, 2))
    start, one, three, two, far = lax.optimization_barrier((current, one, three, two, far))
    near = jnp.concatenate([start, one, two, three], axis=0)
    above, below = from_second(near, 1), from_second(near, 3)
    far = gather(far, from_first)
    own = gather(start, from_z)
    other = [other_core(part) for part in own]
    early, line, panel = call(
        early_square, 1, [where, *own, *other, near, *far],
        [full_block, jax.ShapeDtypeStruct((8 * ROWS, COLS), jnp.bfloat16), panel_shape],
        [pltpu.SemaphoreType.DMA((8,))], block_flops // 2, 10 * MIB)
    square, low, panel = call(
        second_square, 2, [where, keep_square, above, below, early, line, panel],
        [full_block, low_block, panel_shape],
        [pltpu.SemaphoreType.DMA((8,))], block_flops // 2, 8 * MIB, {6: 2})

    own = gather(low, from_z)
    other = [other_core(part) for part in own]
    (early,) = call(
        early_cube, 1, [where, *own, other[0], panel], [full_block], [], block_flops * 5 // 8, 4 * MIB)
    half = jax.ShapeDtypeStruct((B, COLS), jnp.float32)
    stay, leave = call(
        second_density, 1, [where, *other[1:], early, square, panel], [half, half], [],
        block_flops * 3 // 8, 3 * MIB)
    come = other_core(leave)
    first = core == 0
    return jnp.concatenate([jnp.where(first, stay, come), jnp.where(first, come, stay)], axis=1)


def solution(mesh):
    placed = (P("row", "col"), P(), P(), P())
    return jax.shard_map(
        body, mesh=mesh, in_specs=placed, out_specs=P("row", "col"), check_vma=False
    )
```

```python
import jax
import jax.numpy as jnp
from jax import lax
from jax.experimental import pallas as pl
from jax.experimental.pallas import tpu as pltpu
from jax.sharding import PartitionSpec as P

B = 128
N = 4096
K = 1024
ROWS = 256
COLS = 512
AXES = ("row", "col")
MIB = 1024 * 1024


def device(x, y, core, z):
    return (((x % 4) * 4 + y % 4) * 2 + core) * 4 + z % 4


def pairs(target):
    return [
        (device(x, y, core, z), device(*target(x, y, core, z)))
        for x in range(4) for y in range(4) for core in range(2) for z in range(4)
    ]


def other_core(a):
    return lax.ppermute(a, AXES, pairs(lambda x, y, core, z: (x, y, 1 - core, z)))


def from_z(a, d):
    return lax.ppermute(a, AXES, pairs(lambda x, y, core, z: (x, y, core, z - d)))


def from_first(a, d):
    return lax.ppermute(a, AXES, pairs(
        lambda x, y, core, z: (x - d, y, core, z) if core == 0 else (x, y - d, core, z)))


def from_second(a, d):
    return lax.ppermute(a, AXES, pairs(
        lambda x, y, core, z: (x, y - d, core, z) if core == 0 else (x - d, y, core, z)))


def gather(a, fetch):
    one, three, two = fetch(a, 1), fetch(a, 3), fetch(a, 2)
    return [a, one, two, three]


def place(x, y, kind, first, second):
    px = jnp.where(kind == 0, x + first, x + second) & 3
    py = jnp.where(kind == 0, y + second, y + first) & 3
    return px, py


def dot_t(a, b):
    return lax.dot_general(a, b, (((1,), (1,)), ((), ())), preferred_element_type=jnp.float32)


def dot(a, b):
    return jnp.dot(a, b, preferred_element_type=jnp.float32)


def aligned(block, size):
    return pl.ds(pl.multiple_of(block * size, size), size)


def block_at(x, y, kind, place_in_order):
    px, py = place(x, y, kind, place_in_order % 4, place_in_order // 4)
    return px * 8 + py * 2 + kind


def some_rows(where, keep_d, own, other, ns, line):
    x, y, core = where[0], where[1], where[2]
    mine, its = own[0][:B, :], other[0][:B, :]
    rows = jnp.concatenate([jnp.where(core == 0, mine, its), jnp.where(core == 0, its, mine)], axis=0)
    for half, (parts, kind) in enumerate(((own, core), (other, 1 - core))):
        for n in ns:
            value = dot_t(rows, parts[n][...])
            for u in range(4):
                block = block_at(x, y, kind, n * 4 + u)
                at = (half * 16 + n * 4 + u) * B
                for t in range(2):
                    keep = keep_d[0, (x * 4 + y) * 2 + t, block].astype(jnp.float32)
                    piece = value[t * B:(t + 1) * B, u * B:(u + 1) * B] * keep
                    line[t * B:(t + 1) * B, at:at + B] = piece.astype(jnp.bfloat16)


def some_columns(where, keep_d, parts, half, n, m, column, panel):
    x, y, core = where[0], where[1], where[2]
    kind = core if half == 0 else 1 - core
    value = dot_t(parts[n][...], column[...])
    for i in range(4):
        row_block = block_at(x, y, kind, n * 4 + i)
        at = (half * 16 + n * 4 + i) * B
        for u in range(4):
            keep = keep_d[0, row_block, block_at(x, y, core, m * 4 + u)].astype(jnp.float32)
            piece = value[i * B:(i + 1) * B, u * B:(u + 1) * B] * keep
            to = (m * 4 + u) * B
            panel[at:at + B, to:to + B] = piece.astype(jnp.bfloat16)


EARLY = (0, 1, 3)


def early_density(where, keep_d, own0, own1, own3, other0, other1, other3, panel, line):
    own, other = {0: own0, 1: own1, 3: own3}, {0: other0, 1: other1, 3: other3}
    some_rows(where, keep_d, own, other, EARLY, line)
    for half, parts in enumerate((own, other)):
        for n in EARLY:
            for m in EARLY:
                some_columns(where, keep_d, parts, half, n, m, own[m], panel)


def first_square(where, keep_d, keep_s, *refs):
    own, other, (panel, line, low, square, total) = refs[:4], refs[4:8], refs[10:]
    x, y, core, z = where[0], where[1], where[2], where[3]
    some_rows(where, keep_d, own, other, (2,), line)
    for half, parts in enumerate((own, other)):
        for n in range(4):
            for m in range(4):
                if n == 2 or m == 2:
                    some_columns(where, keep_d, parts, half, n, m, own[m], panel)

    @pl.loop(0, 8)
    def _(part):
        at = aligned(part, 256)
        value = dot(line[...], panel[:, at])
        for t in range(2):
            for u in range(2):
                block = block_at(x, y, core, part * 2 + u)
                keep = keep_s[0, (x * 4 + y) * 2 + t, block].astype(jnp.float32)
                piece = value[t * B:(t + 1) * B, u * B:(u + 1) * B] * keep
                total[t * B:(t + 1) * B, aligned(part * 2 + u, B)] = piece
                low[t * B:(t + 1) * B, aligned(part * 2 + u, B)] = piece.astype(jnp.bfloat16)
    for t in range(4):
        square[:, t * B:(t + 1) * B] = total[:, aligned(column_at(where, t), B)]


def column_at(where, t):
    x, y, core, z = where[0], where[1], where[2], where[3]
    dx, dy = (z - x) & 3, (t - y) & 3
    return jnp.where(core == 0, dy * 4 + dx, dx * 4 + dy)


def early_first_cube(where, low, panel, early, columns):
    for t in range(4):
        at = aligned(column_at(where, t), B)
        columns[:, t * B:(t + 1) * B] = panel[:, at]
    early[...] = dot(low[...], columns[:2048, :])


def first_density(where, keep_d, its, columns, early, square, out):
    x, y, core, z = where[0], where[1], where[2], where[3]
    value = 3.0 * square[...] - 2.0 * (early[...] + dot(its[...], columns[2048:, :]))
    for t in range(2):
        for u in range(4):
            keep = keep_d[1, (x * 4 + y) * 2 + t, z * 8 + u * 2 + core].astype(jnp.float32)
            piece = value[t * B:(t + 1) * B, u * B:(u + 1) * B] * keep
            out[t * B:(t + 1) * B, u * B:(u + 1) * B] = piece.astype(jnp.bfloat16)


def parts_times_panel(parts, z, panel):
    total = None
    for ref, d, kind in parts:
        rows = [panel[aligned(((z + d) & 3) * 8 + t * 2 + kind, B), :] for t in range(4)]
        term = dot(ref[...], jnp.concatenate(rows, axis=0))
        total = term if total is None else total + term
    return total


def early_cube(where, *refs):
    own, other, panel, out = refs[:4], refs[4], refs[5], refs[6]
    core, z = where[2], where[3]
    parts = [(own[d], d, core) for d in range(4)] + [(other, 0, 1 - core)]
    out[...] = parts_times_panel(parts, z, panel)


def late_cube(where, others, early, panel):
    core, z = where[2], where[3]
    parts = [(others[d - 1], d, 1 - core) for d in (1, 2, 3)]
    return early[...] + parts_times_panel(parts, z, panel)


def chips_times(where, line, chips, panel, sems):
    x, y, core = where[0], where[1], where[2]
    copies, left, right = [], [], []
    for n, (ref, offset, first, second) in enumerate(chips):
        px, py = place(x, y, core, first, second)
        copies.append(pltpu.make_async_copy(
            ref.at[pl.ds(offset, ROWS)], panel.at[aligned(px * 4 + py, ROWS)], sems.at[n]))
        copies[-1].start()
        left.append(line[:, aligned(px * 4 + py, ROWS)])
        right.append(ref[offset:offset + ROWS, :])
    total = None
    for n in range(0, len(chips), 4):
        term = dot(jnp.concatenate(left[n:n + 4], axis=1), jnp.concatenate(right[n:n + 4], axis=0))
        total = term if total is None else total + term
    return total, copies


def early_square(where, *refs):
    both, parts, (early, line, panel), (sems,) = refs[:4], refs[4:7], refs[7:10], refs[10:]
    core, z = where[2], where[3]
    for d in range(4):
        for half, kind in enumerate((core, 1 - core)):
            for t in range(4):
                line[:, aligned(((z + d) & 3) * 8 + t * 2 + kind, B)] = (
                    both[d][half * ROWS:(half + 1) * ROWS, t * B:(t + 1) * B])
    chips = [(parts[n], i * ROWS, i, EARLY[n]) for n in range(3) for i in range(4)]
    value, copies = chips_times(where, line, chips, panel, sems)
    early[...] = value
    for copy in copies:
        copy.wait()


def second_square(where, keep_s, two, early, line, _, square, low, panel, sems):
    x, y, core, z = where[0], where[1], where[2], where[3]
    value, copies = chips_times(where, line, [(two, i * ROWS, i, 2) for i in range(4)], panel, sems)
    value = early[...] + value
    for t in range(2):
        for u in range(4):
            keep = keep_s[1, (x * 4 + y) * 2 + t, z * 8 + u * 2 + core].astype(jnp.float32)
            piece = value[t * B:(t + 1) * B, u * B:(u + 1) * B] * keep
            square[t * B:(t + 1) * B, u * B:(u + 1) * B] = piece
            low[t * B:(t + 1) * B, u * B:(u + 1) * B] = piece.astype(jnp.bfloat16)
    for copy in copies:
        copy.wait()


def second_density(where, *refs):
    others, (early, square, panel, stay, leave) = refs[:3], refs[3:]
    value = 3.0 * square[...] - 2.0 * late_cube(where, others, early, panel)
    first = where[2] == 0
    stay[...] = jnp.where(first, value[:B], value[B:])
    leave[...] = jnp.where(first, value[B:], value[:B])


def join(where, stay, come, out):
    first = where[2] == 0
    for t in range(4):
        mine, its = stay[:, t * B:(t + 1) * B], come[:, t * B:(t + 1) * B]
        out[:, 2 * t * B:(2 * t + 1) * B] = jnp.where(first, mine, its)
        out[:, (2 * t + 1) * B:(2 * t + 2) * B] = jnp.where(first, its, mine)


SMEM = pl.BlockSpec(memory_space=pltpu.SMEM)
VMEM = pl.BlockSpec(memory_space=pltpu.VMEM)


def call(kernel, n_smem, ins, outs, scratch, flops, moved, aliases={}):
    return pl.pallas_call(
        kernel,
        in_specs=[SMEM] * n_smem + [VMEM] * (len(ins) - n_smem),
        out_specs=[VMEM] * len(outs),
        out_shape=outs,
        scratch_shapes=scratch,
        input_output_aliases=aliases,
        cost_estimate=pl.CostEstimate(flops=flops, bytes_accessed=moved, transcendentals=0),
        compiler_params=pltpu.CompilerParams(vmem_limit_bytes=12 * MIB),
    )(*ins)


def body(coeffs, coef_pattern, keep_density, keep_square):
    r, z = lax.axis_index("row"), lax.axis_index("col")
    x, y, core = r // 8, (r // 2) % 4, r % 2
    where = jnp.stack([x, y, core, z]).astype(jnp.int32)
    low_block = jax.ShapeDtypeStruct((ROWS, COLS), jnp.bfloat16)
    full_block = jax.ShapeDtypeStruct((ROWS, COLS), jnp.float32)
    panel_shape = jax.ShapeDtypeStruct((N, COLS), jnp.bfloat16)
    line_shape = jax.ShapeDtypeStruct((ROWS, N), jnp.bfloat16)
    wide_shape = jax.ShapeDtypeStruct((N, N // 2), jnp.bfloat16)
    block_flops = 2 * ROWS * N * COLS
    pair_flops = 2 * 512 * 512 * K

    kept = jnp.concatenate(gather(coeffs, from_z), axis=1)
    pattern = lax.dynamic_slice(coef_pattern, (r, 0), (1, 8)).reshape(4, 2)
    pattern = jnp.concatenate([pattern, pattern], axis=0)
    pattern = lax.dynamic_slice(pattern, (z, 0), (4, 2)).reshape(1, 8)
    kept = kept * jnp.repeat(pattern, B, 1).astype(jnp.bfloat16)
    near = jnp.concatenate(gather(kept, from_first), axis=0)
    own0, own1, own2, own3 = gather(near, from_second)
    other0, other1, other3 = other_core(own0), other_core(own1), other_core(own3)
    panel, line = call(
        early_density, 2, [where, keep_density, own0, own1, own3, other0, other1, other3],
        [wide_shape, line_shape], [], 2 * pair_flops, 2 * MIB)
    panel, line, own2 = lax.optimization_barrier((panel, line, own2))
    other2 = other_core(own2)
    panel, line, low, square = call(
        first_square, 3,
        [where, keep_density, keep_square, own0, own1, own2, own3, other0, other1, other2, other3, panel, line],
        [wide_shape, line_shape, jax.ShapeDtypeStruct((ROWS, N // 2), jnp.bfloat16), full_block],
        [pltpu.VMEM((ROWS, N // 2), jnp.float32)],
        15 * pair_flops + 4 * block_flops, 40 * MIB, {11: 0, 12: 1})

    its = other_core(low)
    early, columns = call(
        early_first_cube, 1, [where, low, panel], [full_block, panel_shape], [], block_flops // 2, 12 * MIB)
    (current,) = call(
        first_density, 2, [where, keep_density, its, columns, early, square], [low_block], [],
        block_flops // 2, 4 * MIB)

    near = jnp.concatenate(gather(current, from_first), axis=0)
    part0, part1, part2, part3 = gather(near, from_second)
    both = gather(jnp.concatenate([current, other_core(current)], axis=0), from_z)
    early, line, panel = call(
        early_square, 1, [where, *both, part0, part1, part3], [full_block, line_shape, panel_shape],
        [pltpu.SemaphoreType.DMA((12,))], block_flops * 3 // 4, 12 * MIB)
    early, part2 = lax.optimization_barrier((early, part2))
    square, low, panel = call(
        second_square, 2, [where, keep_square, part2, early, line, panel],
        [full_block, low_block, panel_shape],
        [pltpu.SemaphoreType.DMA((4,))], block_flops // 4, 6 * MIB, {5: 2})

    own = gather(low, from_z)
    other = [other_core(part) for part in own]
    (early,) = call(
        early_cube, 1, [where, *own, other[0], panel], [full_block], [], block_flops * 5 // 8, 4 * MIB)
    half = jax.ShapeDtypeStruct((B, COLS), jnp.float32)
    stay, leave = call(
        second_density, 1, [where, *other[1:], early, square, panel], [half, half], [],
        block_flops * 3 // 8, 3 * MIB)
    come = other_core(leave)
    (out,) = call(
        join, 1, [where, stay, come], [jax.ShapeDtypeStruct((B, 2 * COLS), jnp.float32)], [], 0, MIB)
    return out


def solution(mesh):
    placed = (P("row", "col"), P(), P(), P())
    return jax.shard_map(
        body, mesh=mesh, in_specs=placed, out_specs=P("row", "col"), check_vma=False
    )
```

```python
import functools

import jax
import jax.numpy as jnp
from jax import lax
from jax.experimental import pallas as pl
from jax.experimental.pallas import tpu as pltpu
from jax.sharding import PartitionSpec as P

B = 128
N = 4096
K = 1024
ROWS = 256
COLS = 512
AXES = ("row", "col")
MIB = 1024 * 1024


def device(x, y, core, z):
    return (((x % 4) * 4 + y % 4) * 2 + core) * 4 + z % 4


def pairs(target):
    return [
        (device(x, y, core, z), device(*target(x, y, core, z)))
        for x in range(4) for y in range(4) for core in range(2) for z in range(4)
    ]


def other_core(a):
    return lax.ppermute(a, AXES, pairs(lambda x, y, core, z: (x, y, 1 - core, z)))


def from_z(a, d):
    return lax.ppermute(a, AXES, pairs(lambda x, y, core, z: (x, y, core, z - d)))


def from_first(a, d):
    return lax.ppermute(a, AXES, pairs(
        lambda x, y, core, z: (x - d, y, core, z) if core == 0 else (x, y - d, core, z)))


def from_second(a, d):
    return lax.ppermute(a, AXES, pairs(
        lambda x, y, core, z: (x, y - d, core, z) if core == 0 else (x - d, y, core, z)))


def gather(a, fetch):
    one, three, two = fetch(a, 1), fetch(a, 3), fetch(a, 2)
    return [a, one, two, three]


def place(x, y, kind, first, second):
    px = jnp.where(kind == 0, x + first, x + second) & 3
    py = jnp.where(kind == 0, y + second, y + first) & 3
    return px, py


def dot_t(a, b):
    return lax.dot_general(a, b, (((1,), (1,)), ((), ())), preferred_element_type=jnp.float32)


def dot(a, b):
    return jnp.dot(a, b, preferred_element_type=jnp.float32)


def aligned(block, size):
    return pl.ds(pl.multiple_of(block * size, size), size)


def block_at(x, y, kind, place_in_order):
    px, py = place(x, y, kind, place_in_order % 4, place_in_order // 4)
    return px * 8 + py * 2 + kind


def some_rows(where, keep_d, rows, half, parts, line):
    x, y, core = where[0], where[1], where[2]
    kind = core if half == 0 else 1 - core
    for n, part in parts.items():
        value = dot_t(rows[...], part[...])
        for u in range(4):
            block = block_at(x, y, kind, n * 4 + u)
            at = (half * 16 + n * 4 + u) * B
            for t in range(2):
                keep = keep_d[0, (x * 4 + y) * 2 + t, block].astype(jnp.float32)
                piece = value[t * B:(t + 1) * B, u * B:(u + 1) * B] * keep
                line[t * B:(t + 1) * B, at:at + B] = piece.astype(jnp.bfloat16)


def some_columns(where, keep_d, half, parts, columns, panel, skip=()):
    x, y, core = where[0], where[1], where[2]
    kind = core if half == 0 else 1 - core
    for n, part in parts.items():
        for m, column in columns.items():
            if (n, m) in skip:
                continue
            value = dot_t(part[...], column[...])
            for i in range(4):
                row_block = block_at(x, y, kind, n * 4 + i)
                at = (half * 16 + n * 4 + i) * B
                for u in range(4):
                    keep = keep_d[0, row_block, block_at(x, y, core, m * 4 + u)].astype(jnp.float32)
                    piece = value[i * B:(i + 1) * B, u * B:(u + 1) * B] * keep
                    to = (m * 4 + u) * B
                    panel[at:at + B, to:to + B] = piece.astype(jnp.bfloat16)


EARLY = (0, 1, 3)


def density_0(where, keep_d, own0, other0, panel, line, rows):
    first = where[2] == 0
    mine, its = own0[:B, :], other0[:B, :]
    rows[:B, :] = jnp.where(first, mine, its)
    rows[B:, :] = jnp.where(first, its, mine)
    for half, part in enumerate((own0, other0)):
        some_rows(where, keep_d, rows, half, {0: part}, line)
        some_columns(where, keep_d, half, {0: part}, {0: own0}, panel)


def density_1(where, keep_d, own0, own1, own3, other0, rows, _, __, panel, line):
    own = {0: own0, 1: own1, 3: own3}
    some_rows(where, keep_d, rows, 0, {1: own1, 3: own3}, line)
    some_columns(where, keep_d, 0, own, own, panel, ((0, 0),))
    some_columns(where, keep_d, 1, {0: other0}, {1: own1, 3: own3}, panel)


def density_2(where, keep_d, own0, own1, own2, own3, other0, rows, _, __, panel, line):
    some_rows(where, keep_d, rows, 0, {2: own2}, line)
    some_columns(where, keep_d, 0, {2: own2}, {0: own0, 1: own1, 2: own2, 3: own3}, panel)
    some_columns(where, keep_d, 0, {0: own0, 1: own1, 3: own3}, {2: own2}, panel)
    some_columns(where, keep_d, 1, {0: other0}, {2: own2}, panel)


def density_3(where, keep_d, own0, own1, own2, own3, other1, other3, rows, _, __, panel, line):
    other = {1: other1, 3: other3}
    some_rows(where, keep_d, rows, 1, other, line)
    some_columns(where, keep_d, 1, other, {0: own0, 1: own1, 2: own2, 3: own3}, panel)


def first_square(where, keep_d, keep_s, own0, own1, own2, own3, other2, rows, _, __, panel, line, low, square, total):
    x, y, core, z = where[0], where[1], where[2], where[3]
    some_rows(where, keep_d, rows, 1, {2: other2}, line)
    some_columns(where, keep_d, 1, {2: other2}, {0: own0, 1: own1, 2: own2, 3: own3}, panel)
    for half in range(2):
        value = dot(line[...], panel[:, half * 1024:(half + 1) * 1024])
        for t in range(2):
            for u in range(8):
                block = block_at(x, y, core, half * 8 + u)
                keep = keep_s[0, (x * 4 + y) * 2 + t, block].astype(jnp.float32)
                piece = value[t * B:(t + 1) * B, u * B:(u + 1) * B] * keep
                at = (half * 8 + u) * B
                total[t * B:(t + 1) * B, at:at + B] = piece
                low[t * B:(t + 1) * B, at:at + B] = piece.astype(jnp.bfloat16)
    for t in range(4):
        square[:, t * B:(t + 1) * B] = total[:, aligned(column_at(where, t), B)]


def column_at(where, t):
    x, y, core, z = where[0], where[1], where[2], where[3]
    dx, dy = (z - x) & 3, (t - y) & 3
    return jnp.where(core == 0, dy * 4 + dx, dx * 4 + dy)


def early_first_cube(where, low, panel, early, columns):
    for t in range(4):
        at = aligned(column_at(where, t), B)
        columns[:, t * B:(t + 1) * B] = panel[:, at]
    early[...] = dot(low[...], columns[:2048, :])


def first_density(where, keep_d, its, columns, early, square, out):
    x, y, core, z = where[0], where[1], where[2], where[3]
    value = 3.0 * square[...] - 2.0 * (early[...] + dot(its[...], columns[2048:, :]))
    for t in range(2):
        for u in range(4):
            keep = keep_d[1, (x * 4 + y) * 2 + t, z * 8 + u * 2 + core].astype(jnp.float32)
            piece = value[t * B:(t + 1) * B, u * B:(u + 1) * B] * keep
            out[t * B:(t + 1) * B, u * B:(u + 1) * B] = piece.astype(jnp.bfloat16)


def parts_times_panel(parts, z, panel):
    total = None
    for ref, d, kind in parts:
        rows = [panel[aligned(((z + d) & 3) * 8 + t * 2 + kind, B), :] for t in range(4)]
        term = dot(ref[...], jnp.concatenate(rows, axis=0))
        total = term if total is None else total + term
    return total


def early_cube(where, *refs):
    own, other, panel, out = refs[:4], refs[4], refs[5], refs[6]
    core, z = where[2], where[3]
    parts = [(own[d], d, core) for d in range(4)] + [(other, 0, 1 - core)]
    out[...] = parts_times_panel(parts, z, panel)


def chips_times(where, line, chips, panel, sems):
    x, y, core = where[0], where[1], where[2]
    copies, left, right = [], [], []
    for n, (ref, offset, first, second) in enumerate(chips):
        px, py = place(x, y, core, first, second)
        copies.append(pltpu.make_async_copy(
            ref.at[pl.ds(offset, ROWS)], panel.at[aligned(px * 4 + py, ROWS)], sems.at[n]))
        copies[-1].start()
        left.append(line[:, aligned(px * 4 + py, ROWS)])
        right.append(ref[offset:offset + ROWS, :])
    total = None
    for n in range(0, len(chips), 4):
        term = dot(jnp.concatenate(left[n:n + 4], axis=1), jnp.concatenate(right[n:n + 4], axis=0))
        total = term if total is None else total + term
    return total, copies


def early_square(where, *refs):
    own, other, near, far, (early, line, panel), (sems,) = (
        refs[:4], refs[4:8], refs[8], refs[9:13], refs[13:16], refs[16:])
    core, z = where[2], where[3]
    for d in range(4):
        for ref, kind in ((own[d], core), (other[d], 1 - core)):
            for t in range(4):
                line[:, aligned(((z + d) & 3) * 8 + t * 2 + kind, B)] = ref[:, t * B:(t + 1) * B]
    chips = [(near, i * ROWS, i, 0) for i in range(4)] + [(far[i], 0, i, 2) for i in range(4)]
    value, copies = chips_times(where, line, chips, panel, sems)
    early[...] = value
    for copy in copies:
        copy.wait()


def second_square(where, keep_s, one, three, early, line, _, square, low, panel, sems):
    x, y, core, z = where[0], where[1], where[2], where[3]
    chips = [(ref, i * ROWS, i, j) for ref, j in ((one, 1), (three, 3)) for i in range(4)]
    value, copies = chips_times(where, line, chips, panel, sems)
    value = early[...] + value
    for t in range(2):
        for u in range(4):
            keep = keep_s[1, (x * 4 + y) * 2 + t, z * 8 + u * 2 + core].astype(jnp.float32)
            piece = value[t * B:(t + 1) * B, u * B:(u + 1) * B] * keep
            square[t * B:(t + 1) * B, u * B:(u + 1) * B] = piece
            low[t * B:(t + 1) * B, u * B:(u + 1) * B] = piece.astype(jnp.bfloat16)
    for copy in copies:
        copy.wait()


def second_density(leave, where, *refs):
    others, (early, square, panel), (come, out) = refs[:3], refs[3:6], (refs[6:] if not leave else (None,) + refs[6:])
    core, z = where[2], where[3]
    at = aligned(1 - core if leave else core, B)
    total = early[at, :]
    for d in (1, 2, 3):
        rows = [panel[aligned(((z + d) & 3) * 8 + t * 2 + 1 - core, B), :] for t in range(4)]
        total = total + dot(others[d - 1][at, :], jnp.concatenate(rows, axis=0))
    value = 3.0 * square[at, :] - 2.0 * total
    if leave:
        out[...] = value
        return
    first = core == 0
    for t in range(4):
        mine, its = value[:, t * B:(t + 1) * B], come[:, t * B:(t + 1) * B]
        out[:, 2 * t * B:(2 * t + 1) * B] = jnp.where(first, mine, its)
        out[:, (2 * t + 1) * B:(2 * t + 2) * B] = jnp.where(first, its, mine)


SMEM = pl.BlockSpec(memory_space=pltpu.SMEM)
VMEM = pl.BlockSpec(memory_space=pltpu.VMEM)


def call(kernel, n_smem, ins, outs, scratch, flops, moved, aliases={}):
    return pl.pallas_call(
        kernel,
        in_specs=[SMEM] * n_smem + [VMEM] * (len(ins) - n_smem),
        out_specs=[VMEM] * len(outs),
        out_shape=outs,
        scratch_shapes=scratch,
        input_output_aliases=aliases,
        cost_estimate=pl.CostEstimate(flops=flops, bytes_accessed=moved, transcendentals=0),
        compiler_params=pltpu.CompilerParams(vmem_limit_bytes=12 * MIB),
    )(*ins)


def body(coeffs, coef_pattern, keep_density, keep_square):
    r, z = lax.axis_index("row"), lax.axis_index("col")
    x, y, core = r // 8, (r // 2) % 4, r % 2
    where = jnp.stack([x, y, core, z]).astype(jnp.int32)
    low_block = jax.ShapeDtypeStruct((ROWS, COLS), jnp.bfloat16)
    full_block = jax.ShapeDtypeStruct((ROWS, COLS), jnp.float32)
    panel_shape = jax.ShapeDtypeStruct((N, COLS), jnp.bfloat16)
    line_shape = jax.ShapeDtypeStruct((ROWS, N), jnp.bfloat16)
    wide_shape = jax.ShapeDtypeStruct((N, N // 2), jnp.bfloat16)
    block_flops = 2 * ROWS * N * COLS
    pair_flops = 2 * 512 * 512 * K

    kept = jnp.concatenate(gather(coeffs, from_z), axis=1)
    pattern = lax.dynamic_slice(coef_pattern, (r, 0), (1, 8)).reshape(4, 2)
    pattern = jnp.concatenate([pattern, pattern], axis=0)
    pattern = lax.dynamic_slice(pattern, (z, 0), (4, 2)).reshape(1, 8)
    kept = kept * jnp.repeat(pattern, B, 1).astype(jnp.bfloat16)
    near = jnp.concatenate(gather(kept, from_first), axis=0)
    own0, own1, own2, own3 = gather(near, from_second)
    other0 = other_core(own0)
    rows_shape = jax.ShapeDtypeStruct((ROWS, K), jnp.bfloat16)
    out_shapes = [wide_shape, line_shape]
    panel, line, rows = call(
        density_0, 2, [where, keep_density, own0, other0], out_shapes + [rows_shape], [], pair_flops // 8, MIB)
    panel, line, own1, own3 = lax.optimization_barrier((panel, line, own1, own3))
    other1, other3 = other_core(own1), other_core(own3)
    panel, line = call(
        density_1, 2, [where, keep_density, own0, own1, own3, other0, rows, panel, line],
        out_shapes, [], pair_flops // 8, MIB, {7: 0, 8: 1})
    panel, line, own2 = lax.optimization_barrier((panel, line, own2))
    other2 = other_core(own2)
    panel, line = call(
        density_2, 2, [where, keep_density, own0, own1, own2, own3, other0, rows, panel, line],
        out_shapes, [], 9 * pair_flops, 8 * MIB, {8: 0, 9: 1})
    panel, line = call(
        density_3, 2, [where, keep_density, own0, own1, own2, own3, other1, other3, rows, panel, line],
        out_shapes, [], 9 * pair_flops, 8 * MIB, {9: 0, 10: 1})
    panel, line, low, square = call(
        first_square, 3,
        [where, keep_density, keep_square, own0, own1, own2, own3, other2, rows, panel, line],
        out_shapes + [jax.ShapeDtypeStruct((ROWS, N // 2), jnp.bfloat16), full_block],
        [pltpu.VMEM((ROWS, N // 2), jnp.float32)],
        4 * pair_flops + 4 * block_flops, 20 * MIB, {9: 0, 10: 1})

    its = other_core(low)
    early, columns = call(
        early_first_cube, 1, [where, low, panel], [full_block, panel_shape], [], block_flops // 2, 12 * MIB)
    (current,) = call(
        first_density, 2, [where, keep_density, its, columns, early, square], [low_block], [],
        block_flops // 2, 4 * MIB)

    near = gather(current, from_first)
    far = from_second(current, 2)
    own = gather(current, from_z)
    current, far, own1, own2, own3 = lax.optimization_barrier((current, far, *own[1:]))
    near = jnp.concatenate(near, axis=0)
    one, three = from_second(near, 1), from_second(near, 3)
    far = gather(far, from_first)
    own = [current, own1, own2, own3]
    other = [other_core(part) for part in own]
    early, line, panel = call(
        early_square, 1, [where, *own, *other, near, *far], [full_block, line_shape, panel_shape],
        [pltpu.SemaphoreType.DMA((8,))], block_flops // 2, 10 * MIB)
    square, low, panel = call(
        second_square, 2, [where, keep_square, one, three, early, line, panel],
        [full_block, low_block, panel_shape],
        [pltpu.SemaphoreType.DMA((8,))], block_flops // 2, 8 * MIB, {6: 2})

    own = gather(low, from_z)
    other = [other_core(part) for part in own]
    (early,) = call(
        early_cube, 1, [where, *own, other[0], panel], [full_block], [], block_flops * 5 // 8, 4 * MIB)
    last = [*other[1:], early, square, panel]
    (leave,) = call(
        functools.partial(second_density, True), 1, [where, *last],
        [jax.ShapeDtypeStruct((B, COLS), jnp.float32)], [], block_flops * 3 // 16, 3 * MIB)
    (out,) = call(
        functools.partial(second_density, False), 1, [where, *last, other_core(leave)],
        [jax.ShapeDtypeStruct((B, 2 * COLS), jnp.float32)], [], block_flops * 3 // 16, 3 * MIB)
    return out


def solution(mesh):
    placed = (P("row", "col"), P(), P(), P())
    return jax.shard_map(
        body, mesh=mesh, in_specs=placed, out_specs=P("row", "col"), check_vma=False
    )
```

```python
import functools

import jax
import jax.numpy as jnp
from jax import lax
from jax.experimental import pallas as pl
from jax.experimental.pallas import tpu as pltpu
from jax.sharding import PartitionSpec as P

B = 128
N = 4096
K = 1024
ROWS = 256
COLS = 512
AXES = ("row", "col")
MIB = 1024 * 1024


def device(x, y, core, z):
    return (((x % 4) * 4 + y % 4) * 2 + core) * 4 + z % 4


def pairs(target):
    return [
        (device(x, y, core, z), device(*target(x, y, core, z)))
        for x in range(4) for y in range(4) for core in range(2) for z in range(4)
    ]


def other_core(a):
    return lax.ppermute(a, AXES, pairs(lambda x, y, core, z: (x, y, 1 - core, z)))


def from_z(a, d):
    return lax.ppermute(a, AXES, pairs(lambda x, y, core, z: (x, y, core, z - d)))


def from_first(a, d):
    return lax.ppermute(a, AXES, pairs(
        lambda x, y, core, z: (x - d, y, core, z) if core == 0 else (x, y - d, core, z)))


def from_second(a, d):
    return lax.ppermute(a, AXES, pairs(
        lambda x, y, core, z: (x, y - d, core, z) if core == 0 else (x - d, y, core, z)))


def gather(a, fetch):
    one, three, two = fetch(a, 1), fetch(a, 3), fetch(a, 2)
    return [a, one, two, three]


def place(x, y, kind, first, second):
    px = jnp.where(kind == 0, x + first, x + second) & 3
    py = jnp.where(kind == 0, y + second, y + first) & 3
    return px, py


def dot_t(a, b):
    return lax.dot_general(a, b, (((1,), (1,)), ((), ())), preferred_element_type=jnp.float32)


def dot(a, b):
    return jnp.dot(a, b, preferred_element_type=jnp.float32)


def aligned(block, size):
    return pl.ds(pl.multiple_of(block * size, size), size)


def block_at(x, y, kind, place_in_order):
    px, py = place(x, y, kind, place_in_order % 4, place_in_order // 4)
    return px * 8 + py * 2 + kind


def some_rows(where, keep_d, rows, half, parts, line):
    x, y, core = where[0], where[1], where[2]
    kind = core if half == 0 else 1 - core
    for n, part in parts.items():
        value = dot_t(rows[...], part[...])
        for u in range(4):
            block = block_at(x, y, kind, n * 4 + u)
            at = (half * 16 + n * 4 + u) * B
            for t in range(2):
                keep = keep_d[0, (x * 4 + y) * 2 + t, block].astype(jnp.float32)
                piece = value[t * B:(t + 1) * B, u * B:(u + 1) * B] * keep
                line[t * B:(t + 1) * B, at:at + B] = piece.astype(jnp.bfloat16)


def some_columns(where, keep_d, half, parts, columns, panel, skip=()):
    x, y, core = where[0], where[1], where[2]
    kind = core if half == 0 else 1 - core
    for n, part in parts.items():
        for m, column in columns.items():
            if (n, m) in skip:
                continue
            value = dot_t(part[...], column[...])
            for i in range(4):
                row_block = block_at(x, y, kind, n * 4 + i)
                at = (half * 16 + n * 4 + i) * B
                for u in range(4):
                    keep = keep_d[0, row_block, block_at(x, y, core, m * 4 + u)].astype(jnp.float32)
                    piece = value[i * B:(i + 1) * B, u * B:(u + 1) * B] * keep
                    to = (m * 4 + u) * B
                    panel[at:at + B, to:to + B] = piece.astype(jnp.bfloat16)


EARLY = (0, 1, 3)


def density_0(where, keep_d, own0, other0, panel, line, rows):
    first = where[2] == 0
    mine, its = own0[:B, :], other0[:B, :]
    rows[:B, :] = jnp.where(first, mine, its)
    rows[B:, :] = jnp.where(first, its, mine)
    for half, part in enumerate((own0, other0)):
        some_rows(where, keep_d, rows, half, {0: part}, line)
        some_columns(where, keep_d, half, {0: part}, {0: own0}, panel)


def density_1(where, keep_d, own0, own1, own3, other0, rows, _, __, panel, line):
    own = {0: own0, 1: own1, 3: own3}
    some_rows(where, keep_d, rows, 0, {1: own1, 3: own3}, line)
    some_columns(where, keep_d, 0, own, own, panel, ((0, 0),))
    some_columns(where, keep_d, 1, {0: other0}, {1: own1, 3: own3}, panel)


def density_2(where, keep_d, own0, own1, own3, other1, other3, rows, _, __, panel, line):
    other = {1: other1, 3: other3}
    some_rows(where, keep_d, rows, 1, other, line)
    some_columns(where, keep_d, 1, other, {0: own0, 1: own1, 3: own3}, panel)


def density_3(where, keep_d, own0, own1, own2, own3, other0, other1, other3, rows, _, __, panel, line):
    some_rows(where, keep_d, rows, 0, {2: own2}, line)
    some_columns(where, keep_d, 0, {2: own2}, {0: own0, 1: own1, 2: own2, 3: own3}, panel)
    some_columns(where, keep_d, 0, {0: own0, 1: own1, 3: own3}, {2: own2}, panel)
    some_columns(where, keep_d, 1, {0: other0, 1: other1, 3: other3}, {2: own2}, panel)


def first_square(where, keep_d, keep_s, own0, own1, own2, own3, other2, rows, _, __, panel, line, low, square, total):
    x, y, core, z = where[0], where[1], where[2], where[3]
    some_rows(where, keep_d, rows, 1, {2: other2}, line)
    some_columns(where, keep_d, 1, {2: other2}, {0: own0, 1: own1, 2: own2, 3: own3}, panel)
    for half in range(2):
        value = dot(line[...], panel[:, half * 1024:(half + 1) * 1024])
        for t in range(2):
            for u in range(8):
                block = block_at(x, y, core, half * 8 + u)
                keep = keep_s[0, (x * 4 + y) * 2 + t, block].astype(jnp.float32)
                piece = value[t * B:(t + 1) * B, u * B:(u + 1) * B] * keep
                at = (half * 8 + u) * B
                total[t * B:(t + 1) * B, at:at + B] = piece
                low[t * B:(t + 1) * B, at:at + B] = piece.astype(jnp.bfloat16)
    for t in range(4):
        square[:, t * B:(t + 1) * B] = total[:, aligned(column_at(where, t), B)]


def column_at(where, t):
    x, y, core, z = where[0], where[1], where[2], where[3]
    dx, dy = (z - x) & 3, (t - y) & 3
    return jnp.where(core == 0, dy * 4 + dx, dx * 4 + dy)


def early_first_cube(where, low, panel, early, columns):
    for t in range(4):
        at = aligned(column_at(where, t), B)
        columns[:, t * B:(t + 1) * B] = panel[:, at]
    early[...] = dot(low[...], columns[:2048, :])


def first_density(where, keep_d, its, columns, early, square, out):
    x, y, core, z = where[0], where[1], where[2], where[3]
    value = 3.0 * square[...] - 2.0 * (early[...] + dot(its[...], columns[2048:, :]))
    for t in range(2):
        for u in range(4):
            keep = keep_d[1, (x * 4 + y) * 2 + t, z * 8 + u * 2 + core].astype(jnp.float32)
            piece = value[t * B:(t + 1) * B, u * B:(u + 1) * B] * keep
            out[t * B:(t + 1) * B, u * B:(u + 1) * B] = piece.astype(jnp.bfloat16)


def parts_times_panel(parts, z, panel):
    total = None
    for ref, d, kind in parts:
        rows = [panel[aligned(((z + d) & 3) * 8 + t * 2 + kind, B), :] for t in range(4)]
        term = dot(ref[...], jnp.concatenate(rows, axis=0))
        total = term if total is None else total + term
    return total


def early_cube(where, *refs):
    own, other, panel, out = refs[:4], refs[4], refs[5], refs[6]
    core, z = where[2], where[3]
    parts = [(own[d], d, core) for d in range(4)] + [(other, 0, 1 - core)]
    out[...] = parts_times_panel(parts, z, panel)


def chips_times(where, line, chips, panel, sems):
    x, y, core = where[0], where[1], where[2]
    copies, left, right = [], [], []
    for n, (ref, offset, first, second) in enumerate(chips):
        px, py = place(x, y, core, first, second)
        copies.append(pltpu.make_async_copy(
            ref.at[pl.ds(offset, ROWS)], panel.at[aligned(px * 4 + py, ROWS)], sems.at[n]))
        copies[-1].start()
        left.append(line[:, aligned(px * 4 + py, ROWS)])
        right.append(ref[offset:offset + ROWS, :])
    total = None
    for n in range(0, len(chips), 4):
        term = dot(jnp.concatenate(left[n:n + 4], axis=1), jnp.concatenate(right[n:n + 4], axis=0))
        total = term if total is None else total + term
    return total, copies


def early_square(where, *refs):
    own, other, near, far, (early, line, panel), (sems,) = (
        refs[:4], refs[4:8], refs[8], refs[9:13], refs[13:16], refs[16:])
    core, z = where[2], where[3]
    for d in range(4):
        for ref, kind in ((own[d], core), (other[d], 1 - core)):
            for t in range(4):
                line[:, aligned(((z + d) & 3) * 8 + t * 2 + kind, B)] = ref[:, t * B:(t + 1) * B]
    chips = [(near, i * ROWS, i, 0) for i in range(4)] + [(far[i], 0, i, 2) for i in range(4)]
    value, copies = chips_times(where, line, chips, panel, sems)
    early[...] = value
    for copy in copies:
        copy.wait()


def second_square(where, keep_s, one, three, early, line, _, square, low, panel, sems):
    x, y, core, z = where[0], where[1], where[2], where[3]
    chips = [(ref, i * ROWS, i, j) for ref, j in ((one, 1), (three, 3)) for i in range(4)]
    value, copies = chips_times(where, line, chips, panel, sems)
    value = early[...] + value
    for t in range(2):
        for u in range(4):
            keep = keep_s[1, (x * 4 + y) * 2 + t, z * 8 + u * 2 + core].astype(jnp.float32)
            piece = value[t * B:(t + 1) * B, u * B:(u + 1) * B] * keep
            square[t * B:(t + 1) * B, u * B:(u + 1) * B] = piece
            low[t * B:(t + 1) * B, u * B:(u + 1) * B] = piece.astype(jnp.bfloat16)
    for copy in copies:
        copy.wait()


def second_density(leave, where, *refs):
    others, (early, square, panel), (come, out) = refs[:3], refs[3:6], (refs[6:] if not leave else (None,) + refs[6:])
    core, z = where[2], where[3]
    at = aligned(1 - core if leave else core, B)
    total = early[at, :]
    for d in (1, 2, 3):
        rows = [panel[aligned(((z + d) & 3) * 8 + t * 2 + 1 - core, B), :] for t in range(4)]
        total = total + dot(others[d - 1][at, :], jnp.concatenate(rows, axis=0))
    value = 3.0 * square[at, :] - 2.0 * total
    if leave:
        out[...] = value
        return
    first = core == 0
    for t in range(4):
        mine, its = value[:, t * B:(t + 1) * B], come[:, t * B:(t + 1) * B]
        out[:, 2 * t * B:(2 * t + 1) * B] = jnp.where(first, mine, its)
        out[:, (2 * t + 1) * B:(2 * t + 2) * B] = jnp.where(first, its, mine)


SMEM = pl.BlockSpec(memory_space=pltpu.SMEM)
VMEM = pl.BlockSpec(memory_space=pltpu.VMEM)


def call(kernel, n_smem, ins, outs, scratch, flops, moved, aliases={}):
    return pl.pallas_call(
        kernel,
        in_specs=[SMEM] * n_smem + [VMEM] * (len(ins) - n_smem),
        out_specs=[VMEM] * len(outs),
        out_shape=outs,
        scratch_shapes=scratch,
        input_output_aliases=aliases,
        cost_estimate=pl.CostEstimate(flops=flops, bytes_accessed=moved, transcendentals=0),
        compiler_params=pltpu.CompilerParams(vmem_limit_bytes=12 * MIB),
    )(*ins)


def body(coeffs, coef_pattern, keep_density, keep_square):
    r, z = lax.axis_index("row"), lax.axis_index("col")
    x, y, core = r // 8, (r // 2) % 4, r % 2
    where = jnp.stack([x, y, core, z]).astype(jnp.int32)
    low_block = jax.ShapeDtypeStruct((ROWS, COLS), jnp.bfloat16)
    full_block = jax.ShapeDtypeStruct((ROWS, COLS), jnp.float32)
    panel_shape = jax.ShapeDtypeStruct((N, COLS), jnp.bfloat16)
    line_shape = jax.ShapeDtypeStruct((ROWS, N), jnp.bfloat16)
    wide_shape = jax.ShapeDtypeStruct((N, N // 2), jnp.bfloat16)
    block_flops = 2 * ROWS * N * COLS
    pair_flops = 2 * 512 * 512 * K

    kept = jnp.concatenate(gather(coeffs, from_z), axis=1)
    pattern = lax.dynamic_slice(coef_pattern, (r, 0), (1, 8)).reshape(4, 2)
    pattern = jnp.concatenate([pattern, pattern], axis=0)
    pattern = lax.dynamic_slice(pattern, (z, 0), (4, 2)).reshape(1, 8)
    kept = kept * jnp.repeat(pattern, B, 1).astype(jnp.bfloat16)
    near = jnp.concatenate(gather(kept, from_first), axis=0)
    own1, own3, other0 = from_second(near, 1), from_second(near, 3), other_core(near)
    rows_shape = jax.ShapeDtypeStruct((ROWS, K), jnp.bfloat16)
    out_shapes = [wide_shape, line_shape]
    panel, line, rows = call(
        density_0, 2, [where, keep_density, near, other0], out_shapes + [rows_shape], [], pair_flops // 8, MIB)
    panel, line, own0, own1, own3 = lax.optimization_barrier((panel, line, near, own1, own3))
    own2 = from_second(own0, 2)
    other1, other3 = other_core(own1), other_core(own3)
    panel, line = call(
        density_1, 2, [where, keep_density, own0, own1, own3, other0, rows, panel, line],
        out_shapes, [], 11 * pair_flops, 8 * MIB, {7: 0, 8: 1})
    panel, line = call(
        density_2, 2, [where, keep_density, own0, own1, own3, other1, other3, rows, panel, line],
        out_shapes, [], 7 * pair_flops, 8 * MIB, {8: 0, 9: 1})
    panel, line, own2 = lax.optimization_barrier((panel, line, own2))
    other2 = other_core(own2)
    panel, line = call(
        density_3, 2, [where, keep_density, own0, own1, own2, own3, other0, other1, other3, rows, panel, line],
        out_shapes, [], 10 * pair_flops, 8 * MIB, {10: 0, 11: 1})
    panel, line, low, square = call(
        first_square, 3,
        [where, keep_density, keep_square, own0, own1, own2, own3, other2, rows, panel, line],
        out_shapes + [jax.ShapeDtypeStruct((ROWS, N // 2), jnp.bfloat16), full_block],
        [pltpu.VMEM((ROWS, N // 2), jnp.float32)],
        4 * pair_flops + 4 * block_flops, 20 * MIB, {9: 0, 10: 1})

    its = other_core(low)
    early, columns = call(
        early_first_cube, 1, [where, low, panel], [full_block, panel_shape], [], block_flops // 2, 12 * MIB)
    (current,) = call(
        first_density, 2, [where, keep_density, its, columns, early, square], [low_block], [],
        block_flops // 2, 4 * MIB)

    own0, one, three, two, far = lax.optimization_barrier((
        current, from_first(current, 1), from_first(current, 3), from_first(current, 2), from_second(current, 2)))
    near = jnp.concatenate([own0, one, two, three], axis=0)
    one, three = from_second(near, 1), from_second(near, 3)
    own0, far, own1, own2, own3 = lax.optimization_barrier((own0, far, *gather(own0, from_z)[1:]))
    far = gather(far, from_first)
    own = [own0, own1, own2, own3]
    other = [other_core(part) for part in own]
    early, line, panel = call(
        early_square, 1, [where, *own, *other, near, *far], [full_block, line_shape, panel_shape],
        [pltpu.SemaphoreType.DMA((8,))], block_flops // 2, 10 * MIB)
    square, low, panel = call(
        second_square, 2, [where, keep_square, one, three, early, line, panel],
        [full_block, low_block, panel_shape],
        [pltpu.SemaphoreType.DMA((8,))], block_flops // 2, 8 * MIB, {6: 2})

    own = gather(low, from_z)
    other = [other_core(part) for part in own]
    (early,) = call(
        early_cube, 1, [where, *own, other[0], panel], [full_block], [], block_flops * 5 // 8, 4 * MIB)
    last = [*other[1:], early, square, panel]
    (leave,) = call(
        functools.partial(second_density, True), 1, [where, *last],
        [jax.ShapeDtypeStruct((B, COLS), jnp.float32)], [], block_flops * 3 // 16, 3 * MIB)
    (out,) = call(
        functools.partial(second_density, False), 1, [where, *last, other_core(leave)],
        [jax.ShapeDtypeStruct((B, 2 * COLS), jnp.float32)], [], block_flops * 3 // 16, 3 * MIB)
    return out


def solution(mesh):
    placed = (P("row", "col"), P(), P(), P())
    return jax.shard_map(
        body, mesh=mesh, in_specs=placed, out_specs=P("row", "col"), check_vma=False
    )
```

```python
import functools

import jax
import jax.numpy as jnp
from jax import lax
from jax.experimental import pallas as pl
from jax.experimental.pallas import tpu as pltpu
from jax.sharding import PartitionSpec as P

B = 128
N = 4096
K = 1024
ROWS = 256
COLS = 512
AXES = ("row", "col")
MIB = 1024 * 1024


def device(x, y, core, z):
    return (((x % 4) * 4 + y % 4) * 2 + core) * 4 + z % 4


def pairs(target):
    return [
        (device(x, y, core, z), device(*target(x, y, core, z)))
        for x in range(4) for y in range(4) for core in range(2) for z in range(4)
    ]


def other_core(a):
    return lax.ppermute(a, AXES, pairs(lambda x, y, core, z: (x, y, 1 - core, z)))


def from_z(a, d):
    return lax.ppermute(a, AXES, pairs(lambda x, y, core, z: (x, y, core, z - d)))


def from_first(a, d):
    return lax.ppermute(a, AXES, pairs(
        lambda x, y, core, z: (x - d, y, core, z) if core == 0 else (x, y - d, core, z)))


def from_second(a, d):
    return lax.ppermute(a, AXES, pairs(
        lambda x, y, core, z: (x, y - d, core, z) if core == 0 else (x - d, y, core, z)))


def gather(a, fetch):
    one, three, two = fetch(a, 1), fetch(a, 3), fetch(a, 2)
    return [a, one, two, three]


def place(x, y, kind, first, second):
    px = jnp.where(kind == 0, x + first, x + second) & 3
    py = jnp.where(kind == 0, y + second, y + first) & 3
    return px, py


def dot_t(a, b):
    return lax.dot_general(a, b, (((1,), (1,)), ((), ())), preferred_element_type=jnp.float32)


def dot(a, b):
    return jnp.dot(a, b, preferred_element_type=jnp.float32)


def aligned(block, size):
    return pl.ds(pl.multiple_of(block * size, size), size)


def block_at(x, y, kind, place_in_order):
    px, py = place(x, y, kind, place_in_order % 4, place_in_order // 4)
    return px * 8 + py * 2 + kind


def some_rows(where, keep_d, rows, half, parts, line):
    x, y, core = where[0], where[1], where[2]
    kind = core if half == 0 else 1 - core
    for n, part in parts.items():
        value = dot_t(rows[...], part[...])
        for u in range(4):
            block = block_at(x, y, kind, n * 4 + u)
            at = (half * 16 + n * 4 + u) * B
            for t in range(2):
                keep = keep_d[0, (x * 4 + y) * 2 + t, block].astype(jnp.float32)
                piece = value[t * B:(t + 1) * B, u * B:(u + 1) * B] * keep
                line[t * B:(t + 1) * B, at:at + B] = piece.astype(jnp.bfloat16)


def some_columns(where, keep_d, half, parts, columns, panel, mirrored=()):
    x, y, core = where[0], where[1], where[2]
    kind = core if half == 0 else 1 - core

    def put(value, kind, n, i, m, u, turn):
        keep = keep_d[0, block_at(x, y, kind, n * 4 + i), block_at(x, y, core, m * 4 + u)]
        piece = (value * keep.astype(jnp.float32)).astype(jnp.bfloat16)
        at, to = (half * 16 + n * 4 + i) * B, (m * 4 + u) * B
        panel[at:at + B, to:to + B] = piece.T if turn else piece

    for n, part in parts.items():
        for m, column in columns.items():
            if (n, m) in mirrored:
                continue
            value = dot_t(part[...], column[...])
            for i in range(4):
                for u in range(4):
                    piece = value[i * B:(i + 1) * B, u * B:(u + 1) * B]
                    put(piece, kind, n, i, m, u, False)
                    if (m, n) in mirrored:
                        put(piece, core, m, u, n, i, True)


EARLY = (0, 1, 3)


def density_0(where, keep_d, own0, other0, panel, line, rows):
    first = where[2] == 0
    mine, its = own0[:B, :], other0[:B, :]
    rows[:B, :] = jnp.where(first, mine, its)
    rows[B:, :] = jnp.where(first, its, mine)
    for half, part in enumerate((own0, other0)):
        some_rows(where, keep_d, rows, half, {0: part}, line)
        some_columns(where, keep_d, half, {0: part}, {0: own0}, panel)


def density_1(where, keep_d, own0, own1, own3, other0, rows, _, __, panel, line):
    own = {0: own0, 1: own1, 3: own3}
    some_rows(where, keep_d, rows, 0, {1: own1, 3: own3}, line)
    some_columns(where, keep_d, 0, {0: own0}, {1: own1, 3: own3}, panel, ((1, 0), (3, 0)))
    some_columns(where, keep_d, 0, {1: own1, 3: own3}, {1: own1, 3: own3}, panel, ((3, 1),))
    some_columns(where, keep_d, 1, {0: other0}, {1: own1, 3: own3}, panel)


def density_2(where, keep_d, own0, own1, own3, other1, other3, rows, _, __, panel, line):
    other = {1: other1, 3: other3}
    some_rows(where, keep_d, rows, 1, other, line)
    some_columns(where, keep_d, 1, other, {0: own0, 1: own1, 3: own3}, panel)


def density_3(where, keep_d, own0, own1, own2, own3, other0, other1, other3, rows, _, __, panel, line):
    some_rows(where, keep_d, rows, 0, {2: own2}, line)
    own = {0: own0, 1: own1, 2: own2, 3: own3}
    some_columns(where, keep_d, 0, {2: own2}, own, panel, ((0, 2), (1, 2), (3, 2)))
    some_columns(where, keep_d, 1, {0: other0, 1: other1, 3: other3}, {2: own2}, panel)


def first_square(where, keep_d, keep_s, own0, own1, own2, own3, other2, rows, _, __, panel, line, low, square, total):
    x, y, core, z = where[0], where[1], where[2], where[3]
    some_rows(where, keep_d, rows, 1, {2: other2}, line)
    some_columns(where, keep_d, 1, {2: other2}, {0: own0, 1: own1, 2: own2, 3: own3}, panel)

    @pl.loop(0, 2)
    def _(half):
        value = dot(line[...], panel[:, aligned(half, 1024)])
        for t in range(2):
            for u in range(8):
                block = block_at(x, y, core, half * 8 + u)
                keep = keep_s[0, (x * 4 + y) * 2 + t, block].astype(jnp.float32)
                piece = value[t * B:(t + 1) * B, u * B:(u + 1) * B] * keep
                total[t * B:(t + 1) * B, aligned(half * 8 + u, B)] = piece
                low[t * B:(t + 1) * B, aligned(half * 8 + u, B)] = piece.astype(jnp.bfloat16)

    for t in range(4):
        square[:, t * B:(t + 1) * B] = total[:, aligned(column_at(where, t), B)]


def column_at(where, t):
    x, y, core, z = where[0], where[1], where[2], where[3]
    dx, dy = (z - x) & 3, (t - y) & 3
    return jnp.where(core == 0, dy * 4 + dx, dx * 4 + dy)


def early_first_cube(where, low, panel, early, columns):
    for t in range(4):
        at = aligned(column_at(where, t), B)
        columns[:, t * B:(t + 1) * B] = panel[:, at]
    early[...] = dot(low[...], columns[:2048, :])


def first_density(where, keep_d, its, columns, early, square, out):
    x, y, core, z = where[0], where[1], where[2], where[3]
    value = 3.0 * square[...] - 2.0 * (early[...] + dot(its[...], columns[2048:, :]))
    for t in range(2):
        for u in range(4):
            keep = keep_d[1, (x * 4 + y) * 2 + t, z * 8 + u * 2 + core].astype(jnp.float32)
            piece = value[t * B:(t + 1) * B, u * B:(u + 1) * B] * keep
            out[t * B:(t + 1) * B, u * B:(u + 1) * B] = piece.astype(jnp.bfloat16)


def parts_times_panel(parts, z, panel):
    total = None
    for ref, d, kind in parts:
        rows = [panel[aligned(((z + d) & 3) * 8 + t * 2 + kind, B), :] for t in range(4)]
        term = dot(ref[...], jnp.concatenate(rows, axis=0))
        total = term if total is None else total + term
    return total


def early_cube(where, *refs):
    own, other, panel, out = refs[:4], refs[4], refs[5], refs[6]
    core, z = where[2], where[3]
    parts = [(own[d], d, core) for d in range(4)] + [(other, 0, 1 - core)]
    out[...] = parts_times_panel(parts, z, panel)


def chips_times(where, line, chips, panel, sems):
    x, y, core = where[0], where[1], where[2]
    copies, left, right = [], [], []
    for n, (ref, offset, first, second) in enumerate(chips):
        px, py = place(x, y, core, first, second)
        copies.append(pltpu.make_async_copy(
            ref.at[pl.ds(offset, ROWS)], panel.at[aligned(px * 4 + py, ROWS)], sems.at[n]))
        copies[-1].start()
        left.append(line[:, aligned(px * 4 + py, ROWS)])
        right.append(ref[offset:offset + ROWS, :])
    total = None
    for n in range(0, len(chips), 4):
        term = dot(jnp.concatenate(left[n:n + 4], axis=1), jnp.concatenate(right[n:n + 4], axis=0))
        total = term if total is None else total + term
    return total, copies


def early_square(where, *refs):
    own, other, near, far, (early, line, panel), (sems,) = (
        refs[:4], refs[4:8], refs[8], refs[9:13], refs[13:16], refs[16:])
    core, z = where[2], where[3]
    for d in range(4):
        for ref, kind in ((own[d], core), (other[d], 1 - core)):
            for t in range(4):
                line[:, aligned(((z + d) & 3) * 8 + t * 2 + kind, B)] = ref[:, t * B:(t + 1) * B]
    chips = [(near, i * ROWS, i, 0) for i in range(4)] + [(far[i], 0, i, 2) for i in range(4)]
    value, copies = chips_times(where, line, chips, panel, sems)
    early[...] = value
    for copy in copies:
        copy.wait()


def second_square(where, keep_s, one, three, early, line, _, square, low, panel, sems):
    x, y, core, z = where[0], where[1], where[2], where[3]
    chips = [(ref, i * ROWS, i, j) for ref, j in ((one, 1), (three, 3)) for i in range(4)]
    value, copies = chips_times(where, line, chips, panel, sems)
    value = early[...] + value
    for t in range(2):
        for u in range(4):
            keep = keep_s[1, (x * 4 + y) * 2 + t, z * 8 + u * 2 + core].astype(jnp.float32)
            piece = value[t * B:(t + 1) * B, u * B:(u + 1) * B] * keep
            square[t * B:(t + 1) * B, u * B:(u + 1) * B] = piece
            low[t * B:(t + 1) * B, u * B:(u + 1) * B] = piece.astype(jnp.bfloat16)
    for copy in copies:
        copy.wait()


def second_density(leave, where, *refs):
    others, (early, square, panel), (come, out) = refs[:3], refs[3:6], (refs[6:] if not leave else (None,) + refs[6:])
    core, z = where[2], where[3]
    at = aligned(1 - core if leave else core, B)
    total = early[at, :]
    for d in (1, 2, 3):
        rows = [panel[aligned(((z + d) & 3) * 8 + t * 2 + 1 - core, B), :] for t in range(4)]
        total = total + dot(others[d - 1][at, :], jnp.concatenate(rows, axis=0))
    value = 3.0 * square[at, :] - 2.0 * total
    if leave:
        out[...] = value
        return
    first = core == 0
    for t in range(4):
        mine, its = value[:, t * B:(t + 1) * B], come[:, t * B:(t + 1) * B]
        out[:, 2 * t * B:(2 * t + 1) * B] = jnp.where(first, mine, its)
        out[:, (2 * t + 1) * B:(2 * t + 2) * B] = jnp.where(first, its, mine)


SMEM = pl.BlockSpec(memory_space=pltpu.SMEM)
VMEM = pl.BlockSpec(memory_space=pltpu.VMEM)


def call(kernel, n_smem, ins, outs, scratch, flops, moved, aliases={}):
    return pl.pallas_call(
        kernel,
        in_specs=[SMEM] * n_smem + [VMEM] * (len(ins) - n_smem),
        out_specs=[VMEM] * len(outs),
        out_shape=outs,
        scratch_shapes=scratch,
        input_output_aliases=aliases,
        cost_estimate=pl.CostEstimate(flops=flops, bytes_accessed=moved, transcendentals=0),
        compiler_params=pltpu.CompilerParams(vmem_limit_bytes=12 * MIB),
    )(*ins)


def body(coeffs, coef_pattern, keep_density, keep_square):
    r, z = lax.axis_index("row"), lax.axis_index("col")
    x, y, core = r // 8, (r // 2) % 4, r % 2
    where = jnp.stack([x, y, core, z]).astype(jnp.int32)
    low_block = jax.ShapeDtypeStruct((ROWS, COLS), jnp.bfloat16)
    full_block = jax.ShapeDtypeStruct((ROWS, COLS), jnp.float32)
    panel_shape = jax.ShapeDtypeStruct((N, COLS), jnp.bfloat16)
    line_shape = jax.ShapeDtypeStruct((ROWS, N), jnp.bfloat16)
    wide_shape = jax.ShapeDtypeStruct((N, N // 2), jnp.bfloat16)
    block_flops = 2 * ROWS * N * COLS
    pair_flops = 2 * 512 * 512 * K

    kept = jnp.concatenate(gather(coeffs, from_z), axis=1)
    pattern = lax.dynamic_slice(coef_pattern, (r, 0), (1, 8)).reshape(4, 2)
    pattern = jnp.concatenate([pattern, pattern], axis=0)
    pattern = lax.dynamic_slice(pattern, (z, 0), (4, 2)).reshape(1, 8)
    kept = kept * jnp.repeat(pattern, B, 1).astype(jnp.bfloat16)
    near = jnp.concatenate(gather(kept, from_first), axis=0)
    own1, own3, other0 = from_second(near, 1), from_second(near, 3), other_core(near)
    rows_shape = jax.ShapeDtypeStruct((ROWS, K), jnp.bfloat16)
    out_shapes = [wide_shape, line_shape]
    panel, line, rows = call(
        density_0, 2, [where, keep_density, near, other0], out_shapes + [rows_shape], [], pair_flops // 8, MIB)
    panel, line, own0, own1, own3 = lax.optimization_barrier((panel, line, near, own1, own3))
    own2 = from_second(own0, 2)
    other1, other3 = other_core(own1), other_core(own3)
    panel, line = call(
        density_1, 2, [where, keep_density, own0, own1, own3, other0, rows, panel, line],
        out_shapes, [], 11 * pair_flops, 8 * MIB, {7: 0, 8: 1})
    panel, line = call(
        density_2, 2, [where, keep_density, own0, own1, own3, other1, other3, rows, panel, line],
        out_shapes, [], 7 * pair_flops, 8 * MIB, {8: 0, 9: 1})
    panel, line, own2 = lax.optimization_barrier((panel, line, own2))
    other2 = other_core(own2)
    panel, line = call(
        density_3, 2, [where, keep_density, own0, own1, own2, own3, other0, other1, other3, rows, panel, line],
        out_shapes, [], 10 * pair_flops, 8 * MIB, {10: 0, 11: 1})
    panel, line, low, square = call(
        first_square, 3,
        [where, keep_density, keep_square, own0, own1, own2, own3, other2, rows, panel, line],
        out_shapes + [jax.ShapeDtypeStruct((ROWS, N // 2), jnp.bfloat16), full_block],
        [pltpu.VMEM((ROWS, N // 2), jnp.float32)],
        4 * pair_flops + 4 * block_flops, 20 * MIB, {9: 0, 10: 1})

    its = other_core(low)
    early, columns = call(
        early_first_cube, 1, [where, low, panel], [full_block, panel_shape], [], block_flops // 2, 12 * MIB)
    (current,) = call(
        first_density, 2, [where, keep_density, its, columns, early, square], [low_block], [],
        block_flops // 2, 4 * MIB)

    own0, one, three, two, far = lax.optimization_barrier((
        current, from_first(current, 1), from_first(current, 3), from_first(current, 2), from_second(current, 2)))
    near = jnp.concatenate([own0, one, two, three], axis=0)
    one, three = from_second(near, 1), from_second(near, 3)
    far, own1, own2, own3 = lax.optimization_barrier((far, *gather(current, from_z)[1:]))
    far = gather(far, from_first)
    own = [own0, own1, own2, own3]
    other = [other_core(part) for part in own]
    early, line, panel = call(
        early_square, 1, [where, *own, *other, near, *far], [full_block, line_shape, panel_shape],
        [pltpu.SemaphoreType.DMA((8,))], block_flops // 2, 10 * MIB)
    square, low, panel = call(
        second_square, 2, [where, keep_square, one, three, early, line, panel],
        [full_block, low_block, panel_shape],
        [pltpu.SemaphoreType.DMA((8,))], block_flops // 2, 8 * MIB, {6: 2})

    own = gather(low, from_z)
    other = [other_core(part) for part in own]
    (early,) = call(
        early_cube, 1, [where, *own, other[0], panel], [full_block], [], block_flops * 5 // 8, 4 * MIB)
    last = [*other[1:], early, square, panel]
    (leave,) = call(
        functools.partial(second_density, True), 1, [where, *last],
        [jax.ShapeDtypeStruct((B, COLS), jnp.float32)], [], block_flops * 3 // 16, 3 * MIB)
    (out,) = call(
        functools.partial(second_density, False), 1, [where, *last, other_core(leave)],
        [jax.ShapeDtypeStruct((B, 2 * COLS), jnp.float32)], [], block_flops * 3 // 16, 3 * MIB)
    return out


def solution(mesh):
    placed = (P("row", "col"), P(), P(), P())
    return jax.shard_map(
        body, mesh=mesh, in_specs=placed, out_specs=P("row", "col"), check_vma=False
    )
```

```python
import functools

import jax
import jax.numpy as jnp
from jax import lax
from jax.experimental import pallas as pl
from jax.experimental.pallas import tpu as pltpu
from jax.sharding import PartitionSpec as P

B = 128
N = 4096
K = 1024
ROWS = 256
COLS = 512
AXES = ("row", "col")
MIB = 1024 * 1024


def device(x, y, core, z):
    return (((x % 4) * 4 + y % 4) * 2 + core) * 4 + z % 4


def pairs(target):
    return [
        (device(x, y, core, z), device(*target(x, y, core, z)))
        for x in range(4) for y in range(4) for core in range(2) for z in range(4)
    ]


def other_core(a):
    return lax.ppermute(a, AXES, pairs(lambda x, y, core, z: (x, y, 1 - core, z)))


def from_z(a, d):
    return lax.ppermute(a, AXES, pairs(lambda x, y, core, z: (x, y, core, z - d)))


def from_first(a, d):
    return lax.ppermute(a, AXES, pairs(
        lambda x, y, core, z: (x - d, y, core, z) if core == 0 else (x, y - d, core, z)))


def from_second(a, d):
    return lax.ppermute(a, AXES, pairs(
        lambda x, y, core, z: (x, y - d, core, z) if core == 0 else (x - d, y, core, z)))


def gather(a, fetch):
    one, three, two = fetch(a, 1), fetch(a, 3), fetch(a, 2)
    return [a, one, two, three]


def place(x, y, kind, first, second):
    px = jnp.where(kind == 0, x + first, x + second) & 3
    py = jnp.where(kind == 0, y + second, y + first) & 3
    return px, py


def dot_t(a, b):
    return lax.dot_general(a, b, (((1,), (1,)), ((), ())), preferred_element_type=jnp.float32)


def dot(a, b):
    return jnp.dot(a, b, preferred_element_type=jnp.float32)


def aligned(block, size):
    return pl.ds(pl.multiple_of(block * size, size), size)


def block_at(x, y, kind, place_in_order):
    px, py = place(x, y, kind, place_in_order % 4, place_in_order // 4)
    return px * 8 + py * 2 + kind


def some_rows(where, keep_d, rows, half, parts, line):
    x, y, core = where[0], where[1], where[2]
    kind = core if half == 0 else 1 - core
    for n, part in parts.items():
        value = dot_t(rows[...], part[...])
        for u in range(4):
            block = block_at(x, y, kind, n * 4 + u)
            at = (half * 16 + n * 4 + u) * B
            for t in range(2):
                keep = keep_d[0, (x * 4 + y) * 2 + t, block].astype(jnp.float32)
                piece = value[t * B:(t + 1) * B, u * B:(u + 1) * B] * keep
                line[t * B:(t + 1) * B, at:at + B] = piece.astype(jnp.bfloat16)


def some_columns(where, keep_d, half, parts, columns, panel, mirrored=()):
    x, y, core = where[0], where[1], where[2]
    kind = core if half == 0 else 1 - core

    def put(value, kind, n, i, m, u, turn):
        keep = keep_d[0, block_at(x, y, kind, n * 4 + i), block_at(x, y, core, m * 4 + u)]
        piece = (value * keep.astype(jnp.float32)).astype(jnp.bfloat16)
        at, to = (half * 16 + n * 4 + i) * B, (m * 4 + u) * B
        panel[at:at + B, to:to + B] = piece.T if turn else piece

    for n, part in parts.items():
        for m, column in columns.items():
            if (n, m) in mirrored:
                continue
            value = dot_t(part[...], column[...])
            for i in range(4):
                for u in range(4):
                    piece = value[i * B:(i + 1) * B, u * B:(u + 1) * B]
                    put(piece, kind, n, i, m, u, False)
                    if (m, n) in mirrored:
                        put(piece, core, m, u, n, i, True)


EARLY = (0, 1, 3)


def density_0(where, keep_d, own0, other0, panel, line, rows):
    first = where[2] == 0
    mine, its = own0[:B, :], other0[:B, :]
    rows[:B, :] = jnp.where(first, mine, its)
    rows[B:, :] = jnp.where(first, its, mine)
    for half, part in enumerate((own0, other0)):
        some_rows(where, keep_d, rows, half, {0: part}, line)
        some_columns(where, keep_d, half, {0: part}, {0: own0}, panel)


def density_1(where, keep_d, own0, own1, own3, other0, rows, _, __, panel, line):
    own = {0: own0, 1: own1, 3: own3}
    some_rows(where, keep_d, rows, 0, {1: own1, 3: own3}, line)
    some_columns(where, keep_d, 0, {0: own0}, {1: own1, 3: own3}, panel, ((1, 0), (3, 0)))
    some_columns(where, keep_d, 0, {1: own1, 3: own3}, {1: own1, 3: own3}, panel, ((3, 1),))
    some_columns(where, keep_d, 1, {0: other0}, {1: own1, 3: own3}, panel)


def density_2(where, keep_d, own0, own1, own3, other1, other3, rows, _, __, panel, line, some):
    other = {1: other1, 3: other3}
    some_rows(where, keep_d, rows, 1, other, line)
    some_columns(where, keep_d, 1, other, {0: own0, 1: own1, 3: own3}, panel)

    @pl.loop(0, 3)
    def _(part):
        at = aligned(part + part // 2, 512)
        some[:, at] = (
            dot(line[:, :1024], panel[:1024, at])
            + dot(line[:, 1536:3072], panel[1536:3072, at])
            + dot(line[:, 3584:], panel[3584:, at]))


def density_3(where, keep_d, own0, own1, own2, own3, other0, other1, other3, rows, _, __, panel, line):
    some_rows(where, keep_d, rows, 0, {2: own2}, line)
    own = {0: own0, 1: own1, 2: own2, 3: own3}
    some_columns(where, keep_d, 0, {2: own2}, own, panel, ((0, 2), (1, 2), (3, 2)))
    some_columns(where, keep_d, 1, {0: other0, 1: other1, 3: other3}, {2: own2}, panel)


def first_square(where, keep_d, keep_s, own0, own1, own2, own3, other2, rows, some, _, __, panel, line, low, square, total):
    x, y, core, z = where[0], where[1], where[2], where[3]
    some_rows(where, keep_d, rows, 1, {2: other2}, line)
    some_columns(where, keep_d, 1, {2: other2}, {0: own0, 1: own1, 2: own2, 3: own3}, panel)

    def put(value, part):
        for t in range(2):
            for u in range(4):
                block = block_at(x, y, core, part * 4 + u)
                keep = keep_s[0, (x * 4 + y) * 2 + t, block].astype(jnp.float32)
                piece = value[t * B:(t + 1) * B, u * B:(u + 1) * B] * keep
                total[t * B:(t + 1) * B, aligned(part * 4 + u, B)] = piece
                low[t * B:(t + 1) * B, aligned(part * 4 + u, B)] = piece.astype(jnp.bfloat16)

    @pl.loop(0, 3)
    def _(n):
        part = n + n // 2
        at = aligned(part, 512)
        put(some[:, at] + dot(line[:, 1024:1536], panel[1024:1536, at])
            + dot(line[:, 3072:3584], panel[3072:3584, at]), part)

    put(dot(line[...], panel[:, 1024:1536]), 2)
    for t in range(4):
        square[:, t * B:(t + 1) * B] = total[:, aligned(column_at(where, t), B)]


def column_at(where, t):
    x, y, core, z = where[0], where[1], where[2], where[3]
    dx, dy = (z - x) & 3, (t - y) & 3
    return jnp.where(core == 0, dy * 4 + dx, dx * 4 + dy)


def early_first_cube(where, low, panel, early, columns):
    for t in range(4):
        at = aligned(column_at(where, t), B)
        columns[:, t * B:(t + 1) * B] = panel[:, at]
    early[...] = dot(low[...], columns[:2048, :])


def first_density(where, keep_d, its, columns, early, square, out):
    x, y, core, z = where[0], where[1], where[2], where[3]
    value = 3.0 * square[...] - 2.0 * (early[...] + dot(its[...], columns[2048:, :]))
    for t in range(2):
        for u in range(4):
            keep = keep_d[1, (x * 4 + y) * 2 + t, z * 8 + u * 2 + core].astype(jnp.float32)
            piece = value[t * B:(t + 1) * B, u * B:(u + 1) * B] * keep
            out[t * B:(t + 1) * B, u * B:(u + 1) * B] = piece.astype(jnp.bfloat16)


def parts_times_panel(parts, z, panel):
    total = None
    for ref, d, kind in parts:
        rows = [panel[aligned(((z + d) & 3) * 8 + t * 2 + kind, B), :] for t in range(4)]
        term = dot(ref[...], jnp.concatenate(rows, axis=0))
        total = term if total is None else total + term
    return total


def early_cube(where, *refs):
    own, other, panel, out = refs[:4], refs[4], refs[5], refs[6]
    core, z = where[2], where[3]
    parts = [(own[d], d, core) for d in range(4)] + [(other, 0, 1 - core)]
    out[...] = parts_times_panel(parts, z, panel)


def chips_times(where, line, chips, panel, sems):
    x, y, core = where[0], where[1], where[2]
    copies, left, right = [], [], []
    for n, (ref, offset, first, second) in enumerate(chips):
        px, py = place(x, y, core, first, second)
        copies.append(pltpu.make_async_copy(
            ref.at[pl.ds(offset, ROWS)], panel.at[aligned(px * 4 + py, ROWS)], sems.at[n]))
        copies[-1].start()
        left.append(line[:, aligned(px * 4 + py, ROWS)])
        right.append(ref[offset:offset + ROWS, :])
    total = None
    for n in range(0, len(chips), 4):
        term = dot(jnp.concatenate(left[n:n + 4], axis=1), jnp.concatenate(right[n:n + 4], axis=0))
        total = term if total is None else total + term
    return total, copies


def second_square_0(where, *refs):
    own, other, near, (early, line, panel), (sems,) = refs[:4], refs[4:8], refs[8], refs[9:12], refs[12:]
    core, z = where[2], where[3]
    for d in range(4):
        for ref, kind in ((own[d], core), (other[d], 1 - core)):
            for t in range(4):
                line[:, aligned(((z + d) & 3) * 8 + t * 2 + kind, B)] = ref[:, t * B:(t + 1) * B]
    value, copies = chips_times(where, line, [(near, i * ROWS, i, 0) for i in range(4)], panel, sems)
    early[...] = value
    for copy in copies:
        copy.wait()


def second_square_1(where, one, three, early, line, _, out, panel, sems):
    chips = [(ref, i * ROWS, i, j) for ref, j in ((one, 1), (three, 3)) for i in range(4)]
    value, copies = chips_times(where, line, chips, panel, sems)
    out[...] = early[...] + value
    for copy in copies:
        copy.wait()


def second_square_2(where, keep_s, far0, far1, far2, far3, early, line, _, square, low, panel, sems):
    x, y, core, z = where[0], where[1], where[2], where[3]
    chips = [(ref, 0, i, 2) for i, ref in enumerate((far0, far1, far2, far3))]
    value, copies = chips_times(where, line, chips, panel, sems)
    value = early[...] + value
    for t in range(2):
        for u in range(4):
            keep = keep_s[1, (x * 4 + y) * 2 + t, z * 8 + u * 2 + core].astype(jnp.float32)
            piece = value[t * B:(t + 1) * B, u * B:(u + 1) * B] * keep
            square[t * B:(t + 1) * B, u * B:(u + 1) * B] = piece
            low[t * B:(t + 1) * B, u * B:(u + 1) * B] = piece.astype(jnp.bfloat16)
    for copy in copies:
        copy.wait()


def second_density(leave, where, *refs):
    others, (early, square, panel), (come, out) = refs[:3], refs[3:6], (refs[6:] if not leave else (None,) + refs[6:])
    core, z = where[2], where[3]
    at = aligned(1 - core if leave else core, B)
    total = early[at, :]
    for d in (1, 2, 3):
        rows = [panel[aligned(((z + d) & 3) * 8 + t * 2 + 1 - core, B), :] for t in range(4)]
        total = total + dot(others[d - 1][at, :], jnp.concatenate(rows, axis=0))
    value = 3.0 * square[at, :] - 2.0 * total
    if leave:
        out[...] = value
        return
    first = core == 0
    for t in range(4):
        mine, its = value[:, t * B:(t + 1) * B], come[:, t * B:(t + 1) * B]
        out[:, 2 * t * B:(2 * t + 1) * B] = jnp.where(first, mine, its)
        out[:, (2 * t + 1) * B:(2 * t + 2) * B] = jnp.where(first, its, mine)


SMEM = pl.BlockSpec(memory_space=pltpu.SMEM)
VMEM = pl.BlockSpec(memory_space=pltpu.VMEM)


def call(kernel, n_smem, ins, outs, scratch, flops, moved, aliases={}):
    return pl.pallas_call(
        kernel,
        in_specs=[SMEM] * n_smem + [VMEM] * (len(ins) - n_smem),
        out_specs=[VMEM] * len(outs),
        out_shape=outs,
        scratch_shapes=scratch,
        input_output_aliases=aliases,
        cost_estimate=pl.CostEstimate(flops=flops, bytes_accessed=moved, transcendentals=0),
        compiler_params=pltpu.CompilerParams(vmem_limit_bytes=12 * MIB),
    )(*ins)


def body(coeffs, coef_pattern, keep_density, keep_square):
    r, z = lax.axis_index("row"), lax.axis_index("col")
    x, y, core = r // 8, (r // 2) % 4, r % 2
    where = jnp.stack([x, y, core, z]).astype(jnp.int32)
    low_block = jax.ShapeDtypeStruct((ROWS, COLS), jnp.bfloat16)
    full_block = jax.ShapeDtypeStruct((ROWS, COLS), jnp.float32)
    panel_shape = jax.ShapeDtypeStruct((N, COLS), jnp.bfloat16)
    line_shape = jax.ShapeDtypeStruct((ROWS, N), jnp.bfloat16)
    wide_shape = jax.ShapeDtypeStruct((N, N // 2), jnp.bfloat16)
    block_flops = 2 * ROWS * N * COLS
    pair_flops = 2 * 512 * 512 * K

    kept = jnp.concatenate(gather(coeffs, from_z), axis=1)
    pattern = lax.dynamic_slice(coef_pattern, (r, 0), (1, 8)).reshape(4, 2)
    pattern = jnp.concatenate([pattern, pattern], axis=0)
    pattern = lax.dynamic_slice(pattern, (z, 0), (4, 2)).reshape(1, 8)
    kept = kept * jnp.repeat(pattern, B, 1).astype(jnp.bfloat16)
    near = jnp.concatenate(gather(kept, from_first), axis=0)
    own1, own3, other0 = from_second(near, 1), from_second(near, 3), other_core(near)
    rows_shape = jax.ShapeDtypeStruct((ROWS, K), jnp.bfloat16)
    out_shapes = [wide_shape, line_shape]
    panel, line, rows = call(
        density_0, 2, [where, keep_density, near, other0], out_shapes + [rows_shape], [], pair_flops // 8, MIB)
    panel, line, own0, own1, own3 = lax.optimization_barrier((panel, line, near, own1, own3))
    own2 = from_second(own0, 2)
    other1, other3 = other_core(own1), other_core(own3)
    panel, line = call(
        density_1, 2, [where, keep_density, own0, own1, own3, other0, rows, panel, line],
        out_shapes, [], 11 * pair_flops, 8 * MIB, {7: 0, 8: 1})
    panel, line, some = call(
        density_2, 2, [where, keep_density, own0, own1, own3, other1, other3, rows, panel, line],
        out_shapes + [jax.ShapeDtypeStruct((ROWS, N // 2), jnp.float32)], [], 11 * pair_flops, 8 * MIB, {8: 0, 9: 1})
    panel, line, own2 = lax.optimization_barrier((panel, line, own2))
    other2 = other_core(own2)
    panel, line = call(
        density_3, 2, [where, keep_density, own0, own1, own2, own3, other0, other1, other3, rows, panel, line],
        out_shapes, [], 10 * pair_flops, 8 * MIB, {10: 0, 11: 1})
    panel, line, low, square = call(
        first_square, 3,
        [where, keep_density, keep_square, own0, own1, own2, own3, other2, rows, some, panel, line],
        out_shapes + [jax.ShapeDtypeStruct((ROWS, N // 2), jnp.bfloat16), full_block],
        [pltpu.VMEM((ROWS, N // 2), jnp.float32)],
        4 * pair_flops + 2 * block_flops, 20 * MIB, {10: 0, 11: 1})

    its = other_core(low)
    early, columns = call(
        early_first_cube, 1, [where, low, panel], [full_block, panel_shape], [], block_flops // 2, 12 * MIB)
    (current,) = call(
        first_density, 2, [where, keep_density, its, columns, early, square], [low_block], [],
        block_flops // 2, 4 * MIB)

    own0, one, three, two, far = lax.optimization_barrier((
        current, from_first(current, 1), from_first(current, 3), from_first(current, 2), from_second(current, 2)))
    near = jnp.concatenate([own0, one, two, three], axis=0)
    one, three = from_second(near, 1), from_second(near, 3)
    far, own1, own2, own3 = lax.optimization_barrier((far, *gather(current, from_z)[1:]))
    far = gather(far, from_first)
    own = [own0, own1, own2, own3]
    other = [other_core(part) for part in own]
    early, line, panel = call(
        second_square_0, 1, [where, *own, *other, near], [full_block, line_shape, panel_shape],
        [pltpu.SemaphoreType.DMA((4,))], block_flops // 4, 8 * MIB)
    early, panel = call(
        second_square_1, 1, [where, one, three, early, line, panel], [full_block, panel_shape],
        [pltpu.SemaphoreType.DMA((8,))], block_flops // 2, 8 * MIB, {5: 1})
    square, low, panel = call(
        second_square_2, 2, [where, keep_square, *far, early, line, panel],
        [full_block, low_block, panel_shape],
        [pltpu.SemaphoreType.DMA((4,))], block_flops // 4, 6 * MIB, {8: 2})

    own = gather(low, from_z)
    other = [other_core(part) for part in own]
    (early,) = call(
        early_cube, 1, [where, *own, other[0], panel], [full_block], [], block_flops * 5 // 8, 4 * MIB)
    last = [*other[1:], early, square, panel]
    (leave,) = call(
        functools.partial(second_density, True), 1, [where, *last],
        [jax.ShapeDtypeStruct((B, COLS), jnp.float32)], [], block_flops * 3 // 16, 3 * MIB)
    (out,) = call(
        functools.partial(second_density, False), 1, [where, *last, other_core(leave)],
        [jax.ShapeDtypeStruct((B, 2 * COLS), jnp.float32)], [], block_flops * 3 // 16, 3 * MIB)
    return out


def solution(mesh):
    placed = (P("row", "col"), P(), P(), P())
    return jax.shard_map(
        body, mesh=mesh, in_specs=placed, out_specs=P("row", "col"), check_vma=False
    )
```

```python
import jax
import jax.numpy as jnp
from jax import lax
from jax.experimental import pallas as pl
from jax.experimental.pallas import tpu as pltpu
from jax.sharding import PartitionSpec as P

B = 128
N = 4096
K = 1024
ROWS = 256
COLS = 512
AXES = ("row", "col")
MIB = 1024 * 1024


def device(x, y, core, z):
    return (((x % 4) * 4 + y % 4) * 2 + core) * 4 + z % 4


def pairs(target):
    return [
        (device(x, y, core, z), device(*target(x, y, core, z)))
        for x in range(4) for y in range(4) for core in range(2) for z in range(4)
    ]


def other_core(a):
    return lax.ppermute(a, AXES, pairs(lambda x, y, core, z: (x, y, 1 - core, z)))


def from_z(a, d):
    return lax.ppermute(a, AXES, pairs(lambda x, y, core, z: (x, y, core, z - d)))


def from_first(a, d):
    return lax.ppermute(a, AXES, pairs(
        lambda x, y, core, z: (x - d, y, core, z) if core == 0 else (x, y - d, core, z)))


def from_second(a, d):
    return lax.ppermute(a, AXES, pairs(
        lambda x, y, core, z: (x, y - d, core, z) if core == 0 else (x - d, y, core, z)))


def gather(a, fetch):
    one, three, two = fetch(a, 1), fetch(a, 3), fetch(a, 2)
    return [a, one, two, three]


def place(x, y, kind, first, second):
    px = jnp.where(kind == 0, x + first, x + second) & 3
    py = jnp.where(kind == 0, y + second, y + first) & 3
    return px, py


def dot_t(a, b):
    return lax.dot_general(a, b, (((1,), (1,)), ((), ())), preferred_element_type=jnp.float32)


def dot(a, b):
    return jnp.dot(a, b, preferred_element_type=jnp.float32)


def aligned(block, size):
    return pl.ds(pl.multiple_of(block * size, size), size)


def block_at(x, y, kind, place_in_order):
    px, py = place(x, y, kind, place_in_order % 4, place_in_order // 4)
    return px * 8 + py * 2 + kind


def some_rows(where, keep_d, rows, half, parts, line):
    x, y, core = where[0], where[1], where[2]
    kind = core if half == 0 else 1 - core
    for n, part in parts.items():
        value = dot_t(rows[...], part[...])
        for u in range(4):
            block = block_at(x, y, kind, n * 4 + u)
            at = (half * 16 + n * 4 + u) * B
            for t in range(2):
                keep = keep_d[0, (x * 4 + y) * 2 + t, block].astype(jnp.float32)
                piece = value[t * B:(t + 1) * B, u * B:(u + 1) * B] * keep
                line[t * B:(t + 1) * B, at:at + B] = piece.astype(jnp.bfloat16)


def some_columns(where, keep_d, half, parts, columns, panel, mirrored=()):
    x, y, core = where[0], where[1], where[2]
    kind = core if half == 0 else 1 - core

    def put(value, kind, n, i, m, u, turn):
        keep = keep_d[0, block_at(x, y, kind, n * 4 + i), block_at(x, y, core, m * 4 + u)]
        piece = (value * keep.astype(jnp.float32)).astype(jnp.bfloat16)
        at, to = (half * 16 + n * 4 + i) * B, (m * 4 + u) * B
        panel[at:at + B, to:to + B] = piece.T if turn else piece

    for n, part in parts.items():
        for m, column in columns.items():
            if (n, m) in mirrored:
                continue
            value = dot_t(part[...], column[...])
            for i in range(4):
                for u in range(4):
                    piece = value[i * B:(i + 1) * B, u * B:(u + 1) * B]
                    put(piece, kind, n, i, m, u, False)
                    if (m, n) in mirrored:
                        put(piece, core, m, u, n, i, True)


EARLY = (0, 1, 3)


def density_0(where, keep_d, own0, other0, panel, line, rows):
    first = where[2] == 0
    mine, its = own0[:B, :], other0[:B, :]
    rows[:B, :] = jnp.where(first, mine, its)
    rows[B:, :] = jnp.where(first, its, mine)
    for half, part in enumerate((own0, other0)):
        some_rows(where, keep_d, rows, half, {0: part}, line)
        some_columns(where, keep_d, half, {0: part}, {0: own0}, panel)


def density_1(where, keep_d, own0, own1, own3, other0, rows, _, __, panel, line):
    own = {0: own0, 1: own1, 3: own3}
    some_rows(where, keep_d, rows, 0, {1: own1, 3: own3}, line)
    some_columns(where, keep_d, 0, {0: own0}, {1: own1, 3: own3}, panel, ((1, 0), (3, 0)))
    some_columns(where, keep_d, 0, {1: own1, 3: own3}, {1: own1, 3: own3}, panel, ((3, 1),))
    some_columns(where, keep_d, 1, {0: other0}, {1: own1, 3: own3}, panel)


def density_2(where, keep_d, own0, own1, own3, other1, other3, rows, _, __, panel, line, some):
    other = {1: other1, 3: other3}
    some_rows(where, keep_d, rows, 1, other, line)
    some_columns(where, keep_d, 1, other, {0: own0, 1: own1, 3: own3}, panel)

    @pl.loop(0, 3)
    def _(part):
        at = aligned(part + part // 2, 512)
        some[:, at] = (
            dot(line[:, :1024], panel[:1024, at])
            + dot(line[:, 1536:3072], panel[1536:3072, at])
            + dot(line[:, 3584:], panel[3584:, at]))


def density_3(where, keep_d, own0, own1, own2, own3, other0, other1, other3, rows, _, __, panel, line):
    some_rows(where, keep_d, rows, 0, {2: own2}, line)
    own = {0: own0, 1: own1, 2: own2, 3: own3}
    some_columns(where, keep_d, 0, {2: own2}, own, panel, ((0, 2), (1, 2), (3, 2)))
    some_columns(where, keep_d, 1, {0: other0, 1: other1, 3: other3}, {2: own2}, panel)


def first_square(where, keep_d, keep_s, own0, own1, own2, own3, other2, rows, some, _, __, panel, line, low, square, total):
    x, y, core, z = where[0], where[1], where[2], where[3]
    some_rows(where, keep_d, rows, 1, {2: other2}, line)
    some_columns(where, keep_d, 1, {2: other2}, {0: own0, 1: own1, 2: own2, 3: own3}, panel)

    def put(value, part):
        for t in range(2):
            for u in range(4):
                block = block_at(x, y, core, part * 4 + u)
                keep = keep_s[0, (x * 4 + y) * 2 + t, block].astype(jnp.float32)
                piece = value[t * B:(t + 1) * B, u * B:(u + 1) * B] * keep
                total[t * B:(t + 1) * B, aligned(part * 4 + u, B)] = piece
                low[t * B:(t + 1) * B, aligned(part * 4 + u, B)] = piece.astype(jnp.bfloat16)

    @pl.loop(0, 3)
    def _(n):
        part = n + n // 2
        at = aligned(part, 512)
        put(some[:, at] + dot(line[:, 1024:1536], panel[1024:1536, at])
            + dot(line[:, 3072:3584], panel[3072:3584, at]), part)

    put(dot(line[...], panel[:, 1024:1536]), 2)
    for t in range(4):
        square[:, t * B:(t + 1) * B] = total[:, aligned(column_at(where, t), B)]


def column_at(where, t):
    x, y, core, z = where[0], where[1], where[2], where[3]
    dx, dy = (z - x) & 3, (t - y) & 3
    return jnp.where(core == 0, dy * 4 + dx, dx * 4 + dy)


def early_first_cube(where, low, panel, early, columns):
    for t in range(4):
        at = aligned(column_at(where, t), B)
        columns[:, t * B:(t + 1) * B] = panel[:, at]
    early[...] = dot(low[...], columns[:2048, :])


def first_density(where, keep_d, its, columns, early, square, out):
    x, y, core, z = where[0], where[1], where[2], where[3]
    value = 3.0 * square[...] - 2.0 * (early[...] + dot(its[...], columns[2048:, :]))
    for t in range(2):
        for u in range(4):
            keep = keep_d[1, (x * 4 + y) * 2 + t, z * 8 + u * 2 + core].astype(jnp.float32)
            piece = value[t * B:(t + 1) * B, u * B:(u + 1) * B] * keep
            out[t * B:(t + 1) * B, u * B:(u + 1) * B] = piece.astype(jnp.bfloat16)


def chips_times(where, line, chips, mine, its, sems):
    x, y, core = where[0], where[1], where[2]
    copies, left, right = [], [], []
    for n, (ref, offset, first, second) in enumerate(chips):
        px, py = place(x, y, core, first, second)
        chip = px * 4 + py
        for m, (panel, kind) in enumerate(((mine, core), (its, 1 - core))):
            copies.append(pltpu.make_async_copy(
                ref.at[pl.ds(pl.multiple_of(offset + kind * B, B), B)], panel.at[aligned(chip, B)], sems.at[n, m]))
            copies[-1].start()
        left.append(line[:, aligned(chip, ROWS)])
        right.append(ref[offset:offset + ROWS, :])
    total = None
    for n in range(0, len(chips), 4):
        term = dot(jnp.concatenate(left[n:n + 4], axis=1), jnp.concatenate(right[n:n + 4], axis=0))
        total = term if total is None else total + term
    return total, copies


def early_square(where, *refs):
    own, other, near, far, (early, line, mine, its), (sems,) = (
        refs[:4], refs[4:8], refs[8], refs[9:13], refs[13:17], refs[17:])
    core, z = where[2], where[3]
    for d in range(4):
        for ref, kind in ((own[d], core), (other[d], 1 - core)):
            for t in range(4):
                line[:, aligned(((z + d) & 3) * 8 + t * 2 + kind, B)] = ref[:, t * B:(t + 1) * B]
    chips = [(near, i * ROWS, i, 0) for i in range(4)] + [(far[i], 0, i, 2) for i in range(4)]
    value, copies = chips_times(where, line, chips, mine, its, sems)
    early[...] = value
    for copy in copies:
        copy.wait()


def second_square(where, keep_s, one, three, early, line, _, __, square, low, mine, its, sems):
    x, y, core, z = where[0], where[1], where[2], where[3]
    chips = [(ref, i * ROWS, i, j) for ref, j in ((one, 1), (three, 3)) for i in range(4)]
    value, copies = chips_times(where, line, chips, mine, its, sems)
    value = early[...] + value
    for t in range(2):
        for u in range(4):
            keep = keep_s[1, (x * 4 + y) * 2 + t, z * 8 + u * 2 + core].astype(jnp.float32)
            piece = value[t * B:(t + 1) * B, u * B:(u + 1) * B] * keep
            square[t * B:(t + 1) * B, u * B:(u + 1) * B] = piece
            low[t * B:(t + 1) * B, u * B:(u + 1) * B] = piece.astype(jnp.bfloat16)
    for copy in copies:
        copy.wait()


def parts_times_panel(parts, z, mine, come):
    total = [None, None]
    for value, d in parts:
        for n, panel in enumerate((mine, come)):
            term = dot(value, panel[aligned((z + d) & 3, 512), :])
            total[n] = term if total[n] is None else total[n] + term
    return total


def early_cube(where, own0, own1, own3, mine, come, out):
    parts = [(own0[...], 0), (own1[...], 1), (own3[...], 3)]
    out[:, :COLS], out[:, COLS:] = parts_times_panel(parts, where[3], mine, come)


def density_share(where, at, own2, early, square, mine, come):
    first, second = parts_times_panel([(own2[at, :], 2)], where[3], mine, come)
    return 3.0 * square[at, :] - 2.0 * (early[at, :COLS] + first), -2.0 * (early[at, COLS:] + second)


def leaving_density(where, own2, early, square, mine, come, out):
    at = aligned(1 - where[2], B)
    out[:, :COLS], out[:, COLS:] = density_share(where, at, own2, early, square, mine, come)


def second_density(where, own2, early, square, mine, come, share, out):
    own, other = density_share(where, aligned(where[2], B), own2, early, square, mine, come)
    own, other = own + share[:, COLS:], other + share[:, :COLS]
    first = where[2] == 0
    for t in range(4):
        one, two = own[:, t * B:(t + 1) * B], other[:, t * B:(t + 1) * B]
        out[:, 2 * t * B:(2 * t + 1) * B] = jnp.where(first, one, two)
        out[:, (2 * t + 1) * B:(2 * t + 2) * B] = jnp.where(first, two, one)


SMEM = pl.BlockSpec(memory_space=pltpu.SMEM)
VMEM = pl.BlockSpec(memory_space=pltpu.VMEM)


def call(kernel, n_smem, ins, outs, scratch, flops, moved, aliases={}):
    return pl.pallas_call(
        kernel,
        in_specs=[SMEM] * n_smem + [VMEM] * (len(ins) - n_smem),
        out_specs=[VMEM] * len(outs),
        out_shape=outs,
        scratch_shapes=scratch,
        input_output_aliases=aliases,
        cost_estimate=pl.CostEstimate(flops=flops, bytes_accessed=moved, transcendentals=0),
        compiler_params=pltpu.CompilerParams(vmem_limit_bytes=12 * MIB),
    )(*ins)


def body(coeffs, coef_pattern, keep_density, keep_square):
    r, z = lax.axis_index("row"), lax.axis_index("col")
    x, y, core = r // 8, (r // 2) % 4, r % 2
    where = jnp.stack([x, y, core, z]).astype(jnp.int32)
    low_block = jax.ShapeDtypeStruct((ROWS, COLS), jnp.bfloat16)
    full_block = jax.ShapeDtypeStruct((ROWS, COLS), jnp.float32)
    panel_shape = jax.ShapeDtypeStruct((N, COLS), jnp.bfloat16)
    line_shape = jax.ShapeDtypeStruct((ROWS, N), jnp.bfloat16)
    wide_shape = jax.ShapeDtypeStruct((N, N // 2), jnp.bfloat16)
    block_flops = 2 * ROWS * N * COLS
    pair_flops = 2 * 512 * 512 * K

    kept = jnp.concatenate(gather(coeffs, from_z), axis=1)
    pattern = lax.dynamic_slice(coef_pattern, (r, 0), (1, 8)).reshape(4, 2)
    pattern = jnp.concatenate([pattern, pattern], axis=0)
    pattern = lax.dynamic_slice(pattern, (z, 0), (4, 2)).reshape(1, 8)
    kept = kept * jnp.repeat(pattern, B, 1).astype(jnp.bfloat16)
    near = jnp.concatenate(gather(kept, from_first), axis=0)
    own1, own3, other0 = from_second(near, 1), from_second(near, 3), other_core(near)
    rows_shape = jax.ShapeDtypeStruct((ROWS, K), jnp.bfloat16)
    out_shapes = [wide_shape, line_shape]
    panel, line, rows = call(
        density_0, 2, [where, keep_density, near, other0], out_shapes + [rows_shape], [], pair_flops // 8, MIB)
    panel, line, own0, own1, own3 = lax.optimization_barrier((panel, line, near, own1, own3))
    own2 = from_second(own0, 2)
    other1, other3 = other_core(own1), other_core(own3)
    panel, line = call(
        density_1, 2, [where, keep_density, own0, own1, own3, other0, rows, panel, line],
        out_shapes, [], 11 * pair_flops, 8 * MIB, {7: 0, 8: 1})
    panel, line, some = call(
        density_2, 2, [where, keep_density, own0, own1, own3, other1, other3, rows, panel, line],
        out_shapes + [jax.ShapeDtypeStruct((ROWS, N // 2), jnp.float32)], [], 11 * pair_flops, 8 * MIB, {8: 0, 9: 1})
    panel, line, own2 = lax.optimization_barrier((panel, line, own2))
    other2 = other_core(own2)
    panel, line = call(
        density_3, 2, [where, keep_density, own0, own1, own2, own3, other0, other1, other3, rows, panel, line],
        out_shapes, [], 10 * pair_flops, 8 * MIB, {10: 0, 11: 1})
    panel, line, low, square = call(
        first_square, 3,
        [where, keep_density, keep_square, own0, own1, own2, own3, other2, rows, some, panel, line],
        out_shapes + [jax.ShapeDtypeStruct((ROWS, N // 2), jnp.bfloat16), full_block],
        [pltpu.VMEM((ROWS, N // 2), jnp.float32)],
        4 * pair_flops + 2 * block_flops, 20 * MIB, {10: 0, 11: 1})

    its = other_core(low)
    early, columns = call(
        early_first_cube, 1, [where, low, panel], [full_block, panel_shape], [], block_flops // 2, 12 * MIB)
    (current,) = call(
        first_density, 2, [where, keep_density, its, columns, early, square], [low_block], [],
        block_flops // 2, 4 * MIB)

    own0, one, three, two, far = lax.optimization_barrier((
        current, from_first(current, 1), from_first(current, 3), from_first(current, 2), from_second(current, 2)))
    near = jnp.concatenate([own0, one, two, three], axis=0)
    one, three = from_second(near, 1), from_second(near, 3)
    far, *own = lax.optimization_barrier((far, *gather(current, from_z)[1:]))
    far = gather(far, from_first)
    own0, *both = lax.optimization_barrier((own0, *own, *far))
    own, far = [own0, *both[:3]], both[3:]
    other = [other_core(part) for part in own]
    half_shape = jax.ShapeDtypeStruct((N // 2, COLS), jnp.bfloat16)
    early, line, mine, its = call(
        early_square, 1, [where, *own, *other, near, *far], [full_block, line_shape, half_shape, half_shape],
        [pltpu.SemaphoreType.DMA((8, 2))], block_flops // 2, 10 * MIB)
    square, low, mine, its = call(
        second_square, 2, [where, keep_square, one, three, early, line, mine, its],
        [full_block, low_block, half_shape, half_shape],
        [pltpu.SemaphoreType.DMA((8, 2))], block_flops // 2, 8 * MIB, {6: 2, 7: 3})

    own0, own1, own2, own3 = gather(low, from_z)
    come = other_core(its)
    (early,) = call(
        early_cube, 1, [where, own0, own1, own3, mine, come],
        [jax.ShapeDtypeStruct((ROWS, 2 * COLS), jnp.float32)], [], block_flops * 3 // 4, 4 * MIB)
    early, own2 = lax.optimization_barrier((early, own2))
    half = jax.ShapeDtypeStruct((B, 2 * COLS), jnp.float32)
    (leave,) = call(
        leaving_density, 1, [where, own2, early, square, mine, come], [half], [], block_flops // 8, 3 * MIB)
    (out,) = call(
        second_density, 1, [where, own2, early, square, mine, come, other_core(leave)], [half], [],
        block_flops // 8, 3 * MIB)
    return out


def solution(mesh):
    placed = (P("row", "col"), P(), P(), P())
    return jax.shard_map(
        body, mesh=mesh, in_specs=placed, out_specs=P("row", "col"), check_vma=False
    )
```

```python
import jax
import jax.numpy as jnp
from jax import lax
from jax.experimental import pallas as pl
from jax.experimental.pallas import tpu as pltpu
from jax.sharding import PartitionSpec as P

B = 128
N = 4096
K = 1024
ROWS = 256
COLS = 512
AXES = ("row", "col")
MIB = 1024 * 1024


def device(x, y, core, z):
    return (((x % 4) * 4 + y % 4) * 2 + core) * 4 + z % 4


def pairs(target):
    return [
        (device(x, y, core, z), device(*target(x, y, core, z)))
        for x in range(4) for y in range(4) for core in range(2) for z in range(4)
    ]


def other_core(a):
    return lax.ppermute(a, AXES, pairs(lambda x, y, core, z: (x, y, 1 - core, z)))


def from_z(a, d):
    return lax.ppermute(a, AXES, pairs(lambda x, y, core, z: (x, y, core, z - d)))


def from_first(a, d):
    return lax.ppermute(a, AXES, pairs(
        lambda x, y, core, z: (x - d, y, core, z) if core == 0 else (x, y - d, core, z)))


def from_second(a, d):
    return lax.ppermute(a, AXES, pairs(
        lambda x, y, core, z: (x, y - d, core, z) if core == 0 else (x - d, y, core, z)))


def gather(a, fetch):
    one, three, two = fetch(a, 1), fetch(a, 3), fetch(a, 2)
    return [a, one, two, three]


def place(x, y, kind, first, second):
    px = jnp.where(kind == 0, x + first, x + second) & 3
    py = jnp.where(kind == 0, y + second, y + first) & 3
    return px, py


def dot_t(a, b):
    return lax.dot_general(a, b, (((1,), (1,)), ((), ())), preferred_element_type=jnp.float32)


def dot(a, b):
    return jnp.dot(a, b, preferred_element_type=jnp.float32)


def aligned(block, size):
    return pl.ds(pl.multiple_of(block * size, size), size)


def block_at(x, y, kind, place_in_order):
    px, py = place(x, y, kind, place_in_order % 4, place_in_order // 4)
    return px * 8 + py * 2 + kind


def some_rows(where, keep_d, rows, half, parts, line):
    x, y, core = where[0], where[1], where[2]
    kind = core if half == 0 else 1 - core
    for n, part in parts.items():
        value = dot_t(rows[...], part[...])
        for u in range(4):
            block = block_at(x, y, kind, n * 4 + u)
            at = (half * 16 + n * 4 + u) * B
            for t in range(2):
                keep = keep_d[0, (x * 4 + y) * 2 + t, block].astype(jnp.float32)
                piece = value[t * B:(t + 1) * B, u * B:(u + 1) * B] * keep
                line[t * B:(t + 1) * B, at:at + B] = piece.astype(jnp.bfloat16)


def some_columns(where, keep_d, half, parts, columns, panel, mirrored=()):
    x, y, core = where[0], where[1], where[2]
    kind = core if half == 0 else 1 - core

    def put(value, kind, n, i, m, u, turn):
        keep = keep_d[0, block_at(x, y, kind, n * 4 + i), block_at(x, y, core, m * 4 + u)]
        piece = (value * keep.astype(jnp.float32)).astype(jnp.bfloat16)
        at, to = (half * 16 + n * 4 + i) * B, (m * 4 + u) * B
        panel[at:at + B, to:to + B] = piece.T if turn else piece

    for n, part in parts.items():
        for m, column in columns.items():
            if (n, m) in mirrored:
                continue
            value = dot_t(part[...], column[...])
            for i in range(4):
                for u in range(4):
                    piece = value[i * B:(i + 1) * B, u * B:(u + 1) * B]
                    put(piece, kind, n, i, m, u, False)
                    if (m, n) in mirrored:
                        put(piece, core, m, u, n, i, True)


EARLY = (0, 1, 3)


def density_0(where, keep_d, own0, other0, panel, line, rows):
    first = where[2] == 0
    mine, its = own0[:B, :], other0[:B, :]
    rows[:B, :] = jnp.where(first, mine, its)
    rows[B:, :] = jnp.where(first, its, mine)
    for half, part in enumerate((own0, other0)):
        some_rows(where, keep_d, rows, half, {0: part}, line)
        some_columns(where, keep_d, half, {0: part}, {0: own0}, panel)


def density_1(where, keep_d, own0, own1, own3, other0, rows, _, __, panel, line):
    own = {0: own0, 1: own1, 3: own3}
    some_rows(where, keep_d, rows, 0, {1: own1, 3: own3}, line)
    some_columns(where, keep_d, 0, {0: own0}, {1: own1, 3: own3}, panel, ((1, 0), (3, 0)))
    some_columns(where, keep_d, 0, {1: own1, 3: own3}, {1: own1, 3: own3}, panel, ((3, 1),))
    some_columns(where, keep_d, 1, {0: other0}, {1: own1, 3: own3}, panel)


def density_2(where, keep_d, own0, own1, own3, other1, other3, rows, _, __, panel, line, some):
    other = {1: other1, 3: other3}
    some_rows(where, keep_d, rows, 1, other, line)
    some_columns(where, keep_d, 1, other, {0: own0, 1: own1, 3: own3}, panel)

    @pl.loop(0, 3)
    def _(part):
        at = aligned(part + part // 2, 512)
        some[:, at] = (
            dot(line[:, :1024], panel[:1024, at])
            + dot(line[:, 1536:3072], panel[1536:3072, at])
            + dot(line[:, 3584:], panel[3584:, at]))


def density_3(where, keep_d, own0, own1, own2, own3, other0, other1, other3, rows, _, __, panel, line):
    some_rows(where, keep_d, rows, 0, {2: own2}, line)
    own = {0: own0, 1: own1, 2: own2, 3: own3}
    some_columns(where, keep_d, 0, {2: own2}, own, panel, ((0, 2), (1, 2), (3, 2)))
    some_columns(where, keep_d, 1, {0: other0, 1: other1, 3: other3}, {2: own2}, panel)


def first_square(where, keep_d, keep_s, own0, own1, own2, own3, other2, rows, some, _, __, panel, line, low, square, total):
    x, y, core, z = where[0], where[1], where[2], where[3]
    some_rows(where, keep_d, rows, 1, {2: other2}, line)
    some_columns(where, keep_d, 1, {2: other2}, {0: own0, 1: own1, 2: own2, 3: own3}, panel)

    def put(value, part):
        for t in range(2):
            for u in range(4):
                block = block_at(x, y, core, part * 4 + u)
                keep = keep_s[0, (x * 4 + y) * 2 + t, block].astype(jnp.float32)
                piece = value[t * B:(t + 1) * B, u * B:(u + 1) * B] * keep
                total[t * B:(t + 1) * B, aligned(part * 4 + u, B)] = piece
                low[t * B:(t + 1) * B, aligned(part * 4 + u, B)] = piece.astype(jnp.bfloat16)

    @pl.loop(0, 3)
    def _(n):
        part = n + n // 2
        at = aligned(part, 512)
        put(some[:, at] + dot(line[:, 1024:1536], panel[1024:1536, at])
            + dot(line[:, 3072:3584], panel[3072:3584, at]), part)

    put(dot(line[...], panel[:, 1024:1536]), 2)
    for t in range(4):
        square[:, t * B:(t + 1) * B] = total[:, aligned(column_at(where, t), B)]


def column_at(where, t):
    x, y, core, z = where[0], where[1], where[2], where[3]
    dx, dy = (z - x) & 3, (t - y) & 3
    return jnp.where(core == 0, dy * 4 + dx, dx * 4 + dy)


def early_first_cube(where, low, panel, early, columns):
    for t in range(4):
        at = aligned(column_at(where, t), B)
        columns[:, t * B:(t + 1) * B] = panel[:, at]
    early[...] = dot(low[...], columns[:2048, :])


def first_density(where, keep_d, its, columns, early, square, out):
    x, y, core, z = where[0], where[1], where[2], where[3]
    value = 3.0 * square[...] - 2.0 * (early[...] + dot(its[...], columns[2048:, :]))
    for t in range(2):
        for u in range(4):
            keep = keep_d[1, (x * 4 + y) * 2 + t, z * 8 + u * 2 + core].astype(jnp.float32)
            piece = value[t * B:(t + 1) * B, u * B:(u + 1) * B] * keep
            out[t * B:(t + 1) * B, u * B:(u + 1) * B] = piece.astype(jnp.bfloat16)


def chips_times(where, line, chips, mine, its):
    x, y, core = where[0], where[1], where[2]
    left, right = [], []
    for ref, offset, first, second in chips:
        px, py = place(x, y, core, first, second)
        chip = px * 4 + py
        mine[aligned(chip, B), :] = ref[pl.ds(pl.multiple_of(offset + core * B, B), B), :]
        its[aligned(chip, B), :] = ref[pl.ds(pl.multiple_of(offset + (1 - core) * B, B), B), :]
        left.append(line[:, aligned(chip, ROWS)])
        right.append(ref[offset:offset + ROWS, :])
    total = None
    for n in range(0, len(chips), 4):
        term = dot(jnp.concatenate(left[n:n + 4], axis=1), jnp.concatenate(right[n:n + 4], axis=0))
        total = term if total is None else total + term
    return total


def early_square(where, *refs):
    own, other, near, far, (early, line, mine, its) = refs[:4], refs[4:8], refs[8], refs[9:13], refs[13:]
    core, z = where[2], where[3]
    for d in range(4):
        for ref, kind in ((own[d], core), (other[d], 1 - core)):
            for t in range(4):
                line[:, aligned(((z + d) & 3) * 8 + t * 2 + kind, B)] = ref[:, t * B:(t + 1) * B]
    chips = [(near, i * ROWS, i, 0) for i in range(4)] + [(far[i], 0, i, 2) for i in range(4)]
    early[...] = chips_times(where, line, chips, mine, its)


def second_square(where, keep_s, one, three, early, line, _, __, square, low, mine, its):
    x, y, core, z = where[0], where[1], where[2], where[3]
    chips = [(ref, i * ROWS, i, j) for ref, j in ((one, 1), (three, 3)) for i in range(4)]
    value = early[...] + chips_times(where, line, chips, mine, its)
    for t in range(2):
        for u in range(4):
            keep = keep_s[1, (x * 4 + y) * 2 + t, z * 8 + u * 2 + core].astype(jnp.float32)
            piece = value[t * B:(t + 1) * B, u * B:(u + 1) * B] * keep
            square[t * B:(t + 1) * B, u * B:(u + 1) * B] = piece
            low[t * B:(t + 1) * B, u * B:(u + 1) * B] = piece.astype(jnp.bfloat16)


def parts_times_panel(parts, z, mine, come):
    total = [None, None]
    for value, d in parts:
        for n, panel in enumerate((mine, come)):
            term = dot(value, panel[aligned((z + d) & 3, 512), :])
            total[n] = term if total[n] is None else total[n] + term
    return total


def early_cube(where, own0, own1, own3, mine, come, out):
    parts = [(own0[...], 0), (own1[...], 1), (own3[...], 3)]
    out[:, :COLS], out[:, COLS:] = parts_times_panel(parts, where[3], mine, come)


def density_share(where, at, own2, early, square, mine, come):
    first, second = parts_times_panel([(own2[at, :], 2)], where[3], mine, come)
    return 3.0 * square[at, :] - 2.0 * (early[at, :COLS] + first), -2.0 * (early[at, COLS:] + second)


def leaving_density(where, own2, early, square, mine, come, out):
    at = aligned(1 - where[2], B)
    out[:, :COLS], out[:, COLS:] = density_share(where, at, own2, early, square, mine, come)


def second_density(where, own2, early, square, mine, come, share, out):
    own, other = density_share(where, aligned(where[2], B), own2, early, square, mine, come)
    own, other = own + share[:, COLS:], other + share[:, :COLS]
    first = where[2] == 0
    for t in range(4):
        one, two = own[:, t * B:(t + 1) * B], other[:, t * B:(t + 1) * B]
        out[:, 2 * t * B:(2 * t + 1) * B] = jnp.where(first, one, two)
        out[:, (2 * t + 1) * B:(2 * t + 2) * B] = jnp.where(first, two, one)


SMEM = pl.BlockSpec(memory_space=pltpu.SMEM)
VMEM = pl.BlockSpec(memory_space=pltpu.VMEM)


def call(kernel, n_smem, ins, outs, scratch, flops, moved, aliases={}):
    return pl.pallas_call(
        kernel,
        in_specs=[SMEM] * n_smem + [VMEM] * (len(ins) - n_smem),
        out_specs=[VMEM] * len(outs),
        out_shape=outs,
        scratch_shapes=scratch,
        input_output_aliases=aliases,
        cost_estimate=pl.CostEstimate(flops=flops, bytes_accessed=moved, transcendentals=0),
        compiler_params=pltpu.CompilerParams(vmem_limit_bytes=12 * MIB),
    )(*ins)


def body(coeffs, coef_pattern, keep_density, keep_square):
    r, z = lax.axis_index("row"), lax.axis_index("col")
    x, y, core = r // 8, (r // 2) % 4, r % 2
    where = jnp.stack([x, y, core, z]).astype(jnp.int32)
    low_block = jax.ShapeDtypeStruct((ROWS, COLS), jnp.bfloat16)
    full_block = jax.ShapeDtypeStruct((ROWS, COLS), jnp.float32)
    panel_shape = jax.ShapeDtypeStruct((N, COLS), jnp.bfloat16)
    line_shape = jax.ShapeDtypeStruct((ROWS, N), jnp.bfloat16)
    wide_shape = jax.ShapeDtypeStruct((N, N // 2), jnp.bfloat16)
    block_flops = 2 * ROWS * N * COLS
    pair_flops = 2 * 512 * 512 * K

    kept = jnp.concatenate(gather(coeffs, from_z), axis=1)
    pattern = lax.dynamic_slice(coef_pattern, (r, 0), (1, 8)).reshape(4, 2)
    pattern = jnp.concatenate([pattern, pattern], axis=0)
    pattern = lax.dynamic_slice(pattern, (z, 0), (4, 2)).reshape(1, 8)
    kept = kept * jnp.repeat(pattern, B, 1).astype(jnp.bfloat16)
    near = jnp.concatenate(gather(kept, from_first), axis=0)
    own1, own3, other0 = from_second(near, 1), from_second(near, 3), other_core(near)
    rows_shape = jax.ShapeDtypeStruct((ROWS, K), jnp.bfloat16)
    out_shapes = [wide_shape, line_shape]
    panel, line, rows = call(
        density_0, 2, [where, keep_density, near, other0], out_shapes + [rows_shape], [], pair_flops // 8, MIB)
    panel, line, own0, own1, own3 = lax.optimization_barrier((panel, line, near, own1, own3))
    own2 = from_second(own0, 2)
    other1, other3 = other_core(own1), other_core(own3)
    panel, line = call(
        density_1, 2, [where, keep_density, own0, own1, own3, other0, rows, panel, line],
        out_shapes, [], 11 * pair_flops, 8 * MIB, {7: 0, 8: 1})
    panel, line, some = call(
        density_2, 2, [where, keep_density, own0, own1, own3, other1, other3, rows, panel, line],
        out_shapes + [jax.ShapeDtypeStruct((ROWS, N // 2), jnp.float32)], [], 11 * pair_flops, 8 * MIB, {8: 0, 9: 1})
    panel, line, own2 = lax.optimization_barrier((panel, line, own2))
    other2 = other_core(own2)
    panel, line = call(
        density_3, 2, [where, keep_density, own0, own1, own2, own3, other0, other1, other3, rows, panel, line],
        out_shapes, [], 10 * pair_flops, 8 * MIB, {10: 0, 11: 1})
    panel, line, low, square = call(
        first_square, 3,
        [where, keep_density, keep_square, own0, own1, own2, own3, other2, rows, some, panel, line],
        out_shapes + [jax.ShapeDtypeStruct((ROWS, N // 2), jnp.bfloat16), full_block],
        [pltpu.VMEM((ROWS, N // 2), jnp.float32)],
        4 * pair_flops + 2 * block_flops, 20 * MIB, {10: 0, 11: 1})

    its = other_core(low)
    early, columns = call(
        early_first_cube, 1, [where, low, panel], [full_block, panel_shape], [], block_flops // 2, 12 * MIB)
    (current,) = call(
        first_density, 2, [where, keep_density, its, columns, early, square], [low_block], [],
        block_flops // 2, 4 * MIB)

    own0, one, three, two, far = lax.optimization_barrier((
        current, from_first(current, 1), from_first(current, 3), from_first(current, 2), from_second(current, 2)))
    near = jnp.concatenate([own0, one, two, three], axis=0)
    one, three = from_second(near, 1), from_second(near, 3)
    far, *own = lax.optimization_barrier((far, *gather(current, from_z)[1:]))
    far, own = gather(far, from_first), [own0, *own]
    other = [other_core(part) for part in own]
    half_shape = jax.ShapeDtypeStruct((N // 2, COLS), jnp.bfloat16)
    early, line, mine, its = call(
        early_square, 1, [where, *own, *other, near, *far], [full_block, line_shape, half_shape, half_shape],
        [], block_flops // 2, 10 * MIB)
    square, low, mine, its = call(
        second_square, 2, [where, keep_square, one, three, early, line, mine, its],
        [full_block, low_block, half_shape, half_shape],
        [], block_flops // 2, 8 * MIB, {6: 2, 7: 3})

    own0, own1, own2, own3 = gather(low, from_z)
    come = other_core(its)
    (early,) = call(
        early_cube, 1, [where, own0, own1, own3, mine, come],
        [jax.ShapeDtypeStruct((ROWS, 2 * COLS), jnp.float32)], [], block_flops * 3 // 4, 4 * MIB)
    early, own2 = lax.optimization_barrier((early, own2))
    half = jax.ShapeDtypeStruct((B, 2 * COLS), jnp.float32)
    (leave,) = call(
        leaving_density, 1, [where, own2, early, square, mine, come], [half], [], block_flops // 8, 3 * MIB)
    (out,) = call(
        second_density, 1, [where, own2, early, square, mine, come, other_core(leave)], [half], [],
        block_flops // 8, 3 * MIB)
    return out


def solution(mesh):
    placed = (P("row", "col"), P(), P(), P())
    return jax.shard_map(
        body, mesh=mesh, in_specs=placed, out_specs=P("row", "col"), check_vma=False
    )
```

```python
import functools

import jax
import jax.numpy as jnp
from jax import lax
from jax.experimental import pallas as pl
from jax.experimental.pallas import tpu as pltpu
from jax.sharding import PartitionSpec as P

B = 128
N = 4096
K = 1024
ROWS = 256
COLS = 512
AXES = ("row", "col")
MIB = 1024 * 1024


def device(x, y, core, z):
    return (((x % 4) * 4 + y % 4) * 2 + core) * 4 + z % 4


def pairs(target):
    return [
        (device(x, y, core, z), device(*target(x, y, core, z)))
        for x in range(4) for y in range(4) for core in range(2) for z in range(4)
    ]


def other_core(a):
    return lax.ppermute(a, AXES, pairs(lambda x, y, core, z: (x, y, 1 - core, z)))


def from_z(a, d):
    return lax.ppermute(a, AXES, pairs(lambda x, y, core, z: (x, y, core, z - d)))


def from_first(a, d):
    return lax.ppermute(a, AXES, pairs(
        lambda x, y, core, z: (x - d, y, core, z) if core == 0 else (x, y - d, core, z)))


def from_second(a, d):
    return lax.ppermute(a, AXES, pairs(
        lambda x, y, core, z: (x, y - d, core, z) if core == 0 else (x - d, y, core, z)))


def gather(a, fetch):
    one, three, two = fetch(a, 1), fetch(a, 3), fetch(a, 2)
    return [a, one, two, three]


def place(x, y, kind, first, second):
    px = jnp.where(kind == 0, x + first, x + second) & 3
    py = jnp.where(kind == 0, y + second, y + first) & 3
    return px, py


def dot_t(a, b):
    return lax.dot_general(a, b, (((1,), (1,)), ((), ())), preferred_element_type=jnp.float32)


def dot(a, b):
    return jnp.dot(a, b, preferred_element_type=jnp.float32)


def aligned(block, size):
    return pl.ds(pl.multiple_of(block * size, size), size)


def block_at(x, y, kind, place_in_order):
    px, py = place(x, y, kind, place_in_order % 4, place_in_order // 4)
    return px * 8 + py * 2 + kind


def some_rows(where, keep_d, rows, half, parts, line):
    x, y, core = where[0], where[1], where[2]
    kind = core if half == 0 else 1 - core
    for n, part in parts.items():
        value = dot_t(rows[...], part[...])
        for u in range(4):
            block = block_at(x, y, kind, n * 4 + u)
            at = (half * 16 + n * 4 + u) * B
            for t in range(2):
                keep = keep_d[0, (x * 4 + y) * 2 + t, block].astype(jnp.float32)
                piece = value[t * B:(t + 1) * B, u * B:(u + 1) * B] * keep
                line[t * B:(t + 1) * B, at:at + B] = piece.astype(jnp.bfloat16)


def some_columns(where, keep_d, half, parts, columns, panel, mirrored=()):
    x, y, core = where[0], where[1], where[2]
    kind = core if half == 0 else 1 - core

    def put(value, kind, n, i, m, u, turn):
        keep = keep_d[0, block_at(x, y, kind, n * 4 + i), block_at(x, y, core, m * 4 + u)]
        piece = (value * keep.astype(jnp.float32)).astype(jnp.bfloat16)
        at, to = (half * 16 + n * 4 + i) * B, (m * 4 + u) * B
        panel[at:at + B, to:to + B] = piece.T if turn else piece

    for n, part in parts.items():
        for m, column in columns.items():
            if (n, m) in mirrored:
                continue
            value = dot_t(part[...], column[...])
            for i in range(4):
                for u in range(4):
                    piece = value[i * B:(i + 1) * B, u * B:(u + 1) * B]
                    put(piece, kind, n, i, m, u, False)
                    if (m, n) in mirrored:
                        put(piece, core, m, u, n, i, True)


EARLY = (0, 1, 3)


def density_0(where, keep_d, own0, other0, panel, line, rows):
    first = where[2] == 0
    mine, its = own0[:B, :], other0[:B, :]
    rows[:B, :] = jnp.where(first, mine, its)
    rows[B:, :] = jnp.where(first, its, mine)
    for half, part in enumerate((own0, other0)):
        some_rows(where, keep_d, rows, half, {0: part}, line)
        some_columns(where, keep_d, half, {0: part}, {0: own0}, panel)


def density_1(where, keep_d, own0, own1, own3, other0, rows, _, __, panel, line):
    own = {0: own0, 1: own1, 3: own3}
    some_rows(where, keep_d, rows, 0, {1: own1, 3: own3}, line)
    some_columns(where, keep_d, 0, {0: own0}, {1: own1, 3: own3}, panel, ((1, 0), (3, 0)))
    some_columns(where, keep_d, 0, {1: own1, 3: own3}, {1: own1, 3: own3}, panel, ((3, 1),))
    some_columns(where, keep_d, 1, {0: other0}, {1: own1, 3: own3}, panel)


def density_2(where, keep_d, own0, own1, own3, other1, other3, rows, _, __, panel, line, some):
    other = {1: other1, 3: other3}
    some_rows(where, keep_d, rows, 1, other, line)
    some_columns(where, keep_d, 1, other, {0: own0, 1: own1, 3: own3}, panel)

    @pl.loop(0, 3)
    def _(part):
        at = aligned(part + part // 2, 512)
        some[:, at] = (
            dot(line[:, :1024], panel[:1024, at])
            + dot(line[:, 1536:3072], panel[1536:3072, at])
            + dot(line[:, 3584:], panel[3584:, at]))


def density_3(where, keep_d, own0, own1, own2, own3, other0, other1, other3, rows, _, __, panel, line):
    some_rows(where, keep_d, rows, 0, {2: own2}, line)
    own = {0: own0, 1: own1, 2: own2, 3: own3}
    some_columns(where, keep_d, 0, {2: own2}, own, panel, ((0, 2), (1, 2), (3, 2)))
    some_columns(where, keep_d, 1, {0: other0, 1: other1, 3: other3}, {2: own2}, panel)


def first_square(where, keep_d, keep_s, own0, own1, own2, own3, other2, rows, some, _, __, panel, line, low, square, total):
    x, y, core, z = where[0], where[1], where[2], where[3]
    some_rows(where, keep_d, rows, 1, {2: other2}, line)
    some_columns(where, keep_d, 1, {2: other2}, {0: own0, 1: own1, 2: own2, 3: own3}, panel)

    def put(value, part):
        for t in range(2):
            for u in range(4):
                block = block_at(x, y, core, part * 4 + u)
                keep = keep_s[0, (x * 4 + y) * 2 + t, block].astype(jnp.float32)
                piece = value[t * B:(t + 1) * B, u * B:(u + 1) * B] * keep
                total[t * B:(t + 1) * B, aligned(part * 4 + u, B)] = piece
                low[t * B:(t + 1) * B, aligned(part * 4 + u, B)] = piece.astype(jnp.bfloat16)

    @pl.loop(0, 3)
    def _(n):
        part = n + n // 2
        at = aligned(part, 512)
        put(some[:, at] + dot(line[:, 1024:1536], panel[1024:1536, at])
            + dot(line[:, 3072:3584], panel[3072:3584, at]), part)

    put(dot(line[...], panel[:, 1024:1536]), 2)
    for t in range(4):
        square[:, t * B:(t + 1) * B] = total[:, aligned(column_at(where, t), B)]


def column_at(where, t):
    x, y, core, z = where[0], where[1], where[2], where[3]
    dx, dy = (z - x) & 3, (t - y) & 3
    return jnp.where(core == 0, dy * 4 + dx, dx * 4 + dy)


def early_first_cube(where, low, panel, early, columns):
    for t in range(4):
        at = aligned(column_at(where, t), B)
        columns[:, t * B:(t + 1) * B] = panel[:, at]
    early[...] = dot(low[...], columns[:2048, :])


def first_density(where, keep_d, its, columns, early, square, out):
    x, y, core, z = where[0], where[1], where[2], where[3]
    value = 3.0 * square[...] - 2.0 * (early[...] + dot(its[...], columns[2048:, :]))
    for t in range(2):
        for u in range(4):
            keep = keep_d[1, (x * 4 + y) * 2 + t, z * 8 + u * 2 + core].astype(jnp.float32)
            piece = value[t * B:(t + 1) * B, u * B:(u + 1) * B] * keep
            out[t * B:(t + 1) * B, u * B:(u + 1) * B] = piece.astype(jnp.bfloat16)


def chips_times(where, line, chips, mine, its):
    x, y, core = where[0], where[1], where[2]
    left, right = [], []
    for ref, offset, first, second in chips:
        px, py = place(x, y, core, first, second)
        chip = px * 4 + py
        mine[aligned(chip, B), :] = ref[pl.ds(pl.multiple_of(offset + core * B, B), B), :]
        its[aligned(chip, B), :] = ref[pl.ds(pl.multiple_of(offset + (1 - core) * B, B), B), :]
        left.append(line[:, aligned(chip, ROWS)])
        right.append(ref[offset:offset + ROWS, :])
    total = None
    for n in range(0, len(chips), 4):
        term = dot(jnp.concatenate(left[n:n + 4], axis=1), jnp.concatenate(right[n:n + 4], axis=0))
        total = term if total is None else total + term
    return total


def early_square(where, *refs):
    own, other, near, far, (early, line, mine, its) = refs[:4], refs[4:8], refs[8], refs[9:13], refs[13:]
    core, z = where[2], where[3]
    for d in range(4):
        for ref, kind in ((own[d], core), (other[d], 1 - core)):
            for t in range(4):
                line[:, aligned(((z + d) & 3) * 8 + t * 2 + kind, B)] = ref[:, t * B:(t + 1) * B]
    chips = [(near, i * ROWS, i, 0) for i in range(4)] + [(far[i], 0, i, 2) for i in range(4)]
    early[...] = chips_times(where, line, chips, mine, its)


def second_square(where, keep_s, one, three, early, line, _, __, square, low, mine, its):
    x, y, core, z = where[0], where[1], where[2], where[3]
    chips = [(ref, i * ROWS, i, j) for ref, j in ((one, 1), (three, 3)) for i in range(4)]
    value = early[...] + chips_times(where, line, chips, mine, its)
    for t in range(2):
        for u in range(4):
            keep = keep_s[1, (x * 4 + y) * 2 + t, z * 8 + u * 2 + core].astype(jnp.float32)
            piece = value[t * B:(t + 1) * B, u * B:(u + 1) * B] * keep
            square[t * B:(t + 1) * B, u * B:(u + 1) * B] = piece
            low[t * B:(t + 1) * B, u * B:(u + 1) * B] = piece.astype(jnp.bfloat16)


def parts_times_panel(parts, z, panel):
    total = None
    for value, d in parts:
        term = dot(value, panel[aligned((z + d) & 3, 512), :])
        total = term if total is None else total + term
    return total


def early_cube(where, own0, mine, out):
    out[...] = parts_times_panel([(own0[...], 0)], where[3], mine)


def density_share(leave, where, own0, own1, own2, own3, early, square, mine, come, out):
    core, z = where[2], where[3]
    at = aligned(1 - core if leave else core, B)
    parts = [(own1[at, :], 1), (own3[at, :], 3), (own2[at, :], 2)]
    out[:, :COLS] = 3.0 * square[at, :] - 2.0 * (early[at, :] + parts_times_panel(parts, z, mine))
    out[:, COLS:] = -2.0 * parts_times_panel([(own0[at, :], 0)] + parts, z, come)


def join(where, stay, share, out):
    first = where[2] == 0
    for t in range(4):
        at, far = slice(t * B, (t + 1) * B), slice(COLS + t * B, COLS + (t + 1) * B)
        own, other = stay[:, at] + share[:, far], stay[:, far] + share[:, at]
        out[:, 2 * t * B:(2 * t + 1) * B] = jnp.where(first, own, other)
        out[:, (2 * t + 1) * B:(2 * t + 2) * B] = jnp.where(first, other, own)


SMEM = pl.BlockSpec(memory_space=pltpu.SMEM)
VMEM = pl.BlockSpec(memory_space=pltpu.VMEM)


def call(kernel, n_smem, ins, outs, scratch, flops, moved, aliases={}):
    return pl.pallas_call(
        kernel,
        in_specs=[SMEM] * n_smem + [VMEM] * (len(ins) - n_smem),
        out_specs=[VMEM] * len(outs),
        out_shape=outs,
        scratch_shapes=scratch,
        input_output_aliases=aliases,
        cost_estimate=pl.CostEstimate(flops=flops, bytes_accessed=moved, transcendentals=0),
        compiler_params=pltpu.CompilerParams(vmem_limit_bytes=12 * MIB),
    )(*ins)


def body(coeffs, coef_pattern, keep_density, keep_square):
    r, z = lax.axis_index("row"), lax.axis_index("col")
    x, y, core = r // 8, (r // 2) % 4, r % 2
    where = jnp.stack([x, y, core, z]).astype(jnp.int32)
    low_block = jax.ShapeDtypeStruct((ROWS, COLS), jnp.bfloat16)
    full_block = jax.ShapeDtypeStruct((ROWS, COLS), jnp.float32)
    panel_shape = jax.ShapeDtypeStruct((N, COLS), jnp.bfloat16)
    line_shape = jax.ShapeDtypeStruct((ROWS, N), jnp.bfloat16)
    wide_shape = jax.ShapeDtypeStruct((N, N // 2), jnp.bfloat16)
    block_flops = 2 * ROWS * N * COLS
    pair_flops = 2 * 512 * 512 * K

    kept = jnp.concatenate(gather(coeffs, from_z), axis=1)
    pattern = lax.dynamic_slice(coef_pattern, (r, 0), (1, 8)).reshape(4, 2)
    pattern = jnp.concatenate([pattern, pattern], axis=0)
    pattern = lax.dynamic_slice(pattern, (z, 0), (4, 2)).reshape(1, 8)
    kept = kept * jnp.repeat(pattern, B, 1).astype(jnp.bfloat16)
    near = jnp.concatenate(gather(kept, from_first), axis=0)
    own1, own3, other0 = from_second(near, 1), from_second(near, 3), other_core(near)
    rows_shape = jax.ShapeDtypeStruct((ROWS, K), jnp.bfloat16)
    out_shapes = [wide_shape, line_shape]
    panel, line, rows = call(
        density_0, 2, [where, keep_density, near, other0], out_shapes + [rows_shape], [], pair_flops // 8, MIB)
    panel, line, own0, own1, own3 = lax.optimization_barrier((panel, line, near, own1, own3))
    own2 = from_second(own0, 2)
    other1, other3 = other_core(own1), other_core(own3)
    panel, line = call(
        density_1, 2, [where, keep_density, own0, own1, own3, other0, rows, panel, line],
        out_shapes, [], 11 * pair_flops, 8 * MIB, {7: 0, 8: 1})
    panel, line, some = call(
        density_2, 2, [where, keep_density, own0, own1, own3, other1, other3, rows, panel, line],
        out_shapes + [jax.ShapeDtypeStruct((ROWS, N // 2), jnp.float32)], [], 11 * pair_flops, 8 * MIB, {8: 0, 9: 1})
    panel, line, own2 = lax.optimization_barrier((panel, line, own2))
    other2 = other_core(own2)
    panel, line = call(
        density_3, 2, [where, keep_density, own0, own1, own2, own3, other0, other1, other3, rows, panel, line],
        out_shapes, [], 10 * pair_flops, 8 * MIB, {10: 0, 11: 1})
    panel, line, low, square = call(
        first_square, 3,
        [where, keep_density, keep_square, own0, own1, own2, own3, other2, rows, some, panel, line],
        out_shapes + [jax.ShapeDtypeStruct((ROWS, N // 2), jnp.bfloat16), full_block],
        [pltpu.VMEM((ROWS, N // 2), jnp.float32)],
        4 * pair_flops + 2 * block_flops, 20 * MIB, {10: 0, 11: 1})

    its = other_core(low)
    early, columns = call(
        early_first_cube, 1, [where, low, panel], [full_block, panel_shape], [], block_flops // 2, 12 * MIB)
    (current,) = call(
        first_density, 2, [where, keep_density, its, columns, early, square], [low_block], [],
        block_flops // 2, 4 * MIB)

    own0, one, three, two, far = lax.optimization_barrier((
        current, from_first(current, 1), from_first(current, 3), from_first(current, 2), from_second(current, 2)))
    near = jnp.concatenate([own0, one, two, three], axis=0)
    one, three = from_second(near, 1), from_second(near, 3)
    far, *own = lax.optimization_barrier((far, *gather(current, from_z)[1:]))
    far, own = gather(far, from_first), [own0, *own]
    other = [other_core(part) for part in own]
    half_shape = jax.ShapeDtypeStruct((N // 2, COLS), jnp.bfloat16)
    early, line, mine, its = call(
        early_square, 1, [where, *own, *other, near, *far], [full_block, line_shape, half_shape, half_shape],
        [], block_flops // 2, 10 * MIB)
    square, low, mine, its = call(
        second_square, 2, [where, keep_square, one, three, early, line, mine, its],
        [full_block, low_block, half_shape, half_shape],
        [], block_flops // 2, 8 * MIB, {6: 2, 7: 3})

    own0, own1, own2, own3 = gather(low, from_z)
    come = other_core(its)
    (early,) = call(
        early_cube, 1, [where, own0, mine], [full_block], [], block_flops // 8, 2 * MIB)
    half = jax.ShapeDtypeStruct((B, 2 * COLS), jnp.float32)
    last = [where, own0, own1, own2, own3, early, square, mine, come]
    (leave,) = call(functools.partial(density_share, True), 1, last, [half], [], block_flops * 3 // 8, 5 * MIB)
    share = other_core(leave)
    (stay,) = call(functools.partial(density_share, False), 1, last, [half], [], block_flops * 3 // 8, 5 * MIB)
    (out,) = call(join, 1, [where, stay, share], [half], [], 0, 2 * MIB)
    return out


def solution(mesh):
    placed = (P("row", "col"), P(), P(), P())
    return jax.shard_map(
        body, mesh=mesh, in_specs=placed, out_specs=P("row", "col"), check_vma=False
    )
```

```python
import jax
import jax.numpy as jnp
from jax import lax
from jax.experimental import pallas as pl
from jax.experimental.pallas import tpu as pltpu
from jax.sharding import PartitionSpec as P

B = 128
N = 4096
K = 1024
ROWS = 256
COLS = 512
AXES = ("row", "col")
MIB = 1024 * 1024


def device(x, y, core, z):
    return (((x % 4) * 4 + y % 4) * 2 + core) * 4 + z % 4


def pairs(target):
    return [
        (device(x, y, core, z), device(*target(x, y, core, z)))
        for x in range(4) for y in range(4) for core in range(2) for z in range(4)
    ]


def other_core(a):
    return lax.ppermute(a, AXES, pairs(lambda x, y, core, z: (x, y, 1 - core, z)))


def from_z(a, d):
    return lax.ppermute(a, AXES, pairs(lambda x, y, core, z: (x, y, core, z - d)))


def from_first(a, d):
    return lax.ppermute(a, AXES, pairs(
        lambda x, y, core, z: (x - d, y, core, z) if core == 0 else (x, y - d, core, z)))


def from_second(a, d):
    return lax.ppermute(a, AXES, pairs(
        lambda x, y, core, z: (x, y - d, core, z) if core == 0 else (x - d, y, core, z)))


def gather(a, fetch):
    one, three, two = fetch(a, 1), fetch(a, 3), fetch(a, 2)
    return [a, one, two, three]


def place(x, y, kind, first, second):
    px = jnp.where(kind == 0, x + first, x + second) & 3
    py = jnp.where(kind == 0, y + second, y + first) & 3
    return px, py


def dot_t(a, b):
    return lax.dot_general(a, b, (((1,), (1,)), ((), ())), preferred_element_type=jnp.float32)


def dot(a, b):
    return jnp.dot(a, b, preferred_element_type=jnp.float32)


def aligned(block, size):
    return pl.ds(pl.multiple_of(block * size, size), size)


def block_at(x, y, kind, place_in_order):
    px, py = place(x, y, kind, place_in_order % 4, place_in_order // 4)
    return px * 8 + py * 2 + kind


def some_rows(where, keep_d, rows, half, parts, line):
    x, y, core = where[0], where[1], where[2]
    kind = core if half == 0 else 1 - core
    for n, part in parts.items():
        value = dot_t(rows[...], part[...])
        for u in range(4):
            block = block_at(x, y, kind, n * 4 + u)
            at = (half * 16 + n * 4 + u) * B
            for t in range(2):
                keep = keep_d[0, (x * 4 + y) * 2 + t, block].astype(jnp.float32)
                piece = value[t * B:(t + 1) * B, u * B:(u + 1) * B] * keep
                line[t * B:(t + 1) * B, at:at + B] = piece.astype(jnp.bfloat16)


def some_columns(where, keep_d, half, parts, columns, panel, mirrored=()):
    x, y, core = where[0], where[1], where[2]
    kind = core if half == 0 else 1 - core

    def put(value, kind, n, i, m, u, turn):
        keep = keep_d[0, block_at(x, y, kind, n * 4 + i), block_at(x, y, core, m * 4 + u)]
        piece = (value * keep.astype(jnp.float32)).astype(jnp.bfloat16)
        at, to = (half * 16 + n * 4 + i) * B, (m * 4 + u) * B
        panel[at:at + B, to:to + B] = piece.T if turn else piece

    for n, part in parts.items():
        for m, column in columns.items():
            if (n, m) in mirrored:
                continue
            value = dot_t(part[...], column[...])
            for i in range(4):
                for u in range(4):
                    piece = value[i * B:(i + 1) * B, u * B:(u + 1) * B]
                    put(piece, kind, n, i, m, u, False)
                    if (m, n) in mirrored:
                        put(piece, core, m, u, n, i, True)


EARLY = (0, 1, 3)


def density_0(where, keep_d, own0, other0, panel, line, rows):
    first = where[2] == 0
    mine, its = own0[:B, :], other0[:B, :]
    rows[:B, :] = jnp.where(first, mine, its)
    rows[B:, :] = jnp.where(first, its, mine)
    for half, part in enumerate((own0, other0)):
        some_rows(where, keep_d, rows, half, {0: part}, line)
        some_columns(where, keep_d, half, {0: part}, {0: own0}, panel)


def density_1(where, keep_d, own0, own1, own3, other0, rows, _, __, panel, line):
    own = {0: own0, 1: own1, 3: own3}
    some_rows(where, keep_d, rows, 0, {1: own1, 3: own3}, line)
    some_columns(where, keep_d, 0, {0: own0}, {1: own1, 3: own3}, panel, ((1, 0), (3, 0)))
    some_columns(where, keep_d, 0, {1: own1, 3: own3}, {1: own1, 3: own3}, panel, ((3, 1),))
    some_columns(where, keep_d, 1, {0: other0}, {1: own1, 3: own3}, panel)


def density_2(where, keep_d, own0, own1, own3, other1, other3, rows, _, __, panel, line, some):
    other = {1: other1, 3: other3}
    some_rows(where, keep_d, rows, 1, other, line)
    some_columns(where, keep_d, 1, other, {0: own0, 1: own1, 3: own3}, panel)

    @pl.loop(0, 3)
    def _(part):
        at = aligned(part + part // 2, 512)
        some[:, at] = (
            dot(line[:, :1024], panel[:1024, at])
            + dot(line[:, 1536:3072], panel[1536:3072, at])
            + dot(line[:, 3584:], panel[3584:, at]))


def density_3(where, keep_d, own0, own1, own2, own3, other0, other1, other3, rows, _, __, panel, line):
    some_rows(where, keep_d, rows, 0, {2: own2}, line)
    own = {0: own0, 1: own1, 2: own2, 3: own3}
    some_columns(where, keep_d, 0, {2: own2}, own, panel, ((0, 2), (1, 2), (3, 2)))
    some_columns(where, keep_d, 1, {0: other0, 1: other1, 3: other3}, {2: own2}, panel)


def first_square(where, keep_d, keep_s, own0, own1, own2, own3, other2, rows, some, _, __, panel, line, low, total):
    x, y, core, z = where[0], where[1], where[2], where[3]
    some_rows(where, keep_d, rows, 1, {2: other2}, line)
    some_columns(where, keep_d, 1, {2: other2}, {0: own0, 1: own1, 2: own2, 3: own3}, panel)

    def put(value, part):
        for t in range(2):
            for u in range(4):
                block = block_at(x, y, core, part * 4 + u)
                keep = keep_s[0, (x * 4 + y) * 2 + t, block].astype(jnp.float32)
                piece = value[t * B:(t + 1) * B, u * B:(u + 1) * B] * keep
                total[t * B:(t + 1) * B, aligned(part * 4 + u, B)] = piece
                low[t * B:(t + 1) * B, aligned(part * 4 + u, B)] = piece.astype(jnp.bfloat16)

    @pl.loop(0, 3)
    def _(n):
        part = n + n // 2
        at = aligned(part, 512)
        put(some[:, at] + dot(line[:, 1024:1536], panel[1024:1536, at])
            + dot(line[:, 3072:3584], panel[3072:3584, at]), part)

    put(dot(line[...], panel[:, 1024:1536]), 2)


def column_at(where, t):
    x, y, core, z = where[0], where[1], where[2], where[3]
    dx, dy = (z - x) & 3, (t - y) & 3
    return jnp.where(core == 0, dy * 4 + dx, dx * 4 + dy)


def early_first_cube(where, low, panel, early, columns):
    for t in range(4):
        at = aligned(column_at(where, t), B)
        columns[:, t * B:(t + 1) * B] = panel[:, at]
    early[...] = dot(low[...], columns[:2048, :])


def first_density(where, keep_d, its, columns, early, square, out):
    x, y, core, z = where[0], where[1], where[2], where[3]
    cube = early[...] + dot(its[...], columns[2048:, :])
    for u in range(4):
        value = 3.0 * square[:, aligned(column_at(where, u), B)] - 2.0 * cube[:, u * B:(u + 1) * B]
        for t in range(2):
            keep = keep_d[1, (x * 4 + y) * 2 + t, z * 8 + u * 2 + core].astype(jnp.float32)
            piece = value[t * B:(t + 1) * B, :] * keep
            out[t * B:(t + 1) * B, u * B:(u + 1) * B] = piece.astype(jnp.bfloat16)


def density_rows(where, keep_d, low, its, panel, square, out):
    x, y, core = where[0], where[1], where[2]

    @pl.loop(0, 4)
    def _(part):
        at = aligned(part, 512)
        cube = dot(low[...], panel[:2048, at]) + dot(its[...], panel[2048:, at])
        value = 3.0 * square[:, at] - 2.0 * cube
        for t in range(2):
            for u in range(4):
                keep = keep_d[1, (x * 4 + y) * 2 + t, block_at(x, y, core, part * 4 + u)].astype(jnp.float32)
                piece = value[t * B:(t + 1) * B, u * B:(u + 1) * B] * keep
                out[t * B:(t + 1) * B, aligned(part * 4 + u, B)] = piece.astype(jnp.bfloat16)


def chips_times(where, own, other, chips, mine, its):
    x, y, core = where[0], where[1], where[2]
    left, right = [], []
    for ref, offset, first, second in chips:
        px, py = place(x, y, core, first, second)
        chip = px * 4 + py
        for kind, line, at, to in ((core, own, second * 4 + first, mine), (1 - core, other, first * 4 + second, its)):
            block = ref[pl.ds(pl.multiple_of(offset + kind * B, B), B), :]
            to[aligned(chip, B), :] = block
            left.append(line[:, at * B:(at + 1) * B])
            right.append(block)
    total = None
    for n in range(0, len(left), 8):
        term = dot(jnp.concatenate(left[n:n + 8], axis=1), jnp.concatenate(right[n:n + 8], axis=0))
        total = term if total is None else total + term
    return total


def early_square(where, own, other, near, far0, far1, far2, far3, early, mine, its):
    chips = [(near, i * ROWS, i, 0) for i in range(4)]
    chips += [(ref, 0, i, 2) for i, ref in enumerate((far0, far1, far2, far3))]
    early[...] = chips_times(where, own, other, chips, mine, its)


def second_square(where, keep_s, own, other, one, three, early, _, __, square, low, mine, its):
    x, y, core, z = where[0], where[1], where[2], where[3]
    chips = [(ref, i * ROWS, i, j) for ref, j in ((one, 1), (three, 3)) for i in range(4)]
    value = early[...] + chips_times(where, own, other, chips, mine, its)
    for t in range(2):
        for u in range(4):
            keep = keep_s[1, (x * 4 + y) * 2 + t, z * 8 + u * 2 + core].astype(jnp.float32)
            piece = value[t * B:(t + 1) * B, u * B:(u + 1) * B] * keep
            square[t * B:(t + 1) * B, u * B:(u + 1) * B] = piece
            low[t * B:(t + 1) * B, u * B:(u + 1) * B] = piece.astype(jnp.bfloat16)


def parts_times_panel(parts, z, mine, come):
    total = [None, None]
    for value, d in parts:
        for n, panel in enumerate((mine, come)):
            term = dot(value, panel[aligned((z + d) & 3, 512), :])
            total[n] = term if total[n] is None else total[n] + term
    return total


def early_cube(where, own0, own1, own3, mine, come, out):
    parts = [(own0[...], 0), (own1[...], 1), (own3[...], 3)]
    out[:, :COLS], out[:, COLS:] = parts_times_panel(parts, where[3], mine, come)


def density_share(where, at, own2, early, square, mine, come):
    first, second = parts_times_panel([(own2[at, :], 2)], where[3], mine, come)
    return 3.0 * square[at, :] - 2.0 * (early[at, :COLS] + first), -2.0 * (early[at, COLS:] + second)


def leaving_density(where, own2, early, square, mine, come, out):
    at = aligned(1 - where[2], B)
    out[:, :COLS], out[:, COLS:] = density_share(where, at, own2, early, square, mine, come)


def second_density(where, own2, early, square, mine, come, share, out):
    own, other = density_share(where, aligned(where[2], B), own2, early, square, mine, come)
    own, other = own + share[:, COLS:], other + share[:, :COLS]
    first = where[2] == 0
    for t in range(4):
        one, two = own[:, t * B:(t + 1) * B], other[:, t * B:(t + 1) * B]
        out[:, 2 * t * B:(2 * t + 1) * B] = jnp.where(first, one, two)
        out[:, (2 * t + 1) * B:(2 * t + 2) * B] = jnp.where(first, two, one)


SMEM = pl.BlockSpec(memory_space=pltpu.SMEM)
VMEM = pl.BlockSpec(memory_space=pltpu.VMEM)


def call(kernel, n_smem, ins, outs, scratch, flops, moved, aliases={}):
    return pl.pallas_call(
        kernel,
        in_specs=[SMEM] * n_smem + [VMEM] * (len(ins) - n_smem),
        out_specs=[VMEM] * len(outs),
        out_shape=outs,
        scratch_shapes=scratch,
        input_output_aliases=aliases,
        cost_estimate=pl.CostEstimate(flops=flops, bytes_accessed=moved, transcendentals=0),
        compiler_params=pltpu.CompilerParams(vmem_limit_bytes=12 * MIB),
    )(*ins)


def body(coeffs, coef_pattern, keep_density, keep_square):
    r, z = lax.axis_index("row"), lax.axis_index("col")
    x, y, core = r // 8, (r // 2) % 4, r % 2
    where = jnp.stack([x, y, core, z]).astype(jnp.int32)
    low_block = jax.ShapeDtypeStruct((ROWS, COLS), jnp.bfloat16)
    full_block = jax.ShapeDtypeStruct((ROWS, COLS), jnp.float32)
    panel_shape = jax.ShapeDtypeStruct((N, COLS), jnp.bfloat16)
    line_shape = jax.ShapeDtypeStruct((ROWS, N), jnp.bfloat16)
    wide_shape = jax.ShapeDtypeStruct((N, N // 2), jnp.bfloat16)
    block_flops = 2 * ROWS * N * COLS
    pair_flops = 2 * 512 * 512 * K

    kept = jnp.concatenate(gather(coeffs, from_z), axis=1)
    pattern = lax.dynamic_slice(coef_pattern, (r, 0), (1, 8)).reshape(4, 2)
    pattern = jnp.concatenate([pattern, pattern], axis=0)
    pattern = lax.dynamic_slice(pattern, (z, 0), (4, 2)).reshape(1, 8)
    kept = kept * jnp.repeat(pattern, B, 1).astype(jnp.bfloat16)
    near = jnp.concatenate(gather(kept, from_first), axis=0)
    own1, own3, other0 = from_second(near, 1), from_second(near, 3), other_core(near)
    rows_shape = jax.ShapeDtypeStruct((ROWS, K), jnp.bfloat16)
    out_shapes = [wide_shape, line_shape]
    panel, line, rows = call(
        density_0, 2, [where, keep_density, near, other0], out_shapes + [rows_shape], [], pair_flops // 8, MIB)
    panel, line, own0, own1, own3 = lax.optimization_barrier((panel, line, near, own1, own3))
    own2 = from_second(own0, 2)
    other1, other3 = other_core(own1), other_core(own3)
    panel, line = call(
        density_1, 2, [where, keep_density, own0, own1, own3, other0, rows, panel, line],
        out_shapes, [], 11 * pair_flops, 8 * MIB, {7: 0, 8: 1})
    panel, line, some = call(
        density_2, 2, [where, keep_density, own0, own1, own3, other1, other3, rows, panel, line],
        out_shapes + [jax.ShapeDtypeStruct((ROWS, N // 2), jnp.float32)], [], 11 * pair_flops, 8 * MIB, {8: 0, 9: 1})
    panel, line, own2 = lax.optimization_barrier((panel, line, own2))
    other2 = other_core(own2)
    panel, line = call(
        density_3, 2, [where, keep_density, own0, own1, own2, own3, other0, other1, other3, rows, panel, line],
        out_shapes, [], 10 * pair_flops, 8 * MIB, {10: 0, 11: 1})
    panel, line, low, square = call(
        first_square, 3,
        [where, keep_density, keep_square, own0, own1, own2, own3, other2, rows, some, panel, line],
        out_shapes + [jax.ShapeDtypeStruct((ROWS, N // 2), jnp.bfloat16), jax.ShapeDtypeStruct((ROWS, N // 2), jnp.float32)],
        [],
        4 * pair_flops + 2 * block_flops, 20 * MIB, {10: 0, 11: 1})

    its = other_core(low)
    early, columns = call(
        early_first_cube, 1, [where, low, panel], [full_block, panel_shape], [], block_flops // 2, 12 * MIB)
    (current,) = call(
        first_density, 2, [where, keep_density, its, columns, early, square], [low_block], [],
        block_flops // 2, 4 * MIB)

    (own,) = call(
        density_rows, 2, [where, keep_density, low, its, panel, square],
        [jax.ShapeDtypeStruct((ROWS, N // 2), jnp.bfloat16)], [], 4 * block_flops, 22 * MIB)
    start, one, three, two, far, other = lax.optimization_barrier((
        current, from_first(current, 1), from_first(current, 3), from_first(current, 2), from_second(current, 2),
        other_core(own)))
    near = jnp.concatenate([start, one, two, three], axis=0)
    one, three = from_second(near, 1), from_second(near, 3)
    far = gather(far, from_first)
    half_shape = jax.ShapeDtypeStruct((N // 2, COLS), jnp.bfloat16)
    early, mine, its = call(
        early_square, 1, [where, own, other, near, *far], [full_block, half_shape, half_shape],
        [], block_flops // 2, 10 * MIB)
    square, low, mine, its = call(
        second_square, 2, [where, keep_square, own, other, one, three, early, mine, its],
        [full_block, low_block, half_shape, half_shape],
        [], block_flops // 2, 8 * MIB, {7: 2, 8: 3})

    own0, own1, own2, own3 = gather(low, from_z)
    come = other_core(its)
    (early,) = call(
        early_cube, 1, [where, own0, own1, own3, mine, come],
        [jax.ShapeDtypeStruct((ROWS, 2 * COLS), jnp.float32)], [], block_flops * 3 // 4, 4 * MIB)
    early, own2 = lax.optimization_barrier((early, own2))
    half = jax.ShapeDtypeStruct((B, 2 * COLS), jnp.float32)
    (leave,) = call(
        leaving_density, 1, [where, own2, early, square, mine, come], [half], [], block_flops // 8, 3 * MIB)
    (out,) = call(
        second_density, 1, [where, own2, early, square, mine, come, other_core(leave)], [half], [],
        block_flops // 8, 3 * MIB)
    return out


def solution(mesh):
    placed = (P("row", "col"), P(), P(), P())
    return jax.shard_map(
        body, mesh=mesh, in_specs=placed, out_specs=P("row", "col"), check_vma=False
    )
```

```python
import jax
import jax.numpy as jnp
from jax import lax
from jax.experimental import pallas as pl
from jax.experimental.pallas import tpu as pltpu
from jax.sharding import PartitionSpec as P

B = 128
N = 4096
K = 1024
ROWS = 256
COLS = 512
AXES = ("row", "col")
MIB = 1024 * 1024


def device(x, y, core, z):
    return (((x % 4) * 4 + y % 4) * 2 + core) * 4 + z % 4


def pairs(target):
    return [
        (device(x, y, core, z), device(*target(x, y, core, z)))
        for x in range(4) for y in range(4) for core in range(2) for z in range(4)
    ]


def other_core(a):
    return lax.ppermute(a, AXES, pairs(lambda x, y, core, z: (x, y, 1 - core, z)))


def from_z(a, d):
    return lax.ppermute(a, AXES, pairs(lambda x, y, core, z: (x, y, core, z - d)))


def from_first(a, d):
    return lax.ppermute(a, AXES, pairs(
        lambda x, y, core, z: (x - d, y, core, z) if core == 0 else (x, y - d, core, z)))


def from_second(a, d):
    return lax.ppermute(a, AXES, pairs(
        lambda x, y, core, z: (x, y - d, core, z) if core == 0 else (x - d, y, core, z)))


def gather(a, fetch):
    one, three, two = fetch(a, 1), fetch(a, 3), fetch(a, 2)
    return [a, one, two, three]


def place(x, y, kind, first, second):
    px = jnp.where(kind == 0, x + first, x + second) & 3
    py = jnp.where(kind == 0, y + second, y + first) & 3
    return px, py


def dot_t(a, b):
    return lax.dot_general(a, b, (((1,), (1,)), ((), ())), preferred_element_type=jnp.float32)


def dot(a, b):
    return jnp.dot(a, b, preferred_element_type=jnp.float32)


def aligned(block, size):
    return pl.ds(pl.multiple_of(block * size, size), size)


def block_at(x, y, kind, place_in_order):
    px, py = place(x, y, kind, place_in_order % 4, place_in_order // 4)
    return px * 8 + py * 2 + kind


def some_rows(where, keep_d, rows, half, parts, line):
    x, y, core = where[0], where[1], where[2]
    kind = core if half == 0 else 1 - core
    for n, part in parts.items():
        value = dot_t(rows[...], part[...])
        for u in range(4):
            block = block_at(x, y, kind, n * 4 + u)
            at = (half * 16 + n * 4 + u) * B
            for t in range(2):
                keep = keep_d[0, (x * 4 + y) * 2 + t, block].astype(jnp.float32)
                piece = value[t * B:(t + 1) * B, u * B:(u + 1) * B] * keep
                line[t * B:(t + 1) * B, at:at + B] = piece.astype(jnp.bfloat16)


def some_columns(where, keep_d, half, parts, columns, panel, mirrored=()):
    x, y, core = where[0], where[1], where[2]
    kind = core if half == 0 else 1 - core

    def put(value, kind, n, i, m, u, turn):
        keep = keep_d[0, block_at(x, y, kind, n * 4 + i), block_at(x, y, core, m * 4 + u)]
        piece = (value * keep.astype(jnp.float32)).astype(jnp.bfloat16)
        at, to = (half * 16 + n * 4 + i) * B, (m * 4 + u) * B
        panel[at:at + B, to:to + B] = piece.T if turn else piece

    for n, part in parts.items():
        for m, column in columns.items():
            if (n, m) in mirrored:
                continue
            value = dot_t(part[...], column[...])
            for i in range(4):
                for u in range(4):
                    piece = value[i * B:(i + 1) * B, u * B:(u + 1) * B]
                    put(piece, kind, n, i, m, u, False)
                    if (m, n) in mirrored:
                        put(piece, core, m, u, n, i, True)


EARLY = (0, 1, 3)


def density_0(where, keep_d, own0, other0, panel, line, rows):
    first = where[2] == 0
    mine, its = own0[:B, :], other0[:B, :]
    rows[:B, :] = jnp.where(first, mine, its)
    rows[B:, :] = jnp.where(first, its, mine)
    for half, part in enumerate((own0, other0)):
        some_rows(where, keep_d, rows, half, {0: part}, line)
        some_columns(where, keep_d, half, {0: part}, {0: own0}, panel)


def density_1(where, keep_d, own0, own1, own3, other0, rows, _, __, panel, line):
    own = {0: own0, 1: own1, 3: own3}
    some_rows(where, keep_d, rows, 0, {1: own1, 3: own3}, line)
    some_columns(where, keep_d, 0, {0: own0}, {1: own1, 3: own3}, panel, ((1, 0), (3, 0)))
    some_columns(where, keep_d, 0, {1: own1, 3: own3}, {1: own1, 3: own3}, panel, ((3, 1),))
    some_columns(where, keep_d, 1, {0: other0}, {1: own1, 3: own3}, panel)


def density_2(where, keep_d, own0, own1, own3, other1, other3, rows, _, __, panel, line, some):
    other = {1: other1, 3: other3}
    some_rows(where, keep_d, rows, 1, other, line)
    some_columns(where, keep_d, 1, other, {0: own0, 1: own1, 3: own3}, panel)

    @pl.loop(0, 3)
    def _(part):
        at = aligned(part + part // 2, 512)
        some[:, at] = (
            dot(line[:, :1024], panel[:1024, at])
            + dot(line[:, 1536:3072], panel[1536:3072, at])
            + dot(line[:, 3584:], panel[3584:, at]))


def density_3(where, keep_d, own0, own1, own2, own3, other0, other1, other3, rows, _, __, panel, line):
    some_rows(where, keep_d, rows, 0, {2: own2}, line)
    own = {0: own0, 1: own1, 2: own2, 3: own3}
    some_columns(where, keep_d, 0, {2: own2}, own, panel, ((0, 2), (1, 2), (3, 2)))
    some_columns(where, keep_d, 1, {0: other0, 1: other1, 3: other3}, {2: own2}, panel)


def first_square(where, keep_d, keep_s, own0, own1, own2, own3, other2, rows, some, _, __, panel, line, low, total):
    x, y, core, z = where[0], where[1], where[2], where[3]
    some_rows(where, keep_d, rows, 1, {2: other2}, line)
    some_columns(where, keep_d, 1, {2: other2}, {0: own0, 1: own1, 2: own2, 3: own3}, panel)

    def put(value, part):
        for t in range(2):
            for u in range(4):
                block = block_at(x, y, core, part * 4 + u)
                keep = keep_s[0, (x * 4 + y) * 2 + t, block].astype(jnp.float32)
                piece = value[t * B:(t + 1) * B, u * B:(u + 1) * B] * keep
                total[t * B:(t + 1) * B, aligned(part * 4 + u, B)] = piece
                low[t * B:(t + 1) * B, aligned(part * 4 + u, B)] = piece.astype(jnp.bfloat16)

    @pl.loop(0, 3)
    def _(n):
        part = n + n // 2
        at = aligned(part, 512)
        put(some[:, at] + dot(line[:, 1024:1536], panel[1024:1536, at])
            + dot(line[:, 3072:3584], panel[3072:3584, at]), part)

    put(dot(line[...], panel[:, 1024:1536]), 2)


def column_at(where, t):
    x, y, core, z = where[0], where[1], where[2], where[3]
    dx, dy = (z - x) & 3, (t - y) & 3
    return jnp.where(core == 0, dy * 4 + dx, dx * 4 + dy)


def early_first_cube(where, low, panel, early, columns):
    for t in range(4):
        at = aligned(column_at(where, t), B)
        columns[:, t * B:(t + 1) * B] = panel[:, at]
    early[...] = dot(low[...], columns[:2048, :])


def first_density(where, keep_d, its, columns, early, square, out):
    x, y, core, z = where[0], where[1], where[2], where[3]
    cube = early[...] + dot(its[...], columns[2048:, :])
    for u in range(4):
        value = 3.0 * square[:, aligned(column_at(where, u), B)] - 2.0 * cube[:, u * B:(u + 1) * B]
        for t in range(2):
            keep = keep_d[1, (x * 4 + y) * 2 + t, z * 8 + u * 2 + core].astype(jnp.float32)
            piece = value[t * B:(t + 1) * B, :] * keep
            out[t * B:(t + 1) * B, u * B:(u + 1) * B] = piece.astype(jnp.bfloat16)


def density_rows(where, keep_d, low, its, panel, square, out):
    x, y, core = where[0], where[1], where[2]

    @pl.loop(0, 4)
    def _(part):
        at = aligned(part, 512)
        cube = dot(low[...], panel[:2048, at]) + dot(its[...], panel[2048:, at])
        value = 3.0 * square[:, at] - 2.0 * cube
        for t in range(2):
            for u in range(4):
                keep = keep_d[1, (x * 4 + y) * 2 + t, block_at(x, y, core, part * 4 + u)].astype(jnp.float32)
                piece = value[t * B:(t + 1) * B, u * B:(u + 1) * B] * keep
                out[t * B:(t + 1) * B, aligned(part * 4 + u, B)] = piece.astype(jnp.bfloat16)


def chips_times(where, own, other, chips, mine, its):
    x, y, core = where[0], where[1], where[2]
    left, right = [], []
    for ref, offset, first, second in chips:
        px, py = place(x, y, core, first, second)
        chip = px * 4 + py
        for kind, line, at, to in ((core, own, second * 4 + first, mine), (1 - core, other, first * 4 + second, its)):
            block = ref[pl.ds(pl.multiple_of(offset + kind * B, B), B), :]
            to[aligned(chip, B), :] = block
            left.append(line[:, at * B:(at + 1) * B])
            right.append(block)
    total = None
    for n in range(0, len(left), 8):
        term = dot(jnp.concatenate(left[n:n + 8], axis=1), jnp.concatenate(right[n:n + 8], axis=0))
        total = term if total is None else total + term
    return total


def early_square(where, own, other, near, far0, far1, far2, far3, early, mine, its):
    chips = [(near, i * ROWS, i, 0) for i in range(4)]
    chips += [(ref, 0, i, 2) for i, ref in enumerate((far0, far1, far2, far3))]
    early[...] = chips_times(where, own, other, chips, mine, its)


def second_square(where, keep_s, own, other, one, three, early, _, __, square, low, mine, its):
    x, y, core, z = where[0], where[1], where[2], where[3]
    chips = [(ref, i * ROWS, i, j) for ref, j in ((one, 1), (three, 3)) for i in range(4)]
    value = early[...] + chips_times(where, own, other, chips, mine, its)
    for t in range(2):
        for u in range(4):
            keep = keep_s[1, (x * 4 + y) * 2 + t, z * 8 + u * 2 + core].astype(jnp.float32)
            piece = value[t * B:(t + 1) * B, u * B:(u + 1) * B] * keep
            square[t * B:(t + 1) * B, u * B:(u + 1) * B] = piece
            low[t * B:(t + 1) * B, u * B:(u + 1) * B] = piece.astype(jnp.bfloat16)


def parts_times_panel(parts, z, mine, come):
    total = [None, None]
    for value, d in parts:
        for n, panel in enumerate((mine, come)):
            term = dot(value, panel[aligned((z + d) & 3, 512), :])
            total[n] = term if total[n] is None else total[n] + term
    return total


def early_cube(where, own0, own1, own3, mine, come, out):
    parts = [(own0[...], 0), (own1[...], 1), (own3[...], 3)]
    out[:, :COLS], out[:, COLS:] = parts_times_panel(parts, where[3], mine, come)


def density_share(where, at, own2, early, square, mine, come):
    first, second = parts_times_panel([(own2[at, :], 2)], where[3], mine, come)
    return 3.0 * square[at, :] - 2.0 * (early[at, :COLS] + first), -2.0 * (early[at, COLS:] + second)


def leaving_density(where, own2, early, square, mine, come, out):
    at = aligned(1 - where[2], B)
    out[:, :COLS], out[:, COLS:] = density_share(where, at, own2, early, square, mine, come)


def second_density(where, own2, early, square, mine, come, share, out):
    own, other = density_share(where, aligned(where[2], B), own2, early, square, mine, come)
    own, other = own + share[:, COLS:], other + share[:, :COLS]
    first = where[2] == 0
    for t in range(4):
        one, two = own[:, t * B:(t + 1) * B], other[:, t * B:(t + 1) * B]
        out[:, 2 * t * B:(2 * t + 1) * B] = jnp.where(first, one, two)
        out[:, (2 * t + 1) * B:(2 * t + 2) * B] = jnp.where(first, two, one)


SMEM = pl.BlockSpec(memory_space=pltpu.SMEM)
VMEM = pl.BlockSpec(memory_space=pltpu.VMEM)


def call(kernel, n_smem, ins, outs, scratch, flops, moved, aliases={}):
    return pl.pallas_call(
        kernel,
        in_specs=[SMEM] * n_smem + [VMEM] * (len(ins) - n_smem),
        out_specs=[VMEM] * len(outs),
        out_shape=outs,
        scratch_shapes=scratch,
        input_output_aliases=aliases,
        cost_estimate=pl.CostEstimate(flops=flops, bytes_accessed=moved, transcendentals=0),
        compiler_params=pltpu.CompilerParams(vmem_limit_bytes=12 * MIB),
    )(*ins)


def body(coeffs, coef_pattern, keep_density, keep_square):
    r, z = lax.axis_index("row"), lax.axis_index("col")
    x, y, core = r // 8, (r // 2) % 4, r % 2
    where = jnp.stack([x, y, core, z]).astype(jnp.int32)
    low_block = jax.ShapeDtypeStruct((ROWS, COLS), jnp.bfloat16)
    full_block = jax.ShapeDtypeStruct((ROWS, COLS), jnp.float32)
    panel_shape = jax.ShapeDtypeStruct((N, COLS), jnp.bfloat16)
    line_shape = jax.ShapeDtypeStruct((ROWS, N), jnp.bfloat16)
    wide_shape = jax.ShapeDtypeStruct((N, N // 2), jnp.bfloat16)
    block_flops = 2 * ROWS * N * COLS
    pair_flops = 2 * 512 * 512 * K

    kept = jnp.concatenate(gather(coeffs, from_z), axis=1)
    pattern = lax.dynamic_slice(coef_pattern, (r, 0), (1, 8)).reshape(4, 2)
    pattern = jnp.concatenate([pattern, pattern], axis=0)
    pattern = lax.dynamic_slice(pattern, (z, 0), (4, 2)).reshape(1, 8)
    kept = kept * jnp.repeat(pattern, B, 1).astype(jnp.bfloat16)
    near = jnp.concatenate(gather(kept, from_first), axis=0)
    own1, own3, other0 = from_second(near, 1), from_second(near, 3), other_core(near)
    rows_shape = jax.ShapeDtypeStruct((ROWS, K), jnp.bfloat16)
    out_shapes = [wide_shape, line_shape]
    panel, line, rows = call(
        density_0, 2, [where, keep_density, near, other0], out_shapes + [rows_shape], [], pair_flops // 8, MIB)
    panel, line, own0, own1, own3 = lax.optimization_barrier((panel, line, near, own1, own3))
    own2 = from_second(own0, 2)
    other1, other3 = other_core(own1), other_core(own3)
    panel, line = call(
        density_1, 2, [where, keep_density, own0, own1, own3, other0, rows, panel, line],
        out_shapes, [], 11 * pair_flops, 8 * MIB, {7: 0, 8: 1})
    panel, line, some = call(
        density_2, 2, [where, keep_density, own0, own1, own3, other1, other3, rows, panel, line],
        out_shapes + [jax.ShapeDtypeStruct((ROWS, N // 2), jnp.float32)], [], 11 * pair_flops, 8 * MIB, {8: 0, 9: 1})
    panel, line, own2 = lax.optimization_barrier((panel, line, own2))
    other2 = other_core(own2)
    panel, line = call(
        density_3, 2, [where, keep_density, own0, own1, own2, own3, other0, other1, other3, rows, panel, line],
        out_shapes, [], 10 * pair_flops, 8 * MIB, {10: 0, 11: 1})
    panel, line, low, square = call(
        first_square, 3,
        [where, keep_density, keep_square, own0, own1, own2, own3, other2, rows, some, panel, line],
        out_shapes + [jax.ShapeDtypeStruct((ROWS, N // 2), jnp.bfloat16), jax.ShapeDtypeStruct((ROWS, N // 2), jnp.float32)],
        [],
        4 * pair_flops + 2 * block_flops, 20 * MIB, {10: 0, 11: 1})

    its = other_core(low)
    early, columns = call(
        early_first_cube, 1, [where, low, panel], [full_block, panel_shape], [], block_flops // 2, 12 * MIB)
    (current,) = call(
        first_density, 2, [where, keep_density, its, columns, early, square], [low_block], [],
        block_flops // 2, 4 * MIB)

    start, one, three, two, far = lax.optimization_barrier((
        current, from_first(current, 1), from_first(current, 3), from_first(current, 2), from_second(current, 2)))
    (own,) = call(
        density_rows, 2, [where, keep_density, low, its, panel, square],
        [jax.ShapeDtypeStruct((ROWS, N // 2), jnp.bfloat16)], [], 4 * block_flops, 22 * MIB)
    other = other_core(own)
    near = jnp.concatenate([start, one, two, three], axis=0)
    one, three = from_second(near, 1), from_second(near, 3)
    far = gather(far, from_first)
    half_shape = jax.ShapeDtypeStruct((N // 2, COLS), jnp.bfloat16)
    early, mine, its = call(
        early_square, 1, [where, own, other, near, *far], [full_block, half_shape, half_shape],
        [], block_flops // 2, 10 * MIB)
    square, low, mine, its = call(
        second_square, 2, [where, keep_square, own, other, one, three, early, mine, its],
        [full_block, low_block, half_shape, half_shape],
        [], block_flops // 2, 8 * MIB, {7: 2, 8: 3})

    own0, own1, own2, own3 = gather(low, from_z)
    come = other_core(its)
    (early,) = call(
        early_cube, 1, [where, own0, own1, own3, mine, come],
        [jax.ShapeDtypeStruct((ROWS, 2 * COLS), jnp.float32)], [], block_flops * 3 // 4, 4 * MIB)
    early, own2 = lax.optimization_barrier((early, own2))
    half = jax.ShapeDtypeStruct((B, 2 * COLS), jnp.float32)
    (leave,) = call(
        leaving_density, 1, [where, own2, early, square, mine, come], [half], [], block_flops // 8, 3 * MIB)
    (out,) = call(
        second_density, 1, [where, own2, early, square, mine, come, other_core(leave)], [half], [],
        block_flops // 8, 3 * MIB)
    return out


def solution(mesh):
    placed = (P("row", "col"), P(), P(), P())
    return jax.shard_map(
        body, mesh=mesh, in_specs=placed, out_specs=P("row", "col"), check_vma=False
    )
```

```python
import jax
import jax.numpy as jnp
from jax import lax
from jax.experimental import pallas as pl
from jax.experimental.pallas import tpu as pltpu
from jax.sharding import PartitionSpec as P

B = 128
N = 4096
K = 1024
ROWS = 256
COLS = 512
AXES = ("row", "col")
MIB = 1024 * 1024


def device(x, y, core, z):
    return (((x % 4) * 4 + y % 4) * 2 + core) * 4 + z % 4


def pairs(target):
    return [
        (device(x, y, core, z), device(*target(x, y, core, z)))
        for x in range(4) for y in range(4) for core in range(2) for z in range(4)
    ]


def other_core(a):
    return lax.ppermute(a, AXES, pairs(lambda x, y, core, z: (x, y, 1 - core, z)))


def from_z(a, d):
    return lax.ppermute(a, AXES, pairs(lambda x, y, core, z: (x, y, core, z - d)))


def from_first(a, d):
    return lax.ppermute(a, AXES, pairs(
        lambda x, y, core, z: (x - d, y, core, z) if core == 0 else (x, y - d, core, z)))


def from_second(a, d):
    return lax.ppermute(a, AXES, pairs(
        lambda x, y, core, z: (x, y - d, core, z) if core == 0 else (x - d, y, core, z)))


def gather(a, fetch):
    one, three, two = fetch(a, 1), fetch(a, 3), fetch(a, 2)
    return [a, one, two, three]


def place(x, y, kind, first, second):
    px = jnp.where(kind == 0, x + first, x + second) & 3
    py = jnp.where(kind == 0, y + second, y + first) & 3
    return px, py


def dot_t(a, b):
    return lax.dot_general(a, b, (((1,), (1,)), ((), ())), preferred_element_type=jnp.float32)


def dot(a, b):
    return jnp.dot(a, b, preferred_element_type=jnp.float32)


def aligned(block, size):
    return pl.ds(pl.multiple_of(block * size, size), size)


def block_at(x, y, kind, place_in_order):
    px, py = place(x, y, kind, place_in_order % 4, place_in_order // 4)
    return px * 8 + py * 2 + kind


def some_rows(where, keep_d, rows, half, parts, line):
    x, y, core = where[0], where[1], where[2]
    kind = core if half == 0 else 1 - core
    for n, part in parts.items():
        value = dot_t(rows[...], part[...])
        for u in range(4):
            block = block_at(x, y, kind, n * 4 + u)
            at = (half * 16 + n * 4 + u) * B
            for t in range(2):
                keep = keep_d[0, (x * 4 + y) * 2 + t, block].astype(jnp.float32)
                piece = value[t * B:(t + 1) * B, u * B:(u + 1) * B] * keep
                line[t * B:(t + 1) * B, at:at + B] = piece.astype(jnp.bfloat16)


def some_columns(where, keep_d, half, parts, columns, panel, mirrored=()):
    x, y, core = where[0], where[1], where[2]
    kind = core if half == 0 else 1 - core

    def put(value, kind, n, i, m, u, turn):
        keep = keep_d[0, block_at(x, y, kind, n * 4 + i), block_at(x, y, core, m * 4 + u)]
        piece = (value * keep.astype(jnp.float32)).astype(jnp.bfloat16)
        at, to = (half * 16 + n * 4 + i) * B, (m * 4 + u) * B
        panel[at:at + B, to:to + B] = piece.T if turn else piece

    for n, part in parts.items():
        for m, column in columns.items():
            if (n, m) in mirrored:
                continue
            value = dot_t(part[...], column[...])
            for i in range(4):
                for u in range(4):
                    piece = value[i * B:(i + 1) * B, u * B:(u + 1) * B]
                    put(piece, kind, n, i, m, u, False)
                    if (m, n) in mirrored:
                        put(piece, core, m, u, n, i, True)


EARLY = (0, 1, 3)


def density_0(where, keep_d, own0, other0, panel, line, rows):
    first = where[2] == 0
    mine, its = own0[:B, :], other0[:B, :]
    rows[:B, :] = jnp.where(first, mine, its)
    rows[B:, :] = jnp.where(first, its, mine)
    for half, part in enumerate((own0, other0)):
        some_rows(where, keep_d, rows, half, {0: part}, line)
        some_columns(where, keep_d, half, {0: part}, {0: own0}, panel)


def density_1(where, keep_d, own0, own1, own3, other0, rows, _, __, panel, line):
    own = {0: own0, 1: own1, 3: own3}
    some_rows(where, keep_d, rows, 0, {1: own1, 3: own3}, line)
    some_columns(where, keep_d, 0, {0: own0}, {1: own1, 3: own3}, panel, ((1, 0), (3, 0)))
    some_columns(where, keep_d, 0, {1: own1, 3: own3}, {1: own1, 3: own3}, panel, ((3, 1),))
    some_columns(where, keep_d, 1, {0: other0}, {1: own1, 3: own3}, panel)


def density_2(where, keep_d, own0, own1, own3, other1, other3, rows, _, __, panel, line, some):
    other = {1: other1, 3: other3}
    some_rows(where, keep_d, rows, 1, other, line)
    some_columns(where, keep_d, 1, other, {0: own0, 1: own1, 3: own3}, panel)

    @pl.loop(0, 3)
    def _(part):
        at = aligned(part + part // 2, 512)
        some[:, at] = (
            dot(line[:, :1024], panel[:1024, at])
            + dot(line[:, 1536:3072], panel[1536:3072, at])
            + dot(line[:, 3584:], panel[3584:, at]))


def density_3(where, keep_d, own0, own1, own2, own3, other0, other1, other3, rows, _, __, panel, line):
    some_rows(where, keep_d, rows, 0, {2: own2}, line)
    own = {0: own0, 1: own1, 2: own2, 3: own3}
    some_columns(where, keep_d, 0, {2: own2}, own, panel, ((0, 2), (1, 2), (3, 2)))
    some_columns(where, keep_d, 1, {0: other0, 1: other1, 3: other3}, {2: own2}, panel)


def first_square(where, keep_d, keep_s, own0, own1, own2, own3, other2, rows, some, _, __, panel, line, low, total):
    x, y, core, z = where[0], where[1], where[2], where[3]
    some_rows(where, keep_d, rows, 1, {2: other2}, line)
    some_columns(where, keep_d, 1, {2: other2}, {0: own0, 1: own1, 2: own2, 3: own3}, panel)

    def put(value, part):
        for t in range(2):
            for u in range(4):
                block = block_at(x, y, core, part * 4 + u)
                keep = keep_s[0, (x * 4 + y) * 2 + t, block].astype(jnp.float32)
                piece = value[t * B:(t + 1) * B, u * B:(u + 1) * B] * keep
                total[t * B:(t + 1) * B, aligned(part * 4 + u, B)] = piece
                low[t * B:(t + 1) * B, aligned(part * 4 + u, B)] = piece.astype(jnp.bfloat16)

    @pl.loop(0, 3)
    def _(n):
        part = n + n // 2
        at = aligned(part, 512)
        put(some[:, at] + dot(line[:, 1024:1536], panel[1024:1536, at])
            + dot(line[:, 3072:3584], panel[3072:3584, at]), part)

    put(dot(line[...], panel[:, 1024:1536]), 2)


def column_at(where, t):
    x, y, core, z = where[0], where[1], where[2], where[3]
    dx, dy = (z - x) & 3, (t - y) & 3
    return jnp.where(core == 0, dy * 4 + dx, dx * 4 + dy)


def early_first_cube(where, low, panel, early, columns):
    for t in range(4):
        at = aligned(column_at(where, t), B)
        columns[:, t * B:(t + 1) * B] = panel[:, at]
    early[...] = dot(low[...], columns[:2048, :])


def first_density(where, keep_d, its, columns, early, square, out):
    x, y, core, z = where[0], where[1], where[2], where[3]
    cube = early[...] + dot(its[...], columns[2048:, :])
    for u in range(4):
        value = 3.0 * square[:, aligned(column_at(where, u), B)] - 2.0 * cube[:, u * B:(u + 1) * B]
        for t in range(2):
            keep = keep_d[1, (x * 4 + y) * 2 + t, z * 8 + u * 2 + core].astype(jnp.float32)
            piece = value[t * B:(t + 1) * B, :] * keep
            out[t * B:(t + 1) * B, u * B:(u + 1) * B] = piece.astype(jnp.bfloat16)


def density_rows(where, keep_d, low, its, panel, square, out):
    x, y, core = where[0], where[1], where[2]

    @pl.loop(0, 4)
    def _(part):
        at = aligned(part, 512)
        cube = dot(low[...], panel[:2048, at]) + dot(its[...], panel[2048:, at])
        value = 3.0 * square[:, at] - 2.0 * cube
        for t in range(2):
            for u in range(4):
                keep = keep_d[1, (x * 4 + y) * 2 + t, block_at(x, y, core, part * 4 + u)].astype(jnp.float32)
                piece = value[t * B:(t + 1) * B, u * B:(u + 1) * B] * keep
                out[t * B:(t + 1) * B, aligned(part * 4 + u, B)] = piece.astype(jnp.bfloat16)


def chips_times(where, own, other, chips, mine, its):
    x, y, core = where[0], where[1], where[2]
    left, right = [], []
    for ref, offset, first, second in chips:
        px, py = place(x, y, core, first, second)
        chip = px * 4 + py
        for kind, line, at, to in ((core, own, second * 4 + first, mine), (1 - core, other, first * 4 + second, its)):
            block = ref[pl.ds(pl.multiple_of(offset + kind * B, B), B), :]
            to[aligned(chip, B), :] = block
            left.append(line[:, at * B:(at + 1) * B])
            right.append(block)
    total = None
    for n in range(0, len(left), 8):
        term = dot(jnp.concatenate(left[n:n + 8], axis=1), jnp.concatenate(right[n:n + 8], axis=0))
        total = term if total is None else total + term
    return total


def square_near(where, own, other, near, early, mine, its):
    early[...] = chips_times(where, own, other, [(near, i * ROWS, i, 0) for i in range(4)], mine, its)


def square_far(where, own, other, far0, far1, far2, far3, early, _, __, out, mine, its):
    chips = [(ref, 0, i, 2) for i, ref in enumerate((far0, far1, far2, far3))]
    out[...] = early[...] + chips_times(where, own, other, chips, mine, its)


def second_square(where, keep_s, own, other, one, three, early, _, __, square, low, mine, its):
    x, y, core, z = where[0], where[1], where[2], where[3]
    chips = [(ref, i * ROWS, i, j) for ref, j in ((one, 1), (three, 3)) for i in range(4)]
    value = early[...] + chips_times(where, own, other, chips, mine, its)
    for t in range(2):
        for u in range(4):
            keep = keep_s[1, (x * 4 + y) * 2 + t, z * 8 + u * 2 + core].astype(jnp.float32)
            piece = value[t * B:(t + 1) * B, u * B:(u + 1) * B] * keep
            square[t * B:(t + 1) * B, u * B:(u + 1) * B] = piece
            low[t * B:(t + 1) * B, u * B:(u + 1) * B] = piece.astype(jnp.bfloat16)


def parts_times_panel(parts, z, mine, come):
    total = [None, None]
    for value, d in parts:
        for n, panel in enumerate((mine, come)):
            term = dot(value, panel[aligned((z + d) & 3, 512), :])
            total[n] = term if total[n] is None else total[n] + term
    return total


def early_cube(where, own0, own1, own3, mine, come, out):
    parts = [(own0[...], 0), (own1[...], 1), (own3[...], 3)]
    out[:, :COLS], out[:, COLS:] = parts_times_panel(parts, where[3], mine, come)


def density_share(where, at, own2, early, square, mine, come):
    first, second = parts_times_panel([(own2[at, :], 2)], where[3], mine, come)
    return 3.0 * square[at, :] - 2.0 * (early[at, :COLS] + first), -2.0 * (early[at, COLS:] + second)


def leaving_density(where, own2, early, square, mine, come, out):
    at = aligned(1 - where[2], B)
    out[:, :COLS], out[:, COLS:] = density_share(where, at, own2, early, square, mine, come)


def second_density(where, own2, early, square, mine, come, share, out):
    own, other = density_share(where, aligned(where[2], B), own2, early, square, mine, come)
    own, other = own + share[:, COLS:], other + share[:, :COLS]
    first = where[2] == 0
    for t in range(4):
        one, two = own[:, t * B:(t + 1) * B], other[:, t * B:(t + 1) * B]
        out[:, 2 * t * B:(2 * t + 1) * B] = jnp.where(first, one, two)
        out[:, (2 * t + 1) * B:(2 * t + 2) * B] = jnp.where(first, two, one)


SMEM = pl.BlockSpec(memory_space=pltpu.SMEM)
VMEM = pl.BlockSpec(memory_space=pltpu.VMEM)


def call(kernel, n_smem, ins, outs, scratch, flops, moved, aliases={}):
    return pl.pallas_call(
        kernel,
        in_specs=[SMEM] * n_smem + [VMEM] * (len(ins) - n_smem),
        out_specs=[VMEM] * len(outs),
        out_shape=outs,
        scratch_shapes=scratch,
        input_output_aliases=aliases,
        cost_estimate=pl.CostEstimate(flops=flops, bytes_accessed=moved, transcendentals=0),
        compiler_params=pltpu.CompilerParams(vmem_limit_bytes=12 * MIB),
    )(*ins)


def body(coeffs, coef_pattern, keep_density, keep_square):
    r, z = lax.axis_index("row"), lax.axis_index("col")
    x, y, core = r // 8, (r // 2) % 4, r % 2
    where = jnp.stack([x, y, core, z]).astype(jnp.int32)
    low_block = jax.ShapeDtypeStruct((ROWS, COLS), jnp.bfloat16)
    full_block = jax.ShapeDtypeStruct((ROWS, COLS), jnp.float32)
    panel_shape = jax.ShapeDtypeStruct((N, COLS), jnp.bfloat16)
    line_shape = jax.ShapeDtypeStruct((ROWS, N), jnp.bfloat16)
    wide_shape = jax.ShapeDtypeStruct((N, N // 2), jnp.bfloat16)
    block_flops = 2 * ROWS * N * COLS
    pair_flops = 2 * 512 * 512 * K

    kept = jnp.concatenate(gather(coeffs, from_z), axis=1)
    pattern = lax.dynamic_slice(coef_pattern, (r, 0), (1, 8)).reshape(4, 2)
    pattern = jnp.concatenate([pattern, pattern], axis=0)
    pattern = lax.dynamic_slice(pattern, (z, 0), (4, 2)).reshape(1, 8)
    kept = kept * jnp.repeat(pattern, B, 1).astype(jnp.bfloat16)
    near = jnp.concatenate(gather(kept, from_first), axis=0)
    own1, own3, other0 = from_second(near, 1), from_second(near, 3), other_core(near)
    rows_shape = jax.ShapeDtypeStruct((ROWS, K), jnp.bfloat16)
    out_shapes = [wide_shape, line_shape]
    panel, line, rows = call(
        density_0, 2, [where, keep_density, near, other0], out_shapes + [rows_shape], [], pair_flops // 8, MIB)
    panel, line, own0, own1, own3 = lax.optimization_barrier((panel, line, near, own1, own3))
    own2 = from_second(own0, 2)
    other1, other3 = other_core(own1), other_core(own3)
    panel, line = call(
        density_1, 2, [where, keep_density, own0, own1, own3, other0, rows, panel, line],
        out_shapes, [], 11 * pair_flops, 8 * MIB, {7: 0, 8: 1})
    panel, line, some = call(
        density_2, 2, [where, keep_density, own0, own1, own3, other1, other3, rows, panel, line],
        out_shapes + [jax.ShapeDtypeStruct((ROWS, N // 2), jnp.float32)], [], 11 * pair_flops, 8 * MIB, {8: 0, 9: 1})
    panel, line, own2 = lax.optimization_barrier((panel, line, own2))
    other2 = other_core(own2)
    panel, line = call(
        density_3, 2, [where, keep_density, own0, own1, own2, own3, other0, other1, other3, rows, panel, line],
        out_shapes, [], 10 * pair_flops, 8 * MIB, {10: 0, 11: 1})
    panel, line, low, square = call(
        first_square, 3,
        [where, keep_density, keep_square, own0, own1, own2, own3, other2, rows, some, panel, line],
        out_shapes + [jax.ShapeDtypeStruct((ROWS, N // 2), jnp.bfloat16), jax.ShapeDtypeStruct((ROWS, N // 2), jnp.float32)],
        [],
        4 * pair_flops + 2 * block_flops, 20 * MIB, {10: 0, 11: 1})

    its = other_core(low)
    early, columns = call(
        early_first_cube, 1, [where, low, panel], [full_block, panel_shape], [], block_flops // 2, 12 * MIB)
    (current,) = call(
        first_density, 2, [where, keep_density, its, columns, early, square], [low_block], [],
        block_flops // 2, 4 * MIB)

    start, one, three, two, far = lax.optimization_barrier((
        current, from_first(current, 1), from_first(current, 3), from_first(current, 2), from_second(current, 2)))
    (own,) = call(
        density_rows, 2, [where, keep_density, low, its, panel, square],
        [jax.ShapeDtypeStruct((ROWS, N // 2), jnp.bfloat16)], [], 4 * block_flops, 22 * MIB)
    other = other_core(own)
    near = jnp.concatenate([start, one, two, three], axis=0)
    one, three = from_second(near, 1), from_second(near, 3)
    far = gather(far, from_first)
    half_shape = jax.ShapeDtypeStruct((N // 2, COLS), jnp.bfloat16)
    early, mine, its = call(
        square_near, 1, [where, own, other, near], [full_block, half_shape, half_shape],
        [], block_flops // 4, 6 * MIB)
    early, mine, its = call(
        square_far, 1, [where, own, other, *far, early, mine, its], [full_block, half_shape, half_shape],
        [], block_flops // 4, 6 * MIB, {8: 1, 9: 2})
    square, low, mine, its = call(
        second_square, 2, [where, keep_square, own, other, one, three, early, mine, its],
        [full_block, low_block, half_shape, half_shape],
        [], block_flops // 2, 8 * MIB, {7: 2, 8: 3})

    own0, own1, own2, own3 = gather(low, from_z)
    come = other_core(its)
    (early,) = call(
        early_cube, 1, [where, own0, own1, own3, mine, come],
        [jax.ShapeDtypeStruct((ROWS, 2 * COLS), jnp.float32)], [], block_flops * 3 // 4, 4 * MIB)
    early, own2 = lax.optimization_barrier((early, own2))
    half = jax.ShapeDtypeStruct((B, 2 * COLS), jnp.float32)
    (leave,) = call(
        leaving_density, 1, [where, own2, early, square, mine, come], [half], [], block_flops // 8, 3 * MIB)
    (out,) = call(
        second_density, 1, [where, own2, early, square, mine, come, other_core(leave)], [half], [],
        block_flops // 8, 3 * MIB)
    return out


def solution(mesh):
    placed = (P("row", "col"), P(), P(), P())
    return jax.shard_map(
        body, mesh=mesh, in_specs=placed, out_specs=P("row", "col"), check_vma=False
    )
```

```python
import functools

import jax
import jax.numpy as jnp
from jax import lax
from jax.experimental import pallas as pl
from jax.experimental.pallas import tpu as pltpu
from jax.sharding import PartitionSpec as P

B = 128
N = 4096
K = 1024
ROWS = 256
COLS = 512
AXES = ("row", "col")
MIB = 1024 * 1024


def device(x, y, core, z):
    return (((x % 4) * 4 + y % 4) * 2 + core) * 4 + z % 4


def pairs(target):
    return [
        (device(x, y, core, z), device(*target(x, y, core, z)))
        for x in range(4) for y in range(4) for core in range(2) for z in range(4)
    ]


def other_core(a):
    return lax.ppermute(a, AXES, pairs(lambda x, y, core, z: (x, y, 1 - core, z)))


def from_z(a, d):
    return lax.ppermute(a, AXES, pairs(lambda x, y, core, z: (x, y, core, z - d)))


def from_first(a, d):
    return lax.ppermute(a, AXES, pairs(
        lambda x, y, core, z: (x - d, y, core, z) if core == 0 else (x, y - d, core, z)))


def from_second(a, d):
    return lax.ppermute(a, AXES, pairs(
        lambda x, y, core, z: (x, y - d, core, z) if core == 0 else (x - d, y, core, z)))


def gather(a, fetch):
    one, three, two = fetch(a, 1), fetch(a, 3), fetch(a, 2)
    return [a, one, two, three]


def place(x, y, kind, first, second):
    px = jnp.where(kind == 0, x + first, x + second) & 3
    py = jnp.where(kind == 0, y + second, y + first) & 3
    return px, py


def dot_t(a, b):
    return lax.dot_general(a, b, (((1,), (1,)), ((), ())), preferred_element_type=jnp.float32)


def dot(a, b):
    return jnp.dot(a, b, preferred_element_type=jnp.float32)


def aligned(block, size):
    return pl.ds(pl.multiple_of(block * size, size), size)


def block_at(x, y, kind, place_in_order):
    px, py = place(x, y, kind, place_in_order % 4, place_in_order // 4)
    return px * 8 + py * 2 + kind


def some_rows(where, keep_d, rows, half, parts, line):
    x, y, core = where[0], where[1], where[2]
    kind = core if half == 0 else 1 - core
    for n, part in parts.items():
        value = dot_t(rows[...], part[...])
        for u in range(4):
            block = block_at(x, y, kind, n * 4 + u)
            at = (half * 16 + n * 4 + u) * B
            for t in range(2):
                keep = keep_d[0, (x * 4 + y) * 2 + t, block].astype(jnp.float32)
                piece = value[t * B:(t + 1) * B, u * B:(u + 1) * B] * keep
                line[t * B:(t + 1) * B, at:at + B] = piece.astype(jnp.bfloat16)


def some_columns(where, keep_d, half, parts, columns, panel, mirrored=()):
    x, y, core = where[0], where[1], where[2]
    kind = core if half == 0 else 1 - core

    def put(value, kind, n, i, m, u, turn):
        keep = keep_d[0, block_at(x, y, kind, n * 4 + i), block_at(x, y, core, m * 4 + u)]
        piece = (value * keep.astype(jnp.float32)).astype(jnp.bfloat16)
        at, to = (half * 16 + n * 4 + i) * B, (m * 4 + u) * B
        panel[at:at + B, to:to + B] = piece.T if turn else piece

    for n, part in parts.items():
        for m, column in columns.items():
            if (n, m) in mirrored:
                continue
            value = dot_t(part[...], column[...])
            for i in range(4):
                for u in range(4):
                    piece = value[i * B:(i + 1) * B, u * B:(u + 1) * B]
                    put(piece, kind, n, i, m, u, False)
                    if (m, n) in mirrored:
                        put(piece, core, m, u, n, i, True)


EARLY = (0, 1, 3)


def density_0(where, keep_d, own0, other0, panel, line, rows):
    first = where[2] == 0
    mine, its = own0[:B, :], other0[:B, :]
    rows[:B, :] = jnp.where(first, mine, its)
    rows[B:, :] = jnp.where(first, its, mine)
    for half, part in enumerate((own0, other0)):
        some_rows(where, keep_d, rows, half, {0: part}, line)
        some_columns(where, keep_d, half, {0: part}, {0: own0}, panel)


def density_1(where, keep_d, own0, own1, own3, other0, rows, _, __, panel, line):
    own = {0: own0, 1: own1, 3: own3}
    some_rows(where, keep_d, rows, 0, {1: own1, 3: own3}, line)
    some_columns(where, keep_d, 0, {0: own0}, {1: own1, 3: own3}, panel, ((1, 0), (3, 0)))
    some_columns(where, keep_d, 0, {1: own1, 3: own3}, {1: own1, 3: own3}, panel, ((3, 1),))
    some_columns(where, keep_d, 1, {0: other0}, {1: own1, 3: own3}, panel)


def density_2(where, keep_d, own0, own1, own3, other1, other3, rows, _, __, panel, line, some):
    other = {1: other1, 3: other3}
    some_rows(where, keep_d, rows, 1, other, line)
    some_columns(where, keep_d, 1, other, {0: own0, 1: own1, 3: own3}, panel)

    @pl.loop(0, 3)
    def _(part):
        at = aligned(part + part // 2, 512)
        some[:, at] = (
            dot(line[:, :1024], panel[:1024, at])
            + dot(line[:, 1536:3072], panel[1536:3072, at])
            + dot(line[:, 3584:], panel[3584:, at]))


def density_3(where, keep_d, own0, own1, own2, own3, other0, other1, other3, rows, _, __, panel, line):
    some_rows(where, keep_d, rows, 0, {2: own2}, line)
    own = {0: own0, 1: own1, 2: own2, 3: own3}
    some_columns(where, keep_d, 0, {2: own2}, own, panel, ((0, 2), (1, 2), (3, 2)))
    some_columns(where, keep_d, 1, {0: other0, 1: other1, 3: other3}, {2: own2}, panel)


def first_square(where, keep_d, keep_s, own0, own1, own2, own3, other2, rows, some, _, __, panel, line, low, total):
    x, y, core, z = where[0], where[1], where[2], where[3]
    some_rows(where, keep_d, rows, 1, {2: other2}, line)
    some_columns(where, keep_d, 1, {2: other2}, {0: own0, 1: own1, 2: own2, 3: own3}, panel)

    def put(value, part):
        for t in range(2):
            for u in range(4):
                block = block_at(x, y, core, part * 4 + u)
                keep = keep_s[0, (x * 4 + y) * 2 + t, block].astype(jnp.float32)
                piece = value[t * B:(t + 1) * B, u * B:(u + 1) * B] * keep
                total[t * B:(t + 1) * B, aligned(part * 4 + u, B)] = piece
                low[t * B:(t + 1) * B, aligned(part * 4 + u, B)] = piece.astype(jnp.bfloat16)

    @pl.loop(0, 3)
    def _(n):
        part = n + n // 2
        at = aligned(part, 512)
        put(some[:, at] + dot(line[:, 1024:1536], panel[1024:1536, at])
            + dot(line[:, 3072:3584], panel[3072:3584, at]), part)

    put(dot(line[...], panel[:, 1024:1536]), 2)


def column_at(where, t):
    x, y, core, z = where[0], where[1], where[2], where[3]
    dx, dy = (z - x) & 3, (t - y) & 3
    return jnp.where(core == 0, dy * 4 + dx, dx * 4 + dy)


def early_first_cube(where, low, panel, early, columns):
    for t in range(4):
        at = aligned(column_at(where, t), B)
        columns[:, t * B:(t + 1) * B] = panel[:, at]
    early[...] = dot(low[...], columns[:2048, :])


def first_density(where, keep_d, its, columns, early, square, out):
    x, y, core, z = where[0], where[1], where[2], where[3]
    cube = early[...] + dot(its[...], columns[2048:, :])
    for u in range(4):
        value = 3.0 * square[:, aligned(column_at(where, u), B)] - 2.0 * cube[:, u * B:(u + 1) * B]
        for t in range(2):
            keep = keep_d[1, (x * 4 + y) * 2 + t, z * 8 + u * 2 + core].astype(jnp.float32)
            piece = value[t * B:(t + 1) * B, :] * keep
            out[t * B:(t + 1) * B, u * B:(u + 1) * B] = piece.astype(jnp.bfloat16)


def density_rows(where, keep_d, low, its, panel, square, out):
    x, y, core = where[0], where[1], where[2]

    @pl.loop(0, 4)
    def _(part):
        at = aligned(part, 512)
        cube = dot(low[...], panel[:2048, at]) + dot(its[...], panel[2048:, at])
        value = 3.0 * square[:, at] - 2.0 * cube
        for t in range(2):
            for u in range(4):
                keep = keep_d[1, (x * 4 + y) * 2 + t, block_at(x, y, core, part * 4 + u)].astype(jnp.float32)
                piece = value[t * B:(t + 1) * B, u * B:(u + 1) * B] * keep
                out[t * B:(t + 1) * B, aligned(part * 4 + u, B)] = piece.astype(jnp.bfloat16)


def chips_times(where, own, other, chips, mine, its):
    x, y, core = where[0], where[1], where[2]
    left, right = [], []
    for ref, offset, first, second in chips:
        px, py = place(x, y, core, first, second)
        chip = px * 4 + py
        for kind, line, at, to in ((core, own, second * 4 + first, mine), (1 - core, other, first * 4 + second, its)):
            block = ref[pl.ds(pl.multiple_of(offset + kind * B, B), B), :]
            to[aligned(chip, B), :] = block
            left.append(line[:, at * B:(at + 1) * B])
            right.append(block)
    total = None
    for n in range(0, len(left), 8):
        term = dot(jnp.concatenate(left[n:n + 8], axis=1), jnp.concatenate(right[n:n + 8], axis=0))
        total = term if total is None else total + term
    return total


def square_near(where, own, other, near, early, mine, its):
    early[...] = chips_times(where, own, other, [(near, i * ROWS, i, 0) for i in range(4)], mine, its)


def square_far(where, own, other, far0, far1, far2, far3, early, _, __, out, mine, its):
    chips = [(ref, 0, i, 2) for i, ref in enumerate((far0, far1, far2, far3))]
    out[...] = early[...] + chips_times(where, own, other, chips, mine, its)


def second_square(where, keep_s, own, other, one, three, early, _, __, square, low, mine, its):
    x, y, core, z = where[0], where[1], where[2], where[3]
    chips = [(ref, i * ROWS, i, j) for ref, j in ((one, 1), (three, 3)) for i in range(4)]
    value = early[...] + chips_times(where, own, other, chips, mine, its)
    for t in range(2):
        for u in range(4):
            keep = keep_s[1, (x * 4 + y) * 2 + t, z * 8 + u * 2 + core].astype(jnp.float32)
            piece = value[t * B:(t + 1) * B, u * B:(u + 1) * B] * keep
            square[t * B:(t + 1) * B, u * B:(u + 1) * B] = piece
            low[t * B:(t + 1) * B, u * B:(u + 1) * B] = piece.astype(jnp.bfloat16)


def parts_times_panel(parts, z, panel):
    total = None
    for value, d in parts:
        term = dot(value, panel[aligned((z + d) & 3, 512), :])
        total = term if total is None else total + term
    return total


def early_cube(where, own0, mine, out):
    out[...] = parts_times_panel([(own0[...], 0)], where[3], mine)


def density_share(leave, where, own0, own1, own2, own3, early, square, mine, come, out):
    core, z = where[2], where[3]
    at = aligned(1 - core if leave else core, B)
    parts = [(own1[at, :], 1), (own3[at, :], 3), (own2[at, :], 2)]
    out[:, :COLS] = 3.0 * square[at, :] - 2.0 * (early[at, :] + parts_times_panel(parts, z, mine))
    out[:, COLS:] = -2.0 * parts_times_panel([(own0[at, :], 0)] + parts, z, come)


def join(where, stay, share, out):
    first = where[2] == 0
    for t in range(4):
        at, far = slice(t * B, (t + 1) * B), slice(COLS + t * B, COLS + (t + 1) * B)
        own, other = stay[:, at] + share[:, far], stay[:, far] + share[:, at]
        out[:, 2 * t * B:(2 * t + 1) * B] = jnp.where(first, own, other)
        out[:, (2 * t + 1) * B:(2 * t + 2) * B] = jnp.where(first, other, own)


SMEM = pl.BlockSpec(memory_space=pltpu.SMEM)
VMEM = pl.BlockSpec(memory_space=pltpu.VMEM)


def call(kernel, n_smem, ins, outs, scratch, flops, moved, aliases={}):
    return pl.pallas_call(
        kernel,
        in_specs=[SMEM] * n_smem + [VMEM] * (len(ins) - n_smem),
        out_specs=[VMEM] * len(outs),
        out_shape=outs,
        scratch_shapes=scratch,
        input_output_aliases=aliases,
        cost_estimate=pl.CostEstimate(flops=flops, bytes_accessed=moved, transcendentals=0),
        compiler_params=pltpu.CompilerParams(vmem_limit_bytes=12 * MIB),
    )(*ins)


def body(coeffs, coef_pattern, keep_density, keep_square):
    r, z = lax.axis_index("row"), lax.axis_index("col")
    x, y, core = r // 8, (r // 2) % 4, r % 2
    where = jnp.stack([x, y, core, z]).astype(jnp.int32)
    low_block = jax.ShapeDtypeStruct((ROWS, COLS), jnp.bfloat16)
    full_block = jax.ShapeDtypeStruct((ROWS, COLS), jnp.float32)
    panel_shape = jax.ShapeDtypeStruct((N, COLS), jnp.bfloat16)
    line_shape = jax.ShapeDtypeStruct((ROWS, N), jnp.bfloat16)
    wide_shape = jax.ShapeDtypeStruct((N, N // 2), jnp.bfloat16)
    block_flops = 2 * ROWS * N * COLS
    pair_flops = 2 * 512 * 512 * K

    kept = jnp.concatenate(gather(coeffs, from_z), axis=1)
    pattern = lax.dynamic_slice(coef_pattern, (r, 0), (1, 8)).reshape(4, 2)
    pattern = jnp.concatenate([pattern, pattern], axis=0)
    pattern = lax.dynamic_slice(pattern, (z, 0), (4, 2)).reshape(1, 8)
    kept = kept * jnp.repeat(pattern, B, 1).astype(jnp.bfloat16)
    near = jnp.concatenate(gather(kept, from_first), axis=0)
    own1, own3, other0 = from_second(near, 1), from_second(near, 3), other_core(near)
    rows_shape = jax.ShapeDtypeStruct((ROWS, K), jnp.bfloat16)
    out_shapes = [wide_shape, line_shape]
    panel, line, rows = call(
        density_0, 2, [where, keep_density, near, other0], out_shapes + [rows_shape], [], pair_flops // 8, MIB)
    panel, line, own0, own1, own3 = lax.optimization_barrier((panel, line, near, own1, own3))
    own2 = from_second(own0, 2)
    other1, other3 = other_core(own1), other_core(own3)
    panel, line = call(
        density_1, 2, [where, keep_density, own0, own1, own3, other0, rows, panel, line],
        out_shapes, [], 11 * pair_flops, 8 * MIB, {7: 0, 8: 1})
    panel, line, some = call(
        density_2, 2, [where, keep_density, own0, own1, own3, other1, other3, rows, panel, line],
        out_shapes + [jax.ShapeDtypeStruct((ROWS, N // 2), jnp.float32)], [], 11 * pair_flops, 8 * MIB, {8: 0, 9: 1})
    panel, line, own2 = lax.optimization_barrier((panel, line, own2))
    other2 = other_core(own2)
    panel, line = call(
        density_3, 2, [where, keep_density, own0, own1, own2, own3, other0, other1, other3, rows, panel, line],
        out_shapes, [], 10 * pair_flops, 8 * MIB, {10: 0, 11: 1})
    panel, line, low, square = call(
        first_square, 3,
        [where, keep_density, keep_square, own0, own1, own2, own3, other2, rows, some, panel, line],
        out_shapes + [jax.ShapeDtypeStruct((ROWS, N // 2), jnp.bfloat16), jax.ShapeDtypeStruct((ROWS, N // 2), jnp.float32)],
        [],
        4 * pair_flops + 2 * block_flops, 20 * MIB, {10: 0, 11: 1})

    its = other_core(low)
    early, columns = call(
        early_first_cube, 1, [where, low, panel], [full_block, panel_shape], [], block_flops // 2, 12 * MIB)
    (current,) = call(
        first_density, 2, [where, keep_density, its, columns, early, square], [low_block], [],
        block_flops // 2, 4 * MIB)

    start, one, three, two, far = lax.optimization_barrier((
        current, from_first(current, 1), from_first(current, 3), from_first(current, 2), from_second(current, 2)))
    (own,) = call(
        density_rows, 2, [where, keep_density, low, its, panel, square],
        [jax.ShapeDtypeStruct((ROWS, N // 2), jnp.bfloat16)], [], 4 * block_flops, 22 * MIB)
    other = other_core(own)
    near = jnp.concatenate([start, one, two, three], axis=0)
    one, three = from_second(near, 1), from_second(near, 3)
    far = gather(far, from_first)
    half_shape = jax.ShapeDtypeStruct((N // 2, COLS), jnp.bfloat16)
    early, mine, its = call(
        square_near, 1, [where, own, other, near], [full_block, half_shape, half_shape],
        [], block_flops // 4, 6 * MIB)
    early, mine, its = call(
        square_far, 1, [where, own, other, *far, early, mine, its], [full_block, half_shape, half_shape],
        [], block_flops // 4, 6 * MIB, {8: 1, 9: 2})
    square, low, mine, its = call(
        second_square, 2, [where, keep_square, own, other, one, three, early, mine, its],
        [full_block, low_block, half_shape, half_shape],
        [], block_flops // 2, 8 * MIB, {7: 2, 8: 3})

    own0, own1, own2, own3 = gather(low, from_z)
    come = other_core(its)
    (early,) = call(
        early_cube, 1, [where, own0, mine], [full_block], [], block_flops // 8, 2 * MIB)
    half = jax.ShapeDtypeStruct((B, 2 * COLS), jnp.float32)
    last = [where, own0, own1, own2, own3, early, square, mine, come]
    (leave,) = call(functools.partial(density_share, True), 1, last, [half], [], block_flops * 3 // 8, 5 * MIB)
    share = other_core(leave)
    (stay,) = call(functools.partial(density_share, False), 1, last, [half], [], block_flops * 3 // 8, 5 * MIB)
    (out,) = call(join, 1, [where, stay, share], [half], [], 0, 2 * MIB)
    return out


def solution(mesh):
    placed = (P("row", "col"), P(), P(), P())
    return jax.shard_map(
        body, mesh=mesh, in_specs=placed, out_specs=P("row", "col"), check_vma=False
    )
```
